128 devices in a mesh: ep: 16 (over z, x), fsdp: 8 (over y, core).
Axes of the slice: x: 4, y: 4, z: 4, core: 2. Of those that a mesh axis runs over, the one named last changes fastest.
Arguments:
- hidden_in: bfloat16 [16, 1024, 1024], P('ep', 'fsdp'), may hold values from -6 to 6
- cotangent: bfloat16 [16, 1024, 1024], P('ep', 'fsdp'), may hold values from -6 to 6
- lengths: int32 [16], P('ep'), may hold values from 512 to 1024, as said below
- routes: int32 [2, 16, 1024, 8], P(None, 'ep', 'fsdp'), may hold values from 0 to 31, all different within a row; in each aligned block of 128 rows (0 to 127, 128 to 255, ..., all dimensions but the last counted through in order) at most 40 rows name the same one
- gates: float32 [2, 16, 1024, 8], P(None, 'ep', 'fsdp'), may hold values from 0.06 to 0.19
- norm_attn: bfloat16 [2, 1024], P(None, 'fsdp'), may hold values from 0.5 to 1.5
- w_query: bfloat16 [2, 1024, 1024], P(None, 'fsdp'), may hold values from -0.1875 to 0.1875
- w_key: bfloat16 [2, 1024, 512], P(None, 'fsdp'), may hold values from -0.1875 to 0.1875
- w_value: bfloat16 [2, 1024, 512], P(None, 'fsdp'), may hold values from -0.1875 to 0.1875
- w_output: bfloat16 [2, 1024, 1024], P(None, 'fsdp'), may hold values from -0.5 to 0.5
- norm_mlp: bfloat16 [2, 1024], P(None, 'fsdp'), may hold values from 0.5 to 1.5
- w_gate: bfloat16 [2, 32, 1024, 512], P(None, 'ep', 'fsdp'), may hold values from -0.1875 to 0.1875
- w_up: bfloat16 [2, 32, 1024, 512], P(None, 'ep', 'fsdp'), may hold values from -0.1875 to 0.1875
- w_down: bfloat16 [2, 32, 1024, 512], P(None, 'ep', 'fsdp'), may hold values from -1 to 1
Outputs:
- hidden_out: bfloat16 [16, 1024, 1024], P('ep', 'fsdp')
- hidden_grad: float32 [16, 1024, 1024], P('ep', 'fsdp')
- gates_grad: float32 [2, 16, 1024, 8], P(None, 'ep', 'fsdp')
- norm_attn_grad: float32 [2, 1024], P(None, 'fsdp')
- w_query_grad: float32 [2, 1024, 1024], P(None, 'fsdp')
- w_key_grad: float32 [2, 1024, 512], P(None, 'fsdp')
- w_value_grad: float32 [2, 1024, 512], P(None, 'fsdp')
- w_output_grad: float32 [2, 1024, 1024], P(None, 'fsdp')
- norm_mlp_grad: float32 [2, 1024], P(None, 'fsdp')
- w_gate_grad: float32 [2, 32, 1024, 512], P(None, 'ep', 'fsdp')
- w_up_grad: float32 [2, 32, 1024, 512], P(None, 'ep', 'fsdp')
- w_down_grad: float32 [2, 32, 1024, 512], P(None, 'ep', 'fsdp')
The draws below stay inside these ranges and needn't reach their ends.
Inputs may be any that keep to these rules, and one draw needn't show every extreme that they name: Slot s holds one sequence in positions 0 to lengths[s] - 1 and padding after it; 4 slots or more are full. `routes`: within one layer, in each aligned block of 128 positions of one slot (the positions of one device), no expert is named by more than 40 tokens, a bound that some block reaches.
All inputs are finite; a program needn't handle non-finite values.
Results may differ from the reference program's by a relative error of at most 0.033.
Values may be sent and summed in bfloat16 or wider, within the bound.
No kernel may reach another device: no remote copies, remote signals or barrier semaphores. Data moves between devices by JAX's collectives and lax.ppermute only.
A program may use at most 256 MiB of HBM per device.

```python
import math
import jax
import jax.numpy as jnp
import numpy as np
from jax import lax

D = 1024
HEADS = 16
KV_HEADS = 8
HD = 64
FF = 512
TOP = 8
LAYERS = 2
SLOT = 1024
EXPERTS = 32
SLOTS = 16
MOST = 40
N_FSDP = 8


def draw_lengths(key, part):
    key = jax.random.fold_in(key, 11)
    first_key, second_key = jax.random.split(key)
    ragged = jax.random.randint(first_key, (SLOTS,), SLOT // 2, SLOT + 1)
    order = jax.random.permutation(second_key, SLOTS)
    full_slots = order < max(1, SLOTS // 4)
    return jnp.where(full_slots, SLOT, ragged).astype(jnp.int32)


def block_scale(stream_key, shape, cuts, smallest, largest):
    def one(dim, blocks):
        steps = jax.random.uniform(jax.random.fold_in(jax.random.fold_in(stream_key, 6), dim), (blocks,), jnp.float32, smallest / len(cuts), largest / len(cuts))
        return jnp.repeat(jnp.exp(steps), shape[dim] // blocks).reshape((-1,) + (1,) * (len(shape) - dim - 1))

    factor_of = one(*cuts[0])
    for cut in cuts[1:]:
        factor_of = factor_of * one(*cut)
    return factor_of


def shared_out(key, own, number, rows, number_of, top, reach, lean):
    order = jax.random.permutation(key, number_of)
    heavy_load, usual = shares(number_of, rows * top, reach, lean, True), shares(number_of, rows * top, reach, lean, False)
    places = jnp.arange(number_of)

    def named(sizes, turn):
        used = int((sizes > 0).sum())
        fixed = max(1, used // 4)
        moved = fixed + (places - fixed + turn * (used - fixed)) % max(1, number_of - fixed)
        return jnp.zeros((number_of,), jnp.int32).at[order[jnp.where(places < fixed, places, moved)]].set(jnp.asarray(sizes, jnp.int32))

    sizes = jnp.where(number % 4 == 0, named(heavy_load, number // 4), named(usual, number - number // 4 - 1))
    mixed = jax.random.permutation(jax.random.fold_in(own, 3), number_of)
    source_of, sink = mixed[0:number_of // 2 * 2:2], mixed[1:number_of // 2 * 2:2]
    room = jnp.minimum(sizes[source_of] - 1, reach - sizes[sink]) // 2
    room = jnp.where((source_of == order[0]) | (sink == order[0]) | (sizes[sink] == 0), 0, jnp.maximum(room, 0))
    moved = jax.random.randint(jax.random.fold_in(own, 4), (number_of // 2,), 0, 1 << 20) % (room + 1)
    sizes = sizes.at[source_of].add(-moved).at[sink].add(moved)
    labels = jnp.searchsorted(jnp.cumsum(sizes), jnp.arange(rows * top), side="right").astype(jnp.int32)
    grid = labels.reshape(top, rows).T
    grid = grid[jax.random.permutation(jax.random.fold_in(own, 1), rows)]
    turn = jax.random.randint(jax.random.fold_in(own, 2), (rows, 1), 0, top)
    return jnp.take_along_axis(grid, (jnp.arange(top)[None, :] + turn) % top, axis=1)


def shares(number_of, total, limit, slope, full):
    portions = [(1 << 20) // math.isqrt(rank ** slope) + 1 for rank in range(1, number_of + 1)]
    largest = limit if full else min(limit, max(-(-total // number_of), total * portions[0] // sum(portions)))
    least = 1 if total - largest >= number_of - 1 else 0
    given, rest = [largest] + [least] * (number_of - 1), total - largest - least * (number_of - 1)
    while rest > 0:
        candidates = [i for i in range(1, number_of) if given[i] < largest] or [i for i in range(1, number_of) if given[i] < limit]
        mass, remaining = sum([portions[i] for i in candidates]), rest
        for i in candidates:
            more = min(limit - given[i], max(1, remaining * portions[i] // mass), rest)
            given[i] = given[i] + more
            rest = rest - more
    return np.array(given)


def noise(rng, extent, width, bound, shards=(), kind=jnp.bfloat16):
    array = jax.random.normal(rng, extent, jnp.float32) * width
    if len(shards) > 0:
        array = block_scale(rng, extent, shards, -0.22, 0.18) * array
    return jnp.clip(array, min=-bound, max=bound).astype(kind)


def setup_inputs(seed: int = 0) -> dict:
    keys = jax.random.split(jax.random.key(seed), 15)
    hidden_in = noise(keys[0], (SLOTS, SLOT, D), 1.0, 6.0, ((0, 16), (1, 8)))
    cotangent = noise(keys[1], (SLOTS, SLOT, D), 1.0, 6.0, ((0, 16), (1, 8)))
    lengths = draw_lengths(jax.random.fold_in(keys[14], 71), 0)
    routes_keys = jax.random.split(jax.random.fold_in(keys[3], 1), LAYERS * SLOTS * SLOT // (SLOT // N_FSDP))
    routes_turns = jax.random.permutation(jax.random.fold_in(keys[3], 3), LAYERS * SLOTS * SLOT // (SLOT // N_FSDP))
    routes = jax.vmap(lambda own, number: shared_out(jax.random.fold_in(keys[3], 2), own, number, SLOT // N_FSDP, EXPERTS, TOP, MOST, 1))(routes_keys, routes_turns).reshape((LAYERS, SLOTS, SLOT, TOP))
    gates = jnp.clip(0.06 + 0.13 * jax.random.uniform(keys[4], (LAYERS, SLOTS, SLOT, TOP), jnp.float32) ** block_scale(keys[4], (LAYERS, SLOTS, SLOT, TOP), ((1, 16), (2, 8)), -0.2, 0.2), 0.06, 0.19)
    norm_attn = jnp.clip(1.0 + 0.1 * jax.random.normal(keys[5], (LAYERS, D), jnp.float32), 0.5, 1.5).astype(jnp.bfloat16)
    w_query = noise(keys[6], (LAYERS, D, HEADS * HD), D ** -0.5, 0.1875, ((1, 8),))
    w_key = noise(keys[7], (LAYERS, D, KV_HEADS * HD), D ** -0.5, 0.1875, ((1, 8),))
    w_value = noise(keys[8], (LAYERS, D, KV_HEADS * HD), D ** -0.5, 0.1875, ((1, 8),))
    w_output = noise(keys[9], (LAYERS, HEADS * HD, D), (HEADS * HD // 8) ** -0.5, 0.5, ((1, 8),))
    norm_mlp = jnp.clip(1.0 + 0.1 * jax.random.normal(keys[10], (LAYERS, D), jnp.float32), 0.5, 1.5).astype(jnp.bfloat16)
    w_gate = noise(keys[11], (LAYERS, EXPERTS, D, FF), D ** -0.5, 0.1875, ((1, 16), (2, 8)))
    w_up = noise(keys[12], (LAYERS, EXPERTS, D, FF), D ** -0.5, 0.1875, ((1, 16), (2, 8)))
    w_down = noise(keys[13], (LAYERS, EXPERTS, D, FF), (FF // 16) ** -0.5, 1.0, ((1, 16), (2, 8)))
    return dict(hidden_in=hidden_in, cotangent=cotangent, lengths=lengths, routes=routes, gates=gates, norm_attn=norm_attn, w_query=w_query, w_key=w_key, w_value=w_value, w_output=w_output, norm_mlp=norm_mlp, w_gate=w_gate, w_up=w_up, w_down=w_down)


EPS = 1e-06
THETA = 10000.0
NEG_FILL = -1e+30

@jax.custom_vjp
def low(v):
    return lax.optimization_barrier(v.astype(jnp.bfloat16)).astype(jnp.float32)

@jax.custom_vjp
def low_back(v):
    return v

def low_keep(v):
    return (low(v), None)

def low_pass(kept, grad):
    return (grad,)

def back_keep(v):
    return (v, None)

def back_low(kept, grad):
    return (low(grad),)
low.defvjp(low_keep, low_pass)
low_back.defvjp(back_keep, back_low)

def matmul(first_mat, second_mat):
    return jnp.dot(first_mat, second_mat, precision=lax.Precision.HIGHEST)

def rms_scale(hidden, gain_row):
    mean_square = lax.optimization_barrier(jnp.mean(hidden * hidden, axis=-1, keepdims=True))
    return hidden * lax.rsqrt(mean_square + EPS) * gain_row

def rotary_tables(positions, head_dim):
    half_dim = head_dim // 2
    frequency = THETA ** (-2.0 * jnp.arange(half_dim, dtype=jnp.float32) / head_dim)
    angles = positions.astype(jnp.float32)[:, None] * frequency[None, :]
    return (jnp.cos(angles), jnp.sin(angles))

def rotate(values, cos_table, sin_table):
    half_dim = values.shape[-1] // 2
    first_half = values[..., :half_dim]
    second_half = values[..., half_dim:]
    cos_part = cos_table[:, None, :]
    sin_part = sin_table[:, None, :]
    return jnp.concatenate([first_half * cos_part - second_half * sin_part, second_half * cos_part + first_half * sin_part], axis=-1)

def expert_slots(route_flat, capacity):
    onehot = (route_flat[:, None] == jnp.arange(EXPERTS, dtype=jnp.int32)[None, :]).astype(jnp.int32)
    rank_in = lax.optimization_barrier(jnp.sum(jnp.cumsum(onehot, axis=0) * onehot, axis=1)) - 1
    return (route_flat * capacity + rank_in).astype(jnp.int32)

def block_forward(hidden, gate_all, params, route_all, length):
    gains_attn, query_w, key_w, value_w, output_w, gains_mlp, gate_w, up_w, down_w = params
    positions = jnp.arange(SLOT, dtype=jnp.int32)
    live_rows = (positions < length).astype(jnp.float32)
    cos_table, sin_table = rotary_tables(positions, HD)
    allowed = (positions[None, :] <= positions[:, None]) & (positions[None, :] < length)
    group_size = HEADS // KV_HEADS
    capacity = N_FSDP * MOST
    score_scale = HD ** (-0.5)
    token_index = jnp.arange(SLOT * TOP, dtype=jnp.int32) // TOP
    for layer_id in range(LAYERS):
        normed = low(rms_scale(hidden, gains_attn[layer_id]))
        query_raw = low_back(matmul(normed, query_w[layer_id])).reshape(SLOT, HEADS, HD)
        key_raw = low_back(matmul(normed, key_w[layer_id])).reshape(SLOT, KV_HEADS, HD)
        value_rows = low(low_back(matmul(normed, value_w[layer_id]))).reshape(SLOT, KV_HEADS, HD)
        queries = low(rotate(query_raw, cos_table, sin_table)).reshape(SLOT, KV_HEADS, group_size, HD)
        key_rows = low(rotate(key_raw, cos_table, sin_table))
        scores = low_back(jnp.einsum('qgrd,kgd->grqk', queries, key_rows, precision=lax.Precision.HIGHEST) * score_scale)
        masked = jnp.where(allowed, scores, NEG_FILL)
        top_score = lax.optimization_barrier(jnp.max(masked, axis=-1, keepdims=True))
        expo_rows = jnp.exp(masked - top_score)
        attn_probs = low(expo_rows / lax.optimization_barrier(jnp.sum(expo_rows, axis=-1, keepdims=True)))
        mixed_rows = jnp.einsum('grqk,kgd->qgrd', attn_probs, value_rows, precision=lax.Precision.HIGHEST).reshape(SLOT, HEADS * HD)
        mixed_rows = low(low_back(mixed_rows))
        after_attn = hidden + low_back(matmul(mixed_rows, output_w[layer_id]))
        moe_input = low(rms_scale(after_attn, gains_mlp[layer_id]))
        route_flat = route_all[layer_id].reshape(SLOT * TOP)
        slot_index = expert_slots(route_flat, capacity)
        picked = low_back(moe_input[token_index])
        buffer = jnp.zeros((EXPERTS * capacity, D), jnp.float32).at[slot_index].set(picked)
        buffer = buffer.reshape(EXPERTS, capacity, D)
        gate_pre = low_back(jnp.einsum('ecd,edf->ecf', buffer, gate_w[layer_id], precision=lax.Precision.HIGHEST))
        up_pre = low_back(jnp.einsum('ecd,edf->ecf', buffer, up_w[layer_id], precision=lax.Precision.HIGHEST))
        activation = low(jax.nn.silu(gate_pre) * up_pre)
        out_rows = low(low_back(jnp.einsum('ecf,edf->ecd', activation, down_w[layer_id], precision=lax.Precision.HIGHEST)))
        per_route = out_rows.reshape(EXPERTS * capacity, D)[slot_index].reshape(SLOT, TOP, D)
        route_weights = gate_all[layer_id] * live_rows[:, None]
        hidden = after_attn + lax.optimization_barrier(jnp.sum(route_weights[:, :, None] * per_route, axis=1))
    return hidden

def reference(hidden_in, cotangent, lengths, routes, gates, norm_attn, w_query, w_key, w_value, w_output, norm_mlp, w_gate, w_up, w_down):
    params = tuple((param.astype(jnp.float32) for param in (norm_attn, w_query, w_key, w_value, w_output, norm_mlp, w_gate, w_up, w_down)))
    routes_slot = jnp.moveaxis(routes, 1, 0)
    gates_slot = jnp.moveaxis(gates, 1, 0).astype(jnp.float32)

    def slot_step(totals, inputs):
        hidden, grad_out, length, route_all, gate_all = inputs
        live_rows = (jnp.arange(SLOT, dtype=jnp.int32) < length).astype(jnp.float32)

        def forward(hidden_now, gate_now, param_now):
            return block_forward(hidden_now, gate_now, param_now, route_all, length)
        result, pullback = jax.vjp(forward, hidden.astype(jnp.float32), gate_all, params)
        hidden_grad, gate_grad, param_grads = pullback(grad_out.astype(jnp.float32) * live_rows[:, None])
        totals = jax.tree.map(lambda left_val, right_val: left_val + right_val, totals, param_grads)
        return (totals, (result.astype(jnp.bfloat16), hidden_grad, gate_grad))
    zero_grads = jax.tree.map(jnp.zeros_like, params)
    totals, (outputs, input_grads, gate_grads) = lax.scan(slot_step, zero_grads, (hidden_in, cotangent, lengths, routes_slot, gates_slot))
    return (outputs, input_grads, jnp.moveaxis(gate_grads, 0, 1), totals[0], totals[1], totals[2], totals[3], totals[4], totals[5], totals[6], totals[7], totals[8])
```

```python
import functools

import jax
import jax.numpy as jnp
from jax import lax
from jax.experimental import pallas as pl
from jax.experimental.pallas import tpu as pltpu
from jax.sharding import PartitionSpec as P

HD = 64
EPS = 1e-06
THETA = 10000.0
NEG_FILL = -1e30
MOST = 40
MIB = 1024 * 1024
F32 = jnp.float32
BF16 = jnp.bfloat16


def dot(left, right):
    return lax.dot_general(left, right, (((1,), (0,)), ((), ())), preferred_element_type=F32)


def dot_nt(left, right):
    return lax.dot_general(left, right, (((1,), (1,)), ((), ())), preferred_element_type=F32)


def dot_tn(left, right):
    return lax.dot_general(left, right, (((0,), (0,)), ((), ())), preferred_element_type=F32)


def split_low(value):
    high = value.astype(BF16)
    return high, (value - high.astype(F32)).astype(BF16)


def rms_parts(hidden):
    scale = lax.rsqrt(jnp.mean(hidden * hidden, axis=-1, keepdims=True) + EPS)
    return hidden * scale, scale


def rms_back(hidden, gain, grad):
    unit, scale = rms_parts(hidden)
    scaled = grad * gain
    return scale * (scaled - unit * jnp.mean(scaled * unit, axis=-1, keepdims=True))


def swap_halves(value):
    lane = lax.broadcasted_iota(jnp.int32, value.shape, 1) % HD
    return jnp.where(lane < HD // 2, pltpu.roll(value, 128 - HD // 2, 1), pltpu.roll(value, HD // 2, 1))


def low_lanes(shape):
    return lax.broadcasted_iota(jnp.int32, shape, 1) < HD


def call(kernel, outs, *args, vmem=48, scratch=(), **extra):
    return pl.pallas_call(
        kernel,
        out_shape=outs,
        scratch_shapes=scratch,
        compiler_params=pltpu.CompilerParams(vmem_limit_bytes=vmem * MIB),
        **extra,
    )(*args)


def shape(dims, dtype=BF16):
    return jax.ShapeDtypeStruct(dims, dtype)


def routing_kernel(routes_ref, gates_ref, live_ref, pick_ref, place_ref, high_ref, low_ref, high_t_ref, low_t_ref):
    experts, tokens = place_ref.shape[2] // MOST, routes_ref.shape[2]
    earlier = lax.broadcasted_iota(jnp.int32, (tokens, tokens), 0) < lax.broadcasted_iota(
        jnp.int32, (tokens, tokens), 1
    )
    earlier = earlier.astype(F32).astype(BF16)
    expert_id = lax.broadcasted_iota(jnp.int32, (experts, tokens), 0)
    place_id = lax.broadcasted_iota(jnp.int32, (experts, MOST, tokens), 1).astype(F32)
    for layer in range(routes_ref.shape[0]):
        named = jnp.zeros((experts, tokens), F32)
        weight = jnp.zeros((experts, tokens), F32)
        for k in range(routes_ref.shape[1]):
            same = routes_ref[layer, k : k + 1, :] == expert_id
            named = named + jnp.where(same, 1.0, 0.0)
            weight = weight + jnp.where(same, gates_ref[layer, k : k + 1, :], 0.0)
        weight = weight * live_ref[0:1, :]
        rank = dot(named.astype(BF16), earlier)
        rank = jnp.where(named > 0.5, rank, -1.0)
        here = rank[:, None, :] == place_id
        pick = jnp.where(here, 1.0, 0.0).reshape(experts * MOST, tokens)
        weights = jnp.where(here, weight[:, None, :], 0.0).reshape(experts * MOST, tokens)
        high, low = split_low(weights)
        pick_ref[layer] = pick.astype(BF16)
        place_ref[layer] = pick.T.astype(BF16)
        high_ref[layer] = high
        low_ref[layer] = low
        high_t_ref[layer] = high.astype(F32).T.astype(BF16)
        low_t_ref[layer] = low.astype(F32).T.astype(BF16)


def project(hidden, gain, w_ref, cos, sin, normed_ref, qkv_ref):
    unit, _ = rms_parts(hidden)
    normed = (unit * gain).astype(BF16)
    normed_ref[...] = normed
    width = hidden.shape[1]
    raw = dot(normed, w_ref[:, : 2 * width])
    groups = qkv_ref.shape[0]

    def turned(chunk):
        return chunk * cos + swap_halves(chunk) * sin

    low_half = low_lanes((hidden.shape[0], 128))
    for g in range(groups):
        qkv_ref[g, :, 0:128] = turned(raw[:, g * 128 : (g + 1) * 128]).astype(BF16)
    for j in range(groups // 2):
        key = turned(raw[:, width + j * 128 : width + (j + 1) * 128])
        value = raw[:, width + width // 2 + j * 128 : width + width // 2 + (j + 1) * 128]
        qkv_ref[2 * j, :, 128:256] = jnp.where(low_half, key, pltpu.roll(value, HD, 1)).astype(BF16)
        qkv_ref[2 * j + 1, :, 128:256] = jnp.where(low_half, pltpu.roll(key, HD, 1), value).astype(BF16)


def first_kernel(hidden_ref, w_ref, cos_ref, sin_ref, gains_ref, normed_ref, qkv_ref):
    width = hidden_ref.shape[1]
    gains = w_ref[:, 2 * width :].astype(F32).T[0:8, :]
    gains_ref[...] = gains
    project(hidden_ref[...].astype(F32), gains[0:1, :], w_ref, cos_ref[...], sin_ref[...], normed_ref, qkv_ref)


def middle_kernel(after_ref, back_ref, high_ref, low_ref, w_ref, gains_ref, cos_ref, sin_ref, hidden_ref, normed_ref, qkv_ref):
    back = back_ref[...]
    hidden = after_ref[...] + (dot(high_ref[...], back) + dot(low_ref[...], back))
    hidden_ref[...] = hidden
    project(hidden, gains_ref[2:3, :], w_ref, cos_ref[...], sin_ref[...], normed_ref, qkv_ref)


def attend_kernel(length_ref, qkv_ref, mixed_ref, total_ref, *, rows):
    slot = qkv_ref.shape[0]
    length = length_ref[0]
    keyval = qkv_ref[:, 128:256]
    low_half = low_lanes(keyval.shape)
    keyval_turned = pltpu.roll(keyval.astype(F32), HD, 1)
    keyval = keyval.astype(F32)
    zero = jnp.zeros_like(keyval)
    key_wide = (jnp.where(low_half, keyval, zero).astype(BF16), jnp.where(low_half, zero, keyval_turned).astype(BF16))
    value_wide = (jnp.where(low_half, keyval_turned, zero).astype(BF16), jnp.where(low_half, zero, keyval).astype(BF16))
    for block in range(slot // rows):
        span = (block + 1) * rows
        at = pl.ds(block * rows, rows)
        query = qkv_ref[at, 0:128]
        row_id = block * rows + lax.broadcasted_iota(jnp.int32, (rows, span), 0)
        col_id = lax.broadcasted_iota(jnp.int32, (rows, span), 1)
        allowed = (col_id <= row_id) & (col_id < length)
        mixed = jnp.zeros((rows, 128), F32)
        for head in range(2):
            scores = dot_nt(query, key_wide[head][:span]) * (HD**-0.5)
            scores = jnp.where(allowed, scores, NEG_FILL)
            top = jnp.max(scores, axis=-1, keepdims=True)
            expo = jnp.exp(scores - top)
            total = jnp.sum(expo, axis=-1, keepdims=True)
            probs = (expo * (1.0 / total)).astype(BF16)
            mixed = mixed + dot(probs, value_wide[head][:span])
            total_ref[at, head * HD : (head + 1) * HD] = jnp.broadcast_to(top + jnp.log(total), (rows, HD))
        mixed_ref[at, :] = mixed.astype(BF16)


def attend_back_kernel(length_ref, qkv_ref, total_ref, grad_ref, normed_ref, cos_ref, sin_ref, out_ref, dk_ref, dv_ref, *, rows):
    slot = qkv_ref.shape[0]
    length = length_ref[0]
    keyval = qkv_ref[:, 128:256].astype(F32)
    low_half = low_lanes(keyval.shape)
    keyval_turned = pltpu.roll(keyval, HD, 1)
    zero = jnp.zeros_like(keyval)
    key_wide = (jnp.where(low_half, keyval, zero).astype(BF16), jnp.where(low_half, zero, keyval_turned).astype(BF16))
    value_wide = (jnp.where(low_half, keyval_turned, zero).astype(BF16), jnp.where(low_half, zero, keyval).astype(BF16))
    dk_ref[...] = zero
    dv_ref[...] = zero
    low_row = low_lanes((rows, 128))
    zero_row = jnp.zeros((rows, 128), BF16)
    for block in range(slot // rows):
        span = (block + 1) * rows
        at = pl.ds(block * rows, rows)
        query = qkv_ref[at, 0:128]
        grad = grad_ref[at, :]
        row_id = block * rows + lax.broadcasted_iota(jnp.int32, (rows, span), 0)
        col_id = lax.broadcasted_iota(jnp.int32, (rows, span), 1)
        allowed = (col_id <= row_id) & (col_id < length)
        dq = jnp.zeros((rows, 128), F32)
        for head in range(2):
            keep = low_row if head == 0 else jnp.logical_not(low_row)
            scores = dot_nt(query, key_wide[head][:span]) * (HD**-0.5)
            scores = jnp.where(allowed, scores, NEG_FILL)
            probs = jnp.exp(scores - total_ref[at, head * HD : head * HD + 1])
            dprobs = dot_nt(grad, value_wide[head][:span])
            mean = jnp.sum(dprobs * probs, axis=-1, keepdims=True)
            dscores = (probs * (dprobs - mean)).astype(BF16)
            dq = dq + dot(dscores, key_wide[head][:span])
            dk_ref[:span, :] += dot_tn(dscores, jnp.where(keep, query, zero_row))
            dv_ref[:span, :] += dot_tn(probs.astype(BF16), jnp.where(keep, grad, zero_row))
        dq = dq * (HD**-0.5)
        out_ref[at, 0:128] = (dq * cos_ref[at, :] - swap_halves(dq) * sin_ref[at, :]).astype(BF16)
    dk = dk_ref[...]
    dk = (dk + pltpu.roll(dk, HD, 1)) * (HD**-0.5)
    dk = dk * cos_ref[...] - swap_halves(dk) * sin_ref[...]
    dv = dv_ref[...]
    dv = dv + pltpu.roll(dv, HD, 1)
    out_ref[:, 128:256] = jnp.where(low_half, dk, dv).astype(BF16)
    out_ref[:, 256:512] = dot_tn(normed_ref[...], out_ref[:, 0:256]).astype(BF16)


def after_kernel(mixed_ref, w_ref, hidden_ref, gains_ref, pick_ref, after_ref, send_ref, *, first, gain_row):
    mixed = jnp.concatenate([mixed_ref[g] for g in range(mixed_ref.shape[0])], axis=1)
    after = hidden_ref[...].astype(F32) + dot(mixed, w_ref[:, first:])
    after_ref[...] = after
    unit, _ = rms_parts(after)
    moe_in = (unit * gains_ref[gain_row : gain_row + 1, :]).astype(BF16)
    send_ref[...] = dot(pick_ref[...], moe_in).astype(BF16).reshape(send_ref.shape)


def pack(high, low, grad, send_ref):
    grad_high, grad_low = split_low(grad)
    rows = dot(high, grad_high) + (dot(low, grad_high) + dot(high, grad_low))
    send_ref[...] = rows.astype(BF16).reshape(send_ref.shape)


def cotangent_kernel(grad_ref, live_ref, high_ref, low_ref, dh_ref, send_ref):
    grad = grad_ref[...].astype(F32) * live_ref[...]
    dh_ref[...] = grad
    pack(high_ref[...], low_ref[...], grad, send_ref)


def after_back_kernel(back_ref, place_ref, after_ref, gains_ref, dh_ref, w_ref, dafter_ref, dattn_ref, dmixed_ref, *, first, gain_row):
    dmoe = dot(place_ref[...], back_ref[...])
    dafter = dh_ref[...] + rms_back(after_ref[...], gains_ref[gain_row : gain_row + 1, :], dmoe)
    dafter_ref[...] = dafter
    dattn = dafter.astype(BF16)
    dattn_ref[...] = dattn
    dmixed = dot_nt(dattn, w_ref[:, first:]).astype(BF16)
    for g in range(dmixed_ref.shape[0]):
        dmixed_ref[g] = dmixed[:, g * 128 : (g + 1) * 128]


def project_back(back_ref, w_ref, hidden, gain, dafter):
    width = hidden.shape[1]
    groups = back_ref.shape[0]
    low_half = low_lanes((hidden.shape[0], 128))
    parts = [back_ref[g, :, 0:128] for g in range(groups)]
    keys, values = [], []
    for j in range(groups // 2):
        even = back_ref[2 * j, :, 128:256].astype(F32)
        odd = back_ref[2 * j + 1, :, 128:256].astype(F32)
        keys.append(jnp.where(low_half, even, pltpu.roll(odd, HD, 1)).astype(BF16))
        values.append(jnp.where(low_half, pltpu.roll(even, HD, 1), odd).astype(BF16))
    grads = jnp.concatenate(parts + keys + values, axis=1)
    dnormed = dot_nt(grads, w_ref[:, : 2 * width])
    return dafter + rms_back(hidden, gain, dnormed)


def middle_back_kernel(back_ref, w_ref, hidden_ref, gains_ref, dafter_ref, high_ref, low_ref, dh_ref, send_ref):
    dh = project_back(back_ref, w_ref, hidden_ref[...], gains_ref[2:3, :], dafter_ref[...])
    dh_ref[...] = dh
    pack(high_ref[...], low_ref[...], dh, send_ref)


def last_back_kernel(back_ref, w_ref, hidden_ref, gains_ref, dafter_ref, dh_ref):
    dh_ref[...] = project_back(back_ref, w_ref, hidden_ref[...].astype(F32), gains_ref[0:1, :], dafter_ref[...])


def gate_grads(back, dh, pick_ref, routes_ref, out_ref):
    high, low = split_low(dh)
    slots, tokens = pick_ref.shape
    product = dot_nt(back, high) + dot_nt(back, low)
    product = product * pick_ref[...].astype(F32)
    each = jnp.sum(product.reshape(slots // MOST, MOST, tokens), axis=1)
    expert_id = lax.broadcasted_iota(jnp.int32, each.shape, 0)
    for k in range(routes_ref.shape[0]):
        out_ref[k : k + 1, :] = jnp.sum(
            jnp.where(routes_ref[k : k + 1, :] == expert_id, each, 0.0), axis=0, keepdims=True
        )


def gates_kernel(back_ref, dh_ref, live_ref, pick_ref, routes_ref, out_ref):
    gate_grads(back_ref[...], dh_ref[...] * live_ref[...], pick_ref, routes_ref, out_ref)


def final_kernel(after_ref, back_ref, high_ref, low_ref, dh_ref, pick_ref, routes_ref, hidden_ref, out_ref):
    back = back_ref[...]
    hidden = after_ref[...] + (dot(high_ref[...], back) + dot(low_ref[...], back))
    hidden_ref[...] = hidden.astype(BF16)
    gate_grads(back, dh_ref[...], pick_ref, routes_ref, out_ref)


def rows_of(ref, expert):
    both = ref[...].astype(F32)
    rows = both[:, expert * MOST : (expert + 1) * MOST, :]
    return rows.reshape(rows.shape[0] * MOST, rows.shape[2]).astype(BF16)


def weights_of(w_ref, which):
    part = w_ref[:, which]
    return part.reshape(part.shape[0] * part.shape[1], part.shape[2])


def put_rows(rows, expert, held_ref, out_ref):
    sources = out_ref.shape[0]
    rows = rows.reshape(sources, MOST, rows.shape[1])
    if expert == 0:
        held_ref[...] = rows
    else:
        out_ref[...] = jnp.concatenate([held_ref[...], rows], axis=1).astype(BF16)


def expert_kernel(x_ref, w_ref, y_ref, rows_ref, gate_ref, up_ref, act_ref, held_ref):
    def one(expert):
        rows = rows_of(x_ref, expert)
        rows_ref[0] = rows
        gate = dot(rows, weights_of(w_ref, 0))
        up = dot(rows, weights_of(w_ref, 1))
        gate_ref[0] = gate.astype(BF16)
        up_ref[0] = up.astype(BF16)
        act = (gate * (1.0 / (1.0 + jnp.exp(-gate))) * up).astype(BF16)
        act_ref[0] = act
        put_rows(dot_nt(act, weights_of(w_ref, 2)), expert, held_ref, y_ref)

    for expert in range(2):
        pl.when(pl.program_id(0) == expert)(functools.partial(one, expert))


def expert_back_kernel(dy_ref, w_ref, gate_ref, up_ref, dx_ref, rows_ref, dgate_ref, dup_ref, held_ref):
    def one(expert):
        rows = rows_of(dy_ref, expert)
        rows_ref[0] = rows
        dact = dot(rows, weights_of(w_ref, 2))
        gate = gate_ref[0].astype(F32)
        up = up_ref[0].astype(F32)
        sigma = 1.0 / (1.0 + jnp.exp(-gate))
        dgate = (dact * up * (sigma * (1.0 + gate * (1.0 - sigma)))).astype(BF16)
        dup = (dact * (gate * sigma)).astype(BF16)
        dgate_ref[0] = dgate
        dup_ref[0] = dup
        dx = dot_nt(dgate, weights_of(w_ref, 0)) + dot_nt(dup, weights_of(w_ref, 1))
        put_rows(dx, expert, held_ref, dx_ref)

    for expert in range(2):
        pl.when(pl.program_id(0) == expert)(functools.partial(one, expert))


def expert_grads_kernel(x_ref, dy_ref, act_ref, dgate_ref, dup_ref, out_ref):
    shards, _, rows, hidden = out_ref.shape
    x = x_ref[0]
    out_ref[:, 0] = dot_tn(x, dgate_ref[0]).astype(BF16).reshape(shards, rows, hidden)
    out_ref[:, 1] = dot_tn(x, dup_ref[0]).astype(BF16).reshape(shards, rows, hidden)
    out_ref[:, 2] = dot_tn(dy_ref[0], act_ref[0]).astype(BF16).reshape(shards, rows, hidden)


def whole_block(dims):
    return pl.BlockSpec(dims, lambda e: (0,) * len(dims))


def expert_block(dims):
    return pl.BlockSpec((1,) + dims, lambda e: (e,) + (0,) * len(dims))


def weight_block(dims):
    return pl.BlockSpec((dims[0], 3) + dims[2:], lambda e: (0, e, 0, 0))


def expert_call(kernel, specs, out_specs, outs, *args, scratch=()):
    return pl.pallas_call(
        kernel,
        grid=(2,),
        in_specs=specs,
        out_specs=out_specs,
        out_shape=outs,
        scratch_shapes=scratch,
        compiler_params=pltpu.CompilerParams(
            vmem_limit_bytes=56 * MIB, dimension_semantics=("arbitrary",)
        ),
    )(*args)


def on_device(
    hidden_in,
    cotangent,
    lengths,
    routes,
    gates,
    norm_attn,
    w_query,
    w_key,
    w_value,
    w_output,
    norm_mlp,
    w_gate,
    w_up,
    w_down,
):
    _, tokens, width = hidden_in.shape
    hidden_units = w_gate.shape[3]
    ep = lax.axis_size("ep")
    fsdp = lax.axis_size("fsdp")
    slot = tokens * fsdp
    slots = ep * 2 * MOST
    pair = 2 * MOST
    me = lax.axis_index("fsdp")

    def exchange(value, axis):
        return lax.all_to_all(value, axis, 0, 0, tiled=True)

    def gather(value):
        return lax.all_gather(value, "fsdp", axis=0, tiled=True)

    gains = jnp.stack([norm_attn[0], norm_mlp[0], norm_attn[1], norm_mlp[1]], axis=1)
    gains = jnp.pad(gains, ((0, 0), (0, 124)))
    attn_in = gather(jnp.concatenate([w_query[0], w_key[0], w_value[0], gains], axis=1))
    attn_out = gather(w_output[0])

    def expert_shard(layer):
        parts = [w[layer][e][None] for e in range(2) for w in (w_gate, w_up, w_down)]
        return lax.all_gather(jnp.concatenate(parts, axis=0), "fsdp", axis=0)

    experts_0 = expert_shard(0)
    attn_1 = gather(jnp.concatenate([w_query[1], w_key[1], w_value[1], w_output[1]], axis=1))
    experts_1 = expert_shard(1)
    attn_w = (attn_in, attn_1)
    out_w = ((attn_out, 0), (attn_1, 2 * width))
    expert_w = (experts_0, experts_1)

    positions = jnp.arange(slot, dtype=jnp.int32)
    lane = jnp.arange(128, dtype=jnp.int32)
    frequency = THETA ** (-2.0 * (lane % 32).astype(F32) / HD)
    angles = positions.astype(F32)[:, None] * frequency[None, :]
    cos_all = jnp.cos(angles)
    sin_all = jnp.sin(angles) * jnp.where(lane % HD < HD // 2, -1.0, 1.0)[None, :]
    cos_here = lax.dynamic_slice_in_dim(cos_all, me * tokens, tokens, 0)
    sin_here = lax.dynamic_slice_in_dim(sin_all, me * tokens, tokens, 0)
    live = (me * tokens + jnp.arange(tokens, dtype=jnp.int32) < lengths[0]).astype(F32)
    live_col = live[:, None]
    live_row = jnp.broadcast_to(live[None, :], (8, tokens))
    routes_t = jnp.swapaxes(routes[:, 0], 1, 2)
    gates_t = jnp.swapaxes(gates[:, 0], 1, 2)

    pick, place, high_t, low_t, high, low = call(
        routing_kernel,
        [shape((2, slots, tokens)), shape((2, tokens, slots)), shape((2, slots, tokens)), shape((2, slots, tokens))]
        + [shape((2, tokens, slots))] * 2,
        routes_t,
        gates_t,
        live_row,
    )
    send_shape = shape((ep, pair, width))

    dh_2, send = call(
        cotangent_kernel,
        [shape((tokens, width), F32), send_shape],
        cotangent[0],
        live_col,
        high_t[1],
        low_t[1],
    )
    dy_1 = exchange(send, "ep")

    def attend(qkv):
        received = exchange(qkv, "fsdp").reshape(slot, 256)
        mixed, total = call(
            functools.partial(attend_kernel, rows=256),
            [shape((slot, 128)), shape((slot, 128), F32)],
            lengths,
            received,
            in_specs=[pl.BlockSpec(memory_space=pltpu.SMEM), pl.BlockSpec(memory_space=pltpu.VMEM)],
        )
        return received, mixed, total, exchange(mixed.reshape(fsdp, tokens, 128), "fsdp")

    def to_experts(layer, hidden, mixed_back):
        w, first = out_w[layer]
        after, send = call(
            functools.partial(after_kernel, first=first, gain_row=2 * layer + 1),
            [shape((tokens, width), F32), send_shape],
            mixed_back,
            w,
            hidden,
            gains_all,
            pick[layer],
        )
        return after, exchange(send, "ep")

    rows_out = shape((2, ep * MOST, width))
    units_out = shape((2, ep * MOST, hidden_units))
    rows_spec, units_spec = expert_block((ep * MOST, width)), expert_block((ep * MOST, hidden_units))
    pair_spec = whole_block((ep, pair, width))
    held = [pltpu.VMEM((ep, MOST, width), F32)]

    def run_experts(layer, received):
        return expert_call(
            expert_kernel,
            [pair_spec, weight_block(expert_w[layer].shape)],
            [pair_spec, rows_spec, units_spec, units_spec, units_spec],
            [send_shape, rows_out, units_out, units_out, units_out],
            received,
            expert_w[layer],
            scratch=held,
        )

    def experts_back(layer, dy, kept):
        _, x, gate, up, act = kept
        dx, dy_rows, dgate, dup = expert_call(
            expert_back_kernel,
            [pair_spec, weight_block(expert_w[layer].shape), units_spec, units_spec],
            [pair_spec, rows_spec, units_spec, units_spec],
            [send_shape, rows_out, units_out, units_out],
            dy,
            expert_w[layer],
            gate,
            up,
            scratch=held,
        )
        back = exchange(dx, "ep").reshape(slots, width)
        (grads,) = expert_call(
            expert_grads_kernel,
            [rows_spec, rows_spec, units_spec, units_spec, units_spec],
            [weight_block(expert_w[layer].shape)],
            [shape(expert_w[layer].shape)],
            x,
            dy_rows,
            act,
            dgate,
            dup,
        )
        shard = lax.psum_scatter(grads, "fsdp", scatter_dimension=0, tiled=False)
        return back, shard

    def attention_back(layer, back, after, dh, qkv, total, normed_all):
        w, first = out_w[layer]
        dafter, dattn, dmixed = call(
            functools.partial(after_back_kernel, first=first, gain_row=2 * layer + 1),
            [shape((tokens, width), F32), shape((tokens, width)), shape((fsdp, tokens, 128))],
            back,
            place[layer],
            after,
            gains_all,
            dh,
            w,
        )
        dmixed = exchange(dmixed, "fsdp").reshape(slot, 128)
        vm = pl.BlockSpec(memory_space=pltpu.VMEM)
        grads = call(
            functools.partial(attend_back_kernel, rows=256),
            shape((slot, 512)),
            lengths,
            qkv,
            total,
            dmixed,
            normed_all,
            cos_all,
            sin_all,
            in_specs=[pl.BlockSpec(memory_space=pltpu.SMEM)] + [vm] * 6,
            scratch=[pltpu.VMEM((slot, 128), F32)] * 2,
        )
        return dafter, gather(dattn), exchange(grads.reshape(fsdp, tokens, 512), "fsdp")

    hidden_0 = hidden_in[0]
    gains_all, normed_0, qkv = call(
        first_kernel,
        [shape((8, width), F32), shape((tokens, width)), shape((fsdp, tokens, 256))],
        hidden_0,
        attn_w[0],
        cos_here,
        sin_here,
    )
    qkv_0, mixed_0, total_0, mixed_back = attend(qkv)
    after_0, received = to_experts(0, hidden_0, mixed_back)
    kept_0 = run_experts(0, received)
    y_0 = exchange(kept_0[0], "ep").reshape(slots, width)
    hidden_1, normed_1, qkv = call(
        middle_kernel,
        [shape((tokens, width), F32), shape((tokens, width)), shape((fsdp, tokens, 256))],
        after_0,
        y_0,
        high[0],
        low[0],
        attn_w[1],
        gains_all,
        cos_here,
        sin_here,
    )
    qkv_1, mixed_1, total_1, mixed_back = attend(qkv)
    after_1, received = to_experts(1, hidden_1, mixed_back)
    kept_1 = run_experts(1, received)

    normed_all = (gather(normed_0), gather(normed_1))
    back, shard_1 = experts_back(1, dy_1, kept_1)
    dafter, dattn_1, grads_1 = attention_back(1, back, after_1, dh_2, qkv_1, total_1, normed_all[1])
    dh_1, send = call(
        middle_back_kernel,
        [shape((tokens, width), F32), send_shape],
        grads_1,
        attn_w[1],
        hidden_1,
        gains_all,
        dafter,
        high_t[0],
        low_t[0],
    )
    dy_0 = exchange(send, "ep")
    back, shard_0 = experts_back(0, dy_0, kept_0)
    dafter, dattn_0, grads_0 = attention_back(0, back, after_0, dh_1, qkv_0, total_0, normed_all[0])
    dh_0 = call(
        last_back_kernel,
        shape((tokens, width), F32),
        grads_0,
        attn_w[0],
        hidden_0,
        gains_all,
        dafter,
    )

    y_late, grads_0 = lax.optimization_barrier((kept_1[0], grads_0))
    y_1 = exchange(y_late, "ep").reshape(slots, width)
    hidden_out, gate_grad_1 = call(
        final_kernel,
        [shape((tokens, width)), shape((8, tokens), F32)],
        after_1,
        y_1,
        high[1],
        low[1],
        dh_2,
        pick[1],
        routes_t[1],
    )
    gate_grad_0 = call(
        gates_kernel, shape((8, tokens), F32), y_0, dh_1, live_col, pick[0], routes_t[0]
    )
    gates_grad = jnp.swapaxes(jnp.stack([gate_grad_0, gate_grad_1]), 1, 2)[:, None]

    def output_grad(mixed, dattn_all):
        return lax.dot_general(
            mixed, dattn_all, (((0,), (0,)), ((), ())), preferred_element_type=F32
        ).astype(BF16)

    def mlp_gain(layer, shard):
        grads = shard.astype(F32)
        total = jnp.zeros((tokens,), F32)
        for e in range(2):
            total = total + jnp.sum(grads[3 * e] * w_gate[layer, e].astype(F32), axis=1)
            total = total + jnp.sum(grads[3 * e + 1] * w_up[layer, e].astype(F32), axis=1)
        return total / norm_mlp[layer].astype(F32)

    def sum_ep(value):
        side = 4

        def by(along, step):
            return [
                (z * side + x, ((z + step) % side) * side + x) if along else (z * side + x, z * side + (x + step) % side)
                for z in range(side)
                for x in range(side)
            ]

        for along in (0, 1):
            others = [lax.ppermute(value, "ep", by(along, step)) for step in (1, 2, 3)]
            value = sum((o.astype(F32) for o in others), value.astype(F32)).astype(BF16)
        return value

    def attn_sum(grads, mixed, dattn_all, gain_part):
        inner = jnp.concatenate([grads[g, :, 256:512] for g in range(fsdp)], axis=1)
        extra = jnp.pad(gain_part[:, None], ((0, 0), (0, 127)))
        extra = extra.astype(BF16)
        return sum_ep(jnp.concatenate([inner, output_grad(mixed, dattn_all), extra], axis=1))

    summed = (
        attn_sum(grads_0, mixed_0, dattn_0, mlp_gain(0, shard_0)),
        attn_sum(grads_1, mixed_1, dattn_1, mlp_gain(1, shard_1)),
    )

    query_grad, key_grad, value_grad, output_w_grad, attn_gain_grad, mlp_gain_grad = [], [], [], [], [], []
    for layer in range(2):
        total = summed[layer].astype(F32)
        inner = total[:, : 2 * width].reshape(tokens, fsdp, 256)
        query = inner[:, :, :128].reshape(tokens, width)
        key = inner[:, :, 128:192].reshape(tokens, width // 2)
        value = inner[:, :, 192:].reshape(tokens, width // 2)
        query_grad.append(query)
        key_grad.append(key)
        value_grad.append(value)
        output_w_grad.append(total[:, 2 * width : 3 * width])
        mlp_gain_grad.append(total[:, 3 * width])
        gain = (
            jnp.sum(query * w_query[layer].astype(F32), axis=1)
            + jnp.sum(key * w_key[layer].astype(F32), axis=1)
            + jnp.sum(value * w_value[layer].astype(F32), axis=1)
        )
        attn_gain_grad.append(gain / norm_attn[layer].astype(F32))

    def expert_out(which):
        return jnp.stack([jnp.stack([s[which], s[3 + which]]) for s in (shard_0, shard_1)]).astype(F32)

    return (
        hidden_out[None],
        dh_0[None],
        gates_grad,
        jnp.stack(attn_gain_grad),
        jnp.stack(query_grad),
        jnp.stack(key_grad),
        jnp.stack(value_grad),
        jnp.stack(output_w_grad),
        jnp.stack(mlp_gain_grad),
        expert_out(0),
        expert_out(1),
        expert_out(2),
    )


def solution(mesh):
    row = P(None, "fsdp", None)
    expert = P(None, "ep", "fsdp", None)
    hidden = P("ep", "fsdp", None)
    gain = P(None, "fsdp")
    return jax.shard_map(
        on_device,
        mesh=mesh,
        in_specs=(hidden, hidden, P("ep"), expert, expert, gain, row, row, row, row, gain, expert, expert, expert),
        out_specs=(hidden, hidden, expert, gain, row, row, row, row, gain, expert, expert, expert),
        check_vma=False,
    )
```

```python
import functools

import jax
import jax.numpy as jnp
import numpy as np
from jax import lax
from jax.experimental import pallas as pl
from jax.experimental.pallas import tpu as pltpu
from jax.sharding import PartitionSpec as P

HD = 64
EPS = 1e-06
THETA = 10000.0
NEG_FILL = -1e30
MOST = 40
MIB = 1024 * 1024
VMEM = 60
F32 = jnp.float32
BF16 = jnp.bfloat16


def dot(left, right):
    return lax.dot_general(left, right, (((1,), (0,)), ((), ())), preferred_element_type=F32)


def dot_nt(left, right):
    return lax.dot_general(left, right, (((1,), (1,)), ((), ())), preferred_element_type=F32)


def dot_tn(left, right):
    return lax.dot_general(left, right, (((0,), (0,)), ((), ())), preferred_element_type=F32)


def split_low(value):
    high = value.astype(BF16)
    return high, (value - high.astype(F32)).astype(BF16)


def rms_parts(hidden):
    scale = lax.rsqrt(jnp.mean(hidden * hidden, axis=-1, keepdims=True) + EPS)
    return hidden * scale, scale


def rms_back(hidden, gain, grad):
    unit, scale = rms_parts(hidden)
    scaled = grad * gain
    return scale * (scaled - unit * jnp.mean(scaled * unit, axis=-1, keepdims=True))


def swap_halves(value):
    lane = lax.broadcasted_iota(jnp.int32, value.shape, 1) % HD
    return jnp.where(lane < HD // 2, pltpu.roll(value, 128 - HD // 2, 1), pltpu.roll(value, HD // 2, 1))


def low_lanes(shape):
    return lax.broadcasted_iota(jnp.int32, shape, 1) < HD


def call(kernel, outs, *args, vmem=VMEM, scratch=(), **extra):
    return pl.pallas_call(
        kernel,
        out_shape=outs,
        scratch_shapes=scratch,
        compiler_params=pltpu.CompilerParams(vmem_limit_bytes=vmem * MIB),
        **extra,
    )(*args)


def shape(dims, dtype=BF16):
    return jax.ShapeDtypeStruct(dims, dtype)


def routing_kernel(routes_ref, gates_ref, live_ref, *out_refs):
    experts, tokens = out_refs[0].shape[0] // MOST, routes_ref.shape[2]
    earlier = lax.broadcasted_iota(jnp.int32, (tokens, tokens), 0) < lax.broadcasted_iota(
        jnp.int32, (tokens, tokens), 1
    )
    earlier = earlier.astype(F32).astype(BF16)
    expert_id = lax.broadcasted_iota(jnp.int32, (experts, tokens), 0)
    place_id = lax.broadcasted_iota(jnp.int32, (experts, MOST, tokens), 1).astype(F32)
    for layer in range(routes_ref.shape[0]):
        named = jnp.zeros((experts, tokens), F32)
        weight = jnp.zeros((experts, tokens), F32)
        for k in range(routes_ref.shape[1]):
            same = routes_ref[layer, k : k + 1, :] == expert_id
            named = named + jnp.where(same, 1.0, 0.0)
            weight = weight + jnp.where(same, gates_ref[layer, k : k + 1, :], 0.0)
        weight = weight * live_ref[0:1, :]
        rank = dot(named.astype(BF16), earlier)
        rank = jnp.where(named > 0.5, rank, -1.0)
        here = rank[:, None, :] == place_id
        pick = jnp.where(here, 1.0, 0.0).reshape(experts * MOST, tokens)
        weights = jnp.where(here, weight[:, None, :], 0.0).reshape(experts * MOST, tokens)
        high, low = split_low(weights)
        outs = out_refs[6 * layer : 6 * layer + 6]
        outs[0][...] = pick.astype(BF16)
        outs[1][...] = pick.T.astype(BF16)
        outs[2][...] = high
        outs[3][...] = low
        outs[4][...] = high.astype(F32).T.astype(BF16)
        outs[5][...] = low.astype(F32).T.astype(BF16)


def put_groups(wq_ref, wk_ref, wv_ref, out_ref):
    rows = wq_ref.shape[1]
    low_half = low_lanes((rows, 128))
    groups = wq_ref.shape[2] // 128
    for g in range(groups):
        out_ref[g, 0:rows, 0:128] = wq_ref[0, :, g * 128 : (g + 1) * 128]
    for j in range(groups // 2):
        key = wk_ref[0, :, j * 128 : (j + 1) * 128].astype(F32)
        value = wv_ref[0, :, j * 128 : (j + 1) * 128].astype(F32)
        out_ref[2 * j, 0:rows, 128:256] = jnp.where(low_half, key, pltpu.roll(value, HD, 1)).astype(BF16)
        out_ref[2 * j + 1, 0:rows, 128:256] = jnp.where(low_half, pltpu.roll(key, HD, 1), value).astype(BF16)


def group_kernel(wq_ref, wk_ref, wv_ref, wo_ref, attn_ref, mlp_ref, out_ref, wo_out_ref):
    gains = jnp.concatenate([attn_ref[...].astype(F32), mlp_ref[...].astype(F32)], axis=1)
    gains = jnp.concatenate([gains, jnp.zeros((14, 256), F32)], axis=0).astype(BF16)
    put_groups(wq_ref, wk_ref, wv_ref, out_ref)
    wo_out_ref[...] = wo_ref[0]
    for g in range(out_ref.shape[0]):
        out_ref[g, wq_ref.shape[1] :, :] = gains


def shards_kernel(wq_ref, wk_ref, wv_ref, wo_ref, gate_ref, up_ref, down_ref, attn_ref, *expert_refs):
    put_groups(wq_ref, wk_ref, wv_ref, attn_ref)
    groups = wq_ref.shape[2] // 128
    for j in range(attn_ref.shape[0] - groups):
        attn_ref[groups + j] = wo_ref[0, :, j * 256 : (j + 1) * 256]
    for layer, out_ref in enumerate(expert_refs):
        for e in range(2):
            out_ref[3 * e] = gate_ref[layer, e]
            out_ref[3 * e + 1] = up_ref[layer, e]
            out_ref[3 * e + 2] = down_ref[layer, e]


def fetch(source, held_ref, sem):
    copy = pltpu.make_async_copy(source, held_ref, sem)
    copy.start()
    return copy


def blocks_of(w_ref, groups):
    return w_ref if len(w_ref.shape) == 2 else w_ref.at[:, pl.ds(groups, w_ref.shape[1] - groups)]


def times_output(mixed, held_ref):
    if len(held_ref.shape) == 2:
        return dot(mixed, held_ref[...])
    return jnp.concatenate(
        [dot(mixed, held_ref[:, j].reshape(mixed.shape[1], 256)) for j in range(held_ref.shape[1])], axis=1
    )


def times_output_t(grad, held_ref):
    if len(held_ref.shape) == 2:
        return dot_nt(grad, held_ref[...])
    return sum(
        dot_nt(grad[:, j * 256 : (j + 1) * 256], held_ref[:, j].reshape(grad.shape[1], 256))
        for j in range(held_ref.shape[1])
    )


def relative(me, cores, count, step, flip):
    return lax.rem(me // cores - step + count, count) * cores + lax.rem(me % cores + flip, cores)


def turned(chunk, cos, sin):
    return chunk * cos + swap_halves(chunk) * sin


def attend(length, qkv_ref, rows, put):
    slot = qkv_ref.shape[0]
    keyval = qkv_ref[:, 128:256].astype(F32)
    low_half = low_lanes(keyval.shape)
    keyval_turned = pltpu.roll(keyval, HD, 1)
    zero = jnp.zeros_like(keyval)
    key_wide = (jnp.where(low_half, keyval, zero).astype(BF16), jnp.where(low_half, zero, keyval_turned).astype(BF16))
    value_wide = (jnp.where(low_half, keyval_turned, zero).astype(BF16), jnp.where(low_half, zero, keyval).astype(BF16))
    for block in range(slot // rows):
        span = (block + 1) * rows
        query = qkv_ref[pl.ds(block * rows, rows), 0:128]
        row_id = block * rows + lax.broadcasted_iota(jnp.int32, (rows, span), 0)
        col_id = lax.broadcasted_iota(jnp.int32, (rows, span), 1)
        allowed = (col_id <= row_id) & (col_id < length)
        mixed = jnp.zeros((rows, 128), F32)
        totals = []
        for head in range(2):
            scores = dot_nt(query, key_wide[head][:span]) * (HD**-0.5)
            scores = jnp.where(allowed, scores, NEG_FILL)
            top = jnp.max(scores, axis=-1, keepdims=True)
            expo = jnp.exp(scores - top)
            total = jnp.sum(expo, axis=-1, keepdims=True)
            probs = (expo * (1.0 / total)).astype(BF16)
            mixed = mixed + dot(probs, value_wide[head][:span])
            totals.append(top + jnp.log(total))
        put(block, mixed.astype(BF16), totals)


def first_kernel(
    me_ref, length_ref, *refs, pieces, cores, rows
):
    moved = refs[: len(pieces)]
    w_ref, cos_ref, sin_ref, gains_ref, normed_ref, qkv_ref, mixed_ref, total_ref = refs[len(pieces) :]
    me = me_ref[0]
    shards, _, _ = w_ref.shape
    tokens = moved[0].shape[0]
    for row in range(2):
        for half in range(2):
            gains_ref[2 * row + half : 2 * row + half + 1, :] = jnp.concatenate(
                [w_ref[s, tokens + row : tokens + row + 1, half * 128 : (half + 1) * 128] for s in range(shards)], axis=1
            ).astype(F32)
    gain = gains_ref[0:1, :]
    for (step, flip), piece in zip(pieces, moved):
        at = relative(me, cores, shards // cores, step, flip) * tokens
        unit, _ = rms_parts(piece[...].astype(F32))
        normed_ref[pl.ds(pl.multiple_of(at, tokens), tokens), :] = (unit * gain).astype(BF16)
    weights = w_ref[:, :tokens, :].reshape(shards * tokens, 256)
    raw = dot(normed_ref[...], weights)
    cos, sin = cos_ref[...], sin_ref[...]
    qkv_ref[:, 0:128] = turned(raw[:, 0:128], cos, sin).astype(BF16)
    keyval = raw[:, 128:256]
    qkv_ref[:, 128:256] = jnp.where(low_lanes(keyval.shape), turned(keyval, cos, sin), keyval).astype(BF16)

    def put(block, mixed, totals):
        at = pl.ds(block * rows, rows)
        mixed_ref[at, :] = mixed
        for head in range(2):
            total_ref[at, head * HD : (head + 1) * HD] = jnp.broadcast_to(totals[head], (rows, HD))

    attend(length_ref[0], qkv_ref, rows, put)


def second_kernel(me_ref, length_ref, *refs, pieces, cores, rows):
    moved = refs[: len(pieces)]
    w_ref, cos_ref, sin_ref, normed_ref, qkv_ref, total_ref = refs[len(pieces) : len(pieces) + 6]
    mixed_refs = refs[len(pieces) + 6 :]
    me = me_ref[0]
    tokens = moved[0].shape[0]
    devices = normed_ref.shape[0] // tokens
    chips = devices // cores
    for (step, flip), piece in zip(pieces, moved):
        at = relative(me, cores, chips, step, flip) * tokens
        normed_ref[pl.ds(pl.multiple_of(at, tokens), tokens), :] = piece[...]
    normed = normed_ref[...]
    cos, sin = cos_ref[...], sin_ref[...]
    raw = dot(normed, w_ref[...].reshape(normed.shape[1], 256))
    qkv_ref[:, 0:128] = turned(raw[:, 0:128], cos, sin).astype(BF16)
    keyval = raw[:, 128:256]
    qkv_ref[:, 128:256] = jnp.where(low_lanes(keyval.shape), turned(keyval, cos, sin), keyval).astype(BF16)

    def put(block, mixed, totals):
        at = pl.ds(block * rows, rows)
        for head in range(2):
            total_ref[at, head * HD : (head + 1) * HD] = jnp.broadcast_to(totals[head], (rows, HD))
        for part in range(rows // tokens):
            owner = block * (rows // tokens) + part
            piece = mixed[part * tokens : (part + 1) * tokens]
            step = lax.rem(owner // cores - me // cores + chips, chips)
            flip = lax.rem(owner % cores + me % cores, cores)
            for k in range(chips):

                @pl.when(step == k)
                def _():
                    mixed_refs[k][flip] = piece

    attend(length_ref[0], qkv_ref, rows, put)


def middle_kernel(after_ref, back_ref, high_ref, low_ref, gains_ref, hidden_ref, normed_ref):
    back = back_ref[...]
    hidden = after_ref[...] + (dot(high_ref[...], back) + dot(low_ref[...], back))
    hidden_ref[...] = hidden
    unit, _ = rms_parts(hidden)
    normed_ref[...] = (unit * gains_ref[2:3, :]).astype(BF16)


def attend_back_kernel(length_ref, qkv_ref, total_ref, grad_ref, normed_ref, cos_ref, sin_ref, out_ref, dk_ref, dv_ref, *, rows):
    slot = qkv_ref.shape[0]
    length = length_ref[0]
    keyval = qkv_ref[:, 128:256].astype(F32)
    low_half = low_lanes(keyval.shape)
    keyval_turned = pltpu.roll(keyval, HD, 1)
    zero = jnp.zeros_like(keyval)
    key_wide = (jnp.where(low_half, keyval, zero).astype(BF16), jnp.where(low_half, zero, keyval_turned).astype(BF16))
    value_wide = (jnp.where(low_half, keyval_turned, zero).astype(BF16), jnp.where(low_half, zero, keyval).astype(BF16))
    dk_ref[...] = zero
    dv_ref[...] = zero
    low_row = low_lanes((rows, 128))
    zero_row = jnp.zeros((rows, 128), BF16)
    for block in range(slot // rows):
        span = (block + 1) * rows
        at = pl.ds(block * rows, rows)
        query = qkv_ref[at, 0:128]
        grad = grad_ref[at, :]
        row_id = block * rows + lax.broadcasted_iota(jnp.int32, (rows, span), 0)
        col_id = lax.broadcasted_iota(jnp.int32, (rows, span), 1)
        allowed = (col_id <= row_id) & (col_id < length)
        dq = jnp.zeros((rows, 128), F32)
        for head in range(2):
            keep = low_row if head == 0 else jnp.logical_not(low_row)
            scores = dot_nt(query, key_wide[head][:span]) * (HD**-0.5)
            scores = jnp.where(allowed, scores, NEG_FILL)
            probs = jnp.exp(scores - total_ref[at, head * HD : head * HD + 1])
            dprobs = dot_nt(grad, value_wide[head][:span])
            mean = jnp.sum(dprobs * probs, axis=-1, keepdims=True)
            dscores = (probs * (dprobs - mean)).astype(BF16)
            dq = dq + dot(dscores, key_wide[head][:span])
            dk_ref[:span, :] += dot_tn(dscores, jnp.where(keep, query, zero_row))
            dv_ref[:span, :] += dot_tn(probs.astype(BF16), jnp.where(keep, grad, zero_row))
        dq = dq * (HD**-0.5)
        out_ref[at, 0:128] = (dq * cos_ref[at, :] - swap_halves(dq) * sin_ref[at, :]).astype(BF16)
    dk = dk_ref[...]
    dk = (dk + pltpu.roll(dk, HD, 1)) * (HD**-0.5)
    dk = dk * cos_ref[...] - swap_halves(dk) * sin_ref[...]
    dv = dv_ref[...]
    dv = dv + pltpu.roll(dv, HD, 1)
    out_ref[:, 128:256] = jnp.where(low_half, dk, dv).astype(BF16)
    out_ref[:, 256:512] = dot_tn(normed_ref[...], out_ref[:, 0:256]).astype(BF16)


def after_step(mixed, copy, held_ref, hidden_ref, gain, pick_ref, after_ref, send_ref):
    copy.wait()
    after = hidden_ref[...].astype(F32) + times_output(mixed, held_ref)
    after_ref[...] = after
    unit, _ = rms_parts(after)
    send_ref[...] = dot(pick_ref[...], (unit * gain).astype(BF16)).astype(BF16).reshape(send_ref.shape)


def after_first_kernel(
    mixed_ref, w_ref, hidden_ref, gains_ref, pick_ref, mixed_out_ref, after_ref, send_ref, held_ref, sem
):
    copy = fetch(w_ref, held_ref, sem)
    mixed = jnp.concatenate([mixed_ref[g] for g in range(mixed_ref.shape[0])], axis=1)
    mixed_out_ref[...] = mixed
    after_step(mixed, copy, held_ref, hidden_ref, gains_ref[1:2, :], pick_ref, after_ref, send_ref)


def after_second_kernel(me_ref, *refs, steps, cores, groups):
    moved, mate_ref = refs[: len(steps)], refs[len(steps)]
    w_ref, hidden_ref, gains_ref, pick_ref, mixed_out_ref, after_ref, send_ref, held_ref, sem = refs[len(steps) + 1 :]
    copy = fetch(blocks_of(w_ref, groups), held_ref, sem)
    me = me_ref[0]
    for k, step in enumerate(steps):
        own = relative(me, cores, len(steps), step, 0) * 128
        mixed_out_ref[:, pl.ds(pl.multiple_of(own, 128), 128)] = moved[k][0]
        other = relative(me, cores, len(steps), step, 1) * 128
        mixed_out_ref[:, pl.ds(pl.multiple_of(other, 128), 128)] = mate_ref[k]
    after_step(mixed_out_ref[...], copy, held_ref, hidden_ref, gains_ref[3:4, :], pick_ref, after_ref, send_ref)


def pack(high, low, grad, send_ref):
    grad_high, grad_low = split_low(grad)
    rows = dot(high, grad_high) + (dot(low, grad_high) + dot(high, grad_low))
    send_ref[...] = rows.astype(BF16).reshape(send_ref.shape)


def cotangent_kernel(grad_ref, live_ref, high_ref, low_ref, dh_ref, send_ref):
    grad = grad_ref[...].astype(F32) * live_ref[...]
    dh_ref[...] = grad
    pack(high_ref[...], low_ref[...], grad, send_ref)


def after_back_kernel(
    back_ref, place_ref, after_ref, gains_ref, dh_ref, w_ref, dafter_ref, dattn_ref, dmixed_ref, held_ref, sem, *, groups, gain_row
):
    copy = fetch(blocks_of(w_ref, groups), held_ref, sem)
    dmoe = dot(place_ref[...], back_ref[...])
    dafter = dh_ref[...] + rms_back(after_ref[...], gains_ref[gain_row : gain_row + 1, :], dmoe)
    dafter_ref[...] = dafter
    dattn = dafter.astype(BF16)
    dattn_ref[...] = dattn
    copy.wait()
    dmixed = times_output_t(dattn, held_ref).astype(BF16)
    for g in range(dmixed_ref.shape[0]):
        dmixed_ref[g] = dmixed[:, g * 128 : (g + 1) * 128]


def project_back(back_ref, w_ref, held_ref, sem, hidden, gain, dafter):
    groups = back_ref.shape[0]
    copy = fetch(w_ref.at[:, pl.ds(0, groups)], held_ref, sem)
    grads = jnp.concatenate([back_ref[g, :, 0:256] for g in range(groups)], axis=1)
    rows = back_ref.shape[1]
    copy.wait()
    dnormed = [
        dot_nt(grads, jnp.concatenate([held_ref[s, g, 0:rows] for g in range(groups)], axis=1))
        for s in range(held_ref.shape[0])
    ]
    return dafter + rms_back(hidden, gain, jnp.concatenate(dnormed, axis=1))


def middle_back_kernel(
    back_ref, w_ref, hidden_ref, gains_ref, dafter_ref, high_ref, low_ref, dh_ref, send_ref, held_ref, sem
):
    dh = project_back(back_ref, w_ref, held_ref, sem, hidden_ref[...], gains_ref[2:3, :], dafter_ref[...])
    dh_ref[...] = dh
    pack(high_ref[...], low_ref[...], dh, send_ref)


def last_back_kernel(back_ref, w_ref, hidden_ref, gains_ref, dafter_ref, dh_ref, held_ref, sem):
    dh_ref[...] = project_back(
        back_ref, w_ref, held_ref, sem, hidden_ref[...].astype(F32), gains_ref[0:1, :], dafter_ref[...]
    )


def chunks_kernel(place_ref, back_ref, part_ref, *refs):
    *chunk_refs, whole_ref = refs
    groups = back_ref.shape[0]
    for g in range(groups):
        whole_ref[:, g * 256 : (g + 1) * 256] = back_ref[g, :, 256:512]
    whole_ref[:, groups * 256 :] = part_ref[...]
    count = len(chunk_refs)
    size = whole_ref.shape[0] // count
    for k, chunk_ref in enumerate(chunk_refs):
        at = lax.rem(place_ref[0] + k, count) * size
        chunk_ref[...] = whole_ref[pl.ds(pl.multiple_of(at, size), size), :]


def sum_split_kernel(place_ref, *refs, count):
    arrived, chunk_refs, held_ref = refs[:count], refs[count:-1], refs[-1]
    held_ref[...] = sum((r[...].astype(F32) for r in arrived[1:]), arrived[0][...].astype(F32))
    size = held_ref.shape[0] // count
    for k, chunk_ref in enumerate(chunk_refs):
        at = lax.rem(place_ref[1] + k, count) * size
        chunk_ref[...] = held_ref[pl.ds(pl.multiple_of(at, size), size), :].astype(BF16)


def sum_kernel(*refs):
    refs[-1][...] = sum((r[...].astype(F32) for r in refs[1:-1]), refs[0][...].astype(F32)).astype(BF16)


def join_kernel(place_ref, *refs, count):
    arrived, out_ref, held_ref = refs[:count], refs[count], refs[count + 1]
    size = arrived[0].shape[0]
    for k, piece in enumerate(arrived):
        at = lax.rem(place_ref[1] - k + count, count) * size
        held_ref[pl.ds(pl.multiple_of(at, size), size), :] = piece[...].astype(F32)
    out_ref[...] = held_ref[...].astype(BF16)


def attention_out_kernel(
    place_ref, *refs, count
):
    arrived = (refs[:count], refs[count : 2 * count])
    (wq_ref, wk_ref, wv_ref, gain_ref, query_ref, key_ref, value_ref, out_ref, attn_ref, mlp_ref, *held_refs) = refs[2 * count :]
    size = arrived[0][0].shape[0]
    width = wq_ref.shape[2]
    for layer in range(2):
        for k, piece in enumerate(arrived[layer]):
            at = lax.rem(place_ref[0] - k + count, count) * size
            held_refs[layer][pl.ds(pl.multiple_of(at, size), size), :] = piece[...]
    low_half = low_lanes((size * count, 128))
    for layer, ref in enumerate(held_refs):
        total = jnp.zeros(low_half.shape, F32)
        for g in range(width // 128):
            query = ref[:, g * 256 : g * 256 + 128].astype(F32)
            query_ref[layer, :, g * 128 : (g + 1) * 128] = query
            total = total + query * wq_ref[layer, :, g * 128 : (g + 1) * 128].astype(F32)
        for j in range(width // 256):
            even = ref[:, 512 * j + 128 : 512 * j + 256].astype(F32)
            odd = ref[:, 512 * j + 384 : 512 * j + 512].astype(F32)
            key = jnp.where(low_half, even, pltpu.roll(odd, HD, 1))
            value = jnp.where(low_half, pltpu.roll(even, HD, 1), odd)
            at = slice(j * 128, (j + 1) * 128)
            key_ref[layer, :, at] = key
            value_ref[layer, :, at] = value
            total = total + key * wk_ref[layer, :, at].astype(F32) + value * wv_ref[layer, :, at].astype(F32)
        out_ref[layer] = ref[:, 2 * width : 3 * width].astype(F32)
        gain = jnp.sum(total, axis=1, keepdims=True) / gain_ref[:, layer : layer + 1]
        attn_ref[layer : layer + 1, :] = jnp.broadcast_to(gain, low_half.shape).T[0:1, :]
        mlp_ref[layer : layer + 1, :] = ref[:, 3 * width :].astype(F32).T[0:1, :]


def part_kernel(shard_ref, gate_ref, up_ref, gain_ref, part_ref):
    total = jnp.zeros(gate_ref.shape[1:], F32)
    for e in range(2):
        total = total + shard_ref[3 * e].astype(F32) * gate_ref[e].astype(F32)
        total = total + shard_ref[3 * e + 1].astype(F32) * up_ref[e].astype(F32)
    hidden = total.shape[1]
    part_ref[:, 0:hidden] = shard_ref[6]
    part_ref[:, hidden : 2 * hidden] = shard_ref[7]
    gain = jnp.sum(total, axis=1, keepdims=True) / gain_ref[...]
    lane = lax.broadcasted_iota(jnp.int32, (total.shape[0], 128), 1)
    part_ref[:, 2 * hidden :] = jnp.where(lane == 0, gain, 0.0).astype(BF16)


def expert_out_kernel(first_ref, second_ref, gate_ref, up_ref, down_ref):
    for layer, ref in enumerate((first_ref, second_ref)):
        for e in range(2):
            gate_ref[layer, e] = ref[3 * e].astype(F32)
            up_ref[layer, e] = ref[3 * e + 1].astype(F32)
            down_ref[layer, e] = ref[3 * e + 2].astype(F32)


def output_grads_kernel(mixed_ref, dattn_ref, _, out_ref):
    shards, halves, rows, hidden = out_ref.shape
    grads = dot_tn(mixed_ref[...], dattn_ref[...]).astype(BF16)
    for half in range(halves):
        out_ref[:, half] = grads[:, half * hidden : (half + 1) * hidden].reshape(shards, rows, hidden)


def gate_grads(back, dh, pick_ref, routes_ref, out_ref):
    high, low = split_low(dh)
    slots, tokens = pick_ref.shape
    product = dot_nt(back, high) + dot_nt(back, low)
    product = product * pick_ref[...].astype(F32)
    each = jnp.sum(product.reshape(slots // MOST, MOST, tokens), axis=1)
    expert_id = lax.broadcasted_iota(jnp.int32, each.shape, 0)
    for k in range(routes_ref.shape[0]):
        out_ref[k : k + 1, :] = jnp.sum(
            jnp.where(routes_ref[k : k + 1, :] == expert_id, each, 0.0), axis=0, keepdims=True
        )


def gates_kernel(back_ref, dh_ref, live_ref, pick_ref, routes_ref, out_ref):
    gate_grads(back_ref[...], dh_ref[...] * live_ref[...], pick_ref, routes_ref, out_ref)


def final_kernel(after_ref, sums_ref, live_ref, routes_ref, hidden_ref, out_ref):
    width = after_ref.shape[1]
    hidden_ref[...] = (after_ref[...] + sums_ref[:, 0:width].astype(F32)).astype(BF16)
    each = sums_ref[:, width:].astype(F32).T * live_ref[0:1, :]
    expert_id = lax.broadcasted_iota(jnp.int32, each.shape, 0)
    for k in range(routes_ref.shape[0]):
        out_ref[k : k + 1, :] = jnp.sum(
            jnp.where(routes_ref[k : k + 1, :] == expert_id, each, 0.0), axis=0, keepdims=True
        )


def rows_of(ref, expert):
    both = ref[...].astype(F32)
    rows = both[:, expert * MOST : (expert + 1) * MOST, :]
    return rows.reshape(rows.shape[0] * MOST, rows.shape[2]).astype(BF16)


def weights_of(w_ref, which):
    part = w_ref[:, which]
    return part.reshape(part.shape[0] * part.shape[1], part.shape[2])


def put_rows(rows, expert, held_ref, out_ref):
    sources = out_ref.shape[0]
    rows = rows.reshape(sources, MOST, rows.shape[1])
    if expert == 0:
        held_ref[...] = rows
    else:
        out_ref[...] = jnp.concatenate([held_ref[...], rows], axis=1).astype(BF16)


def expert_kernel(x_ref, w_ref, y_ref, rows_ref, gate_ref, up_ref, act_ref, held_ref):
    def one(expert):
        rows = rows_of(x_ref, expert)
        rows_ref[0] = rows
        gate = dot(rows, weights_of(w_ref, 0))
        up = dot(rows, weights_of(w_ref, 1))
        gate_ref[0] = gate.astype(BF16)
        up_ref[0] = up.astype(BF16)
        act = (gate * (1.0 / (1.0 + jnp.exp(-gate))) * up).astype(BF16)
        act_ref[0] = act
        put_rows(dot_nt(act, weights_of(w_ref, 2)), expert, held_ref, y_ref)

    for expert in range(2):
        pl.when(pl.program_id(0) == expert)(functools.partial(one, expert))


def expert_back_kernel(dy_ref, w_ref, gate_ref, up_ref, act_ref, dx_ref, rows_ref, dgate_ref, dup_ref, sums_ref, held_ref):
    def one(expert):
        rows = rows_of(dy_ref, expert)
        rows_ref[0] = rows
        dact = dot(rows, weights_of(w_ref, 2))
        sums = jnp.sum(dact * act_ref[0].astype(F32), axis=1, keepdims=True)
        sums_ref[0] = jnp.broadcast_to(sums, sums_ref.shape[1:])
        gate = gate_ref[0].astype(F32)
        up = up_ref[0].astype(F32)
        sigma = 1.0 / (1.0 + jnp.exp(-gate))
        dgate = (dact * up * (sigma * (1.0 + gate * (1.0 - sigma)))).astype(BF16)
        dup = (dact * (gate * sigma)).astype(BF16)
        dgate_ref[0] = dgate
        dup_ref[0] = dup
        dx = dot_nt(dgate, weights_of(w_ref, 0)) + dot_nt(dup, weights_of(w_ref, 1))
        put_rows(dx, expert, held_ref, dx_ref)

    for expert in range(2):
        pl.when(pl.program_id(0) == expert)(functools.partial(one, expert))


def expert_grads_kernel(x_ref, dy_ref, act_ref, dgate_ref, dup_ref, out_ref):
    shards, _, rows, hidden = out_ref.shape
    x = x_ref[0]
    out_ref[:, 0] = dot_tn(x, dgate_ref[0]).astype(BF16).reshape(shards, rows, hidden)
    out_ref[:, 1] = dot_tn(x, dup_ref[0]).astype(BF16).reshape(shards, rows, hidden)
    out_ref[:, 2] = dot_tn(dy_ref[0], act_ref[0]).astype(BF16).reshape(shards, rows, hidden)


def return_kernel(place_ref, y_ref, sums_ref, meta_ref, out_ref):
    sources, pair, width = y_ref.shape
    tokens = meta_ref.shape[2]
    top, side = 8, 4
    first = (place_ref[2] * 2).astype(F32)
    earlier = lax.broadcasted_iota(jnp.int32, (tokens, tokens), 0) < lax.broadcasted_iota(
        jnp.int32, (tokens, tokens), 1
    )
    earlier = earlier.astype(F32).astype(BF16)
    named, gates, live = [], [], []
    for s in range(sources):
        came = lax.rem(place_ref[1] - s // side + side, side) * side + lax.rem(place_ref[0] - s % side + side, side)
        meta = meta_ref[came]
        routes, weight = meta[0:top], meta[top : 2 * top]
        for e in range(2):
            same = routes == first + e
            named.append(jnp.sum(jnp.where(same, 1.0, 0.0), axis=0, keepdims=True))
            gates.append(jnp.sum(jnp.where(same, weight, 0.0), axis=0, keepdims=True))
            live.append(meta[2 * top : 2 * top + 1])
    named = jnp.concatenate(named, axis=0)
    gates = jnp.concatenate(gates, axis=0)
    live = jnp.concatenate(live, axis=0)
    rank = jnp.where(named > 0.5, dot(named.astype(BF16), earlier), -1.0)
    place_id = lax.broadcasted_iota(jnp.int32, (2 * sources, MOST, tokens), 1).astype(F32)
    here = rank[:, None, :] == place_id
    sums = jnp.concatenate(
        [sums_ref[e, s * MOST : (s + 1) * MOST][None] for s in range(sources) for e in range(2)], axis=0
    )
    grads = jnp.sum(jnp.where(here, sums, 0.0), axis=1) / jnp.where(named > 0.5, gates, 1.0)
    high, low = split_low(jnp.where(here, (gates * live)[:, None, :], 0.0))
    row = lax.broadcasted_iota(jnp.int32, (128, tokens), 0).astype(F32)
    for s in range(sources):
        y = y_ref[s]
        total = dot_tn(high[2 * s : 2 * s + 2].reshape(pair, tokens), y)
        total = total + dot_tn(low[2 * s : 2 * s + 2].reshape(pair, tokens), y)
        out_ref[s, :, 0:width] = total.astype(BF16)
        part = jnp.where(row == first, grads[2 * s : 2 * s + 1], 0.0)
        part = part + jnp.where(row == first + 1.0, grads[2 * s + 1 : 2 * s + 2], 0.0)
        out_ref[s, :, width:] = part.T.astype(BF16)


def whole_block(dims):
    return pl.BlockSpec(dims, lambda e: (0,) * len(dims))


def expert_block(dims):
    return pl.BlockSpec((1,) + dims, lambda e: (e,) + (0,) * len(dims))


def weight_block(dims):
    return pl.BlockSpec((dims[0], 3) + dims[2:], lambda e: (0, e, 0, 0))


def expert_call(kernel, specs, out_specs, outs, *args, vmem=VMEM, scratch=()):
    return pl.pallas_call(
        kernel,
        grid=(2,),
        in_specs=specs,
        out_specs=out_specs,
        out_shape=outs,
        scratch_shapes=scratch,
        compiler_params=pltpu.CompilerParams(
            vmem_limit_bytes=vmem * MIB, dimension_semantics=("arbitrary",)
        ),
    )(*args)


def on_device(
    hidden_in,
    cotangent,
    lengths,
    routes,
    gates,
    norm_attn,
    w_query,
    w_key,
    w_value,
    w_output,
    norm_mlp,
    w_gate,
    w_up,
    w_down,
):
    _, tokens, width = hidden_in.shape
    hidden_units = w_gate.shape[3]
    ep = lax.axis_size("ep")
    fsdp = lax.axis_size("fsdp")
    slot = tokens * fsdp
    slots = ep * 2 * MOST
    pair = 2 * MOST
    me = lax.axis_index("fsdp")

    def exchange(value, axis):
        return lax.all_to_all(value, axis, 0, 0, tiled=True)

    def gather(value):
        return lax.all_gather(value, "fsdp", axis=0, tiled=True)

    cores = 2
    chips = fsdp // cores
    side = 4
    here = lax.axis_index("ep")
    place = jnp.stack([here % side, here // side, here]).astype(jnp.int32)
    me_arg = me.reshape(1).astype(jnp.int32)

    def along_fsdp(step, flip):
        return [
            (f, (f // cores + step) % chips * cores + (f % cores + flip) % cores) for f in range(fsdp)
        ]

    def along_ep(step_z, step_x):
        return [
            (e, (e // side + step_z) % (ep // side) * side + (e % side + step_x) % side) for e in range(ep)
        ]

    steps = (0, 1, 3, 2)
    pieces = [(step, flip) for flip in range(cores) for step in steps]

    def gather_slot(value):
        own = [value] + [lax.ppermute(value, "fsdp", along_fsdp(step, 0)) for step in steps[1:]]
        return own + [lax.ppermute(piece, "fsdp", along_fsdp(0, 1)) for piece in own]

    def layer_of(array, layer):
        dims = (1,) + array.shape[1:]
        return pl.BlockSpec(dims, lambda _: (layer,) + (0,) * (len(dims) - 1))

    hidden_0 = hidden_in[0]
    pieces_0 = gather_slot(hidden_0)
    group_0, output_0 = pl.pallas_call(
        group_kernel,
        grid=(1,),
        in_specs=[layer_of(w, 0) for w in (w_query, w_key, w_value, w_output)]
        + [pl.BlockSpec((2, tokens), lambda _: (0, 0))] * 2,
        out_specs=[
            pl.BlockSpec((fsdp, tokens + 16, 256), lambda _: (0, 0, 0)),
            pl.BlockSpec((tokens, width), lambda _: (0, 0)),
        ],
        out_shape=[shape((fsdp, tokens + 16, 256)), shape((tokens, width))],
        compiler_params=pltpu.CompilerParams(vmem_limit_bytes=VMEM * MIB),
    )(w_query, w_key, w_value, w_output, norm_attn, norm_mlp)
    attn_out = gather(output_0)
    expert_dims = (6,) + w_gate.shape[2:]
    blocks = fsdp + width // 256
    output_0, *rest = lax.optimization_barrier((output_0, w_query, w_key, w_value, w_output, w_gate, w_up, w_down))
    shard_1, *expert_shards = pl.pallas_call(
        shards_kernel,
        grid=(1,),
        in_specs=[layer_of(w, 1) for w in rest[:4]] + [pl.BlockSpec(w.shape, lambda _: (0,) * 4) for w in rest[4:]],
        out_specs=[pl.BlockSpec((blocks, tokens, 256), lambda _: (0, 0, 0))]
        + [pl.BlockSpec(expert_dims, lambda _: (0, 0, 0))] * 2,
        out_shape=[shape((blocks, tokens, 256)), shape(expert_dims), shape(expert_dims)],
        compiler_params=pltpu.CompilerParams(vmem_limit_bytes=VMEM * MIB),
    )(*rest)
    experts_0 = lax.all_gather(expert_shards[0], "fsdp", axis=0)
    attn_1 = lax.all_gather(shard_1, "fsdp", axis=0)
    experts_1 = lax.all_gather(expert_shards[1], "fsdp", axis=0)
    group_back, group_0 = group_0, exchange(group_0, "fsdp")
    out_w = (attn_out, attn_1)
    expert_w = (experts_0, experts_1)

    lane = np.arange(128)
    frequency = np.float32(THETA) ** (np.float32(-2.0) * (lane % 32).astype(np.float32) / np.float32(HD))
    angles = np.arange(slot, dtype=np.float32)[:, None] * frequency.astype(np.float32)[None, :]
    cos_all = jnp.asarray(np.cos(angles).astype(np.float32))
    sin_all = jnp.asarray((np.sin(angles) * np.where(lane % HD < HD // 2, -1.0, 1.0)[None, :]).astype(np.float32))
    live = (me * tokens + jnp.arange(tokens, dtype=jnp.int32) < lengths[0]).astype(F32)
    live_col = live[:, None]
    live_row = jnp.broadcast_to(live[None, :], (8, tokens))
    routes_t = jnp.swapaxes(routes[:, 0], 1, 2)
    gates_t = jnp.swapaxes(gates[:, 0], 1, 2)

    by_row, by_token = shape((slots, tokens)), shape((tokens, slots))
    routing = call(
        routing_kernel, [by_row, by_token, by_row, by_row, by_token, by_token] * 2, routes_t, gates_t, live_row
    )
    pick, spread, high_t, low_t, high, low = zip(routing[:6], routing[6:])
    send_shape = shape((ep, pair, width))

    dh_2, send_cotangent = call(
        cotangent_kernel,
        [shape((tokens, width), F32), send_shape],
        cotangent[0],
        live_col,
        high_t[1],
        low_t[1],
    )

    in_smem = pl.BlockSpec(memory_space=pltpu.SMEM)
    in_vmem = pl.BlockSpec(memory_space=pltpu.VMEM)
    in_hbm = pl.BlockSpec(memory_space=pltpu.HBM)

    def held(dims):
        return [pltpu.VMEM(dims, BF16), pltpu.SemaphoreType.DMA(())]

    output_dims = ((width, width), (fsdp, blocks - fsdp, tokens, 256))

    rows_out = shape((2, ep * MOST, width))
    units_out = shape((2, ep * MOST, hidden_units))
    rows_spec, units_spec = expert_block((ep * MOST, width)), expert_block((ep * MOST, hidden_units))
    pair_spec = whole_block((ep, pair, width))
    held_rows = [pltpu.VMEM((ep, MOST, width), F32)]

    def run_experts(layer, received):
        return expert_call(
            expert_kernel,
            [pair_spec, weight_block(expert_w[layer].shape)],
            [pair_spec, rows_spec, units_spec, units_spec, units_spec],
            [send_shape, rows_out, units_out, units_out, units_out],
            received,
            expert_w[layer],
            scratch=held_rows,
        )

    def experts_back(layer, dy, kept, beside):
        _, x, gate, up, act = kept
        dx, dy_rows, dgate, dup, sums = expert_call(
            expert_back_kernel,
            [pair_spec, weight_block(expert_w[layer].shape), units_spec, units_spec, units_spec],
            [pair_spec, rows_spec, units_spec, units_spec, expert_block((ep * MOST, 128))],
            [send_shape, rows_out, units_out, units_out, shape((2, ep * MOST, 128), F32)],
            dy,
            expert_w[layer],
            gate,
            up,
            act,
            scratch=held_rows,
        )
        back = exchange(dx, "ep").reshape(slots, width)
        (grads,) = expert_call(
            expert_grads_kernel,
            [rows_spec, rows_spec, units_spec, units_spec, units_spec],
            [weight_block(expert_w[layer].shape)],
            [shape(grads_dims)],
            x,
            dy_rows,
            act,
            dgate,
            dup,
        )
        return lax.optimization_barrier((back, grads, beside(sums)))

    def gather_ep(value):
        row = jnp.concatenate([value] + [lax.ppermute(value, "ep", along_ep(0, k)) for k in (1, 2, 3)], axis=0)
        return jnp.concatenate([row] + [lax.ppermute(row, "ep", along_ep(k, 0)) for k in (1, 2, 3)], axis=0)

    meta = gather_ep(jnp.concatenate([routes_t[1].astype(F32), gates_t[1], live_row], axis=0)[None])

    def return_sums(y, sums, meta):
        return call(
            return_kernel,
            shape((ep, tokens, width + 128)),
            place,
            y,
            sums,
            meta,
            in_specs=[in_smem] + [in_vmem] * 3,
        )

    grads_dims = (fsdp, 8, tokens, hidden_units)

    def scatter_grads(layer, mixed, dattn, grads):
        grads = pl.pallas_call(
            output_grads_kernel,
            grid=(1,),
            in_specs=[
                pl.BlockSpec((tokens, width), lambda e: (0, 0)),
                pl.BlockSpec((tokens, width), lambda e: (0, 0)),
                pl.BlockSpec(memory_space=pl.ANY),
            ],
            out_specs=pl.BlockSpec((fsdp, 2, tokens, hidden_units), lambda e: (0, 3, 0, 0)),
            out_shape=shape(grads_dims),
            input_output_aliases={2: 0},
            compiler_params=pltpu.CompilerParams(vmem_limit_bytes=VMEM * MIB),
        )(mixed, dattn, grads)
        shard = lax.psum_scatter(grads, "fsdp", scatter_dimension=0, tiled=False)
        part = call(
            part_kernel,
            shape((tokens, 2 * hidden_units + 128)),
            shard,
            w_gate[layer],
            w_up[layer],
            norm_mlp[layer].astype(F32)[:, None],
        )
        return shard, part

    def attention_back(layer, back, after, dh, qkv, total, normed_all, first=None):
        w = out_w[layer]
        dafter, dattn, dmixed = call(
            functools.partial(after_back_kernel, groups=fsdp, gain_row=2 * layer + 1),
            [shape((tokens, width), F32), shape((tokens, width)), shape((fsdp, tokens, 128))],
            back,
            spread[layer],
            after,
            gains_all,
            dh,
            w,
            in_specs=[in_vmem] * 5 + [in_hbm],
            scratch=held(output_dims[layer]),
        )
        dmixed = exchange(dmixed, "fsdp").reshape(slot, 128)
        grads = call(
            functools.partial(attend_back_kernel, rows=256),
            shape((slot, 512)),
            lengths,
            qkv,
            total,
            dmixed,
            normed_all,
            cos_all,
            sin_all,
            in_specs=[in_smem] + [in_vmem] * 6,
            scratch=[pltpu.VMEM((slot, 128), F32)] * 2,
        )
        if first is not None:
            grads, first[0] = lax.optimization_barrier((grads, first[0]))
        return dafter, dattn, exchange(grads.reshape(fsdp, tokens, 512), "fsdp")

    row_size, all_size = tokens // side, 3 * width + 128

    def sum_ep(grads, part, beside=((), (), ())):
        chunks = call(
            chunks_kernel,
            [shape((row_size, all_size))] * side,
            place,
            grads,
            part,
            in_specs=[in_smem] + [in_vmem] * 2,
            scratch=[pltpu.VMEM((tokens, all_size), BF16)],
        )
        arrived = [chunks[0]] + [lax.ppermute(chunks[k], "ep", along_ep(0, k)) for k in steps[1:]]
        chunks = call(
            functools.partial(sum_split_kernel, count=side),
            [shape((row_size // side, all_size))] * side,
            place,
            *arrived,
            in_specs=[in_smem] + [in_vmem] * side,
            scratch=[pltpu.VMEM((row_size, all_size), F32)],
        )
        arrived = [chunks[0]] + [lax.ppermute(chunks[k], "ep", along_ep(k, 0)) for k in steps[1:]]
        arrived[0], first = lax.optimization_barrier((arrived[0], beside[0]))
        piece = call(sum_kernel, shape((row_size // side, all_size)), *arrived)
        arrived = [piece] + [lax.ppermute(piece, "ep", along_ep(k, 0)) for k in (1, 2, 3)]
        arrived[0], second = lax.optimization_barrier((arrived[0], beside[1]))
        piece = call(
            functools.partial(join_kernel, count=side),
            shape((row_size, all_size)),
            place,
            *arrived,
            in_specs=[in_smem] + [in_vmem] * side,
            scratch=[pltpu.VMEM((row_size, all_size), F32)],
        )
        arrived = [piece] + [lax.ppermute(piece, "ep", along_ep(0, k)) for k in (1, 2, 3)]
        arrived[0], third = lax.optimization_barrier((arrived[0], beside[2]))
        return arrived, (*first, *second, *third)

    kept_out = [shape((slot, width)), shape((slot, 256))]

    gains_all, normed_0, qkv_0, mixed, total_0 = call(
        functools.partial(first_kernel, pieces=pieces, cores=cores, rows=256),
        [shape((8, width), F32)] + kept_out + [shape((slot, 128)), shape((slot, 128), F32)],
        me_arg,
        lengths,
        *pieces_0,
        group_0,
        cos_all,
        sin_all,
        in_specs=[in_smem] * 2 + [in_vmem] * (len(pieces) + 3),
    )
    mixed_back, meta = lax.optimization_barrier((exchange(mixed.reshape(fsdp, tokens, 128), "fsdp"), meta))
    mixed_0, after_0, send = call(
        after_first_kernel,
        [shape((tokens, width)), shape((tokens, width), F32), send_shape],
        mixed_back,
        attn_out,
        hidden_0,
        gains_all,
        pick[0],
        in_specs=[in_vmem, in_hbm] + [in_vmem] * 3,
        scratch=held(output_dims[0]),
    )
    kept_0 = run_experts(0, exchange(send, "ep"))
    y_0 = exchange(kept_0[0], "ep").reshape(slots, width)
    y_0, send_cotangent = lax.optimization_barrier((y_0, send_cotangent))
    dy_1 = exchange(send_cotangent, "ep")
    hidden_1, normed = call(
        middle_kernel,
        [shape((tokens, width), F32), shape((tokens, width))],
        after_0,
        y_0,
        high[0],
        low[0],
        gains_all,
    )
    normed_1, qkv_1, total_1, *mixed = call(
        functools.partial(second_kernel, pieces=pieces, cores=cores, rows=256),
        kept_out + [shape((slot, 128), F32)] + [shape((cores, tokens, 128))] * chips,
        me_arg,
        lengths,
        *gather_slot(normed),
        lax.dynamic_index_in_dim(attn_1, me, 1, False),
        cos_all,
        sin_all,
        in_specs=[in_smem] * 2 + [in_vmem] * (len(pieces) + 3),
    )
    moved = [mixed[0]] + [lax.ppermute(mixed[step], "fsdp", along_fsdp(step, 0)) for step in steps[1:]]
    mates = lax.ppermute(jnp.concatenate([m[1:2] for m in moved], axis=0), "fsdp", along_fsdp(0, 1))
    mixed_1, after_1, send = call(
        functools.partial(after_second_kernel, steps=steps, cores=cores, groups=fsdp),
        [shape((tokens, width)), shape((tokens, width), F32), send_shape],
        me_arg,
        *moved,
        mates,
        attn_1,
        hidden_1,
        gains_all,
        pick[1],
        in_specs=[in_smem] + [in_vmem] * (chips + 1) + [in_hbm] + [in_vmem] * 3,
        scratch=held(output_dims[1]),
    )
    send, dy_1, group_back = lax.optimization_barrier((send, dy_1, group_back))
    attn_0 = lax.all_gather(group_back, "fsdp", axis=0)
    kept_1 = run_experts(1, exchange(send, "ep"))

    back, grads, returned = experts_back(1, dy_1, kept_1, lambda sums: return_sums(kept_1[0], sums, meta))
    returned = lax.psum_scatter(returned, "ep", scatter_dimension=0, tiled=False)
    back, attn_0 = lax.optimization_barrier((back, attn_0))
    dafter, dattn, grads_1 = attention_back(1, back, after_1, dh_2, qkv_1, total_1, normed_1)
    shard_1, part_1 = scatter_grads(1, mixed_1, dattn, grads)
    dh_1, send = call(
        middle_back_kernel,
        [shape((tokens, width), F32), send_shape],
        grads_1,
        attn_1,
        hidden_1,
        gains_all,
        dafter,
        high_t[0],
        low_t[0],
        in_specs=[in_vmem, in_hbm] + [in_vmem] * 5,
        scratch=held((fsdp, fsdp, tokens, 256)),
    )
    dy_0 = exchange(send, "ep")
    back, grads, _ = experts_back(0, dy_0, kept_0, lambda sums: ())
    back, part_1, returned = lax.optimization_barrier((back, part_1, returned))
    summed_1, _ = sum_ep(grads_1, part_1)
    dafter, dattn, grads_0 = attention_back(0, back, after_0, dh_1, qkv_0, total_0, normed_0, summed_1)
    shard_0, part_0 = scatter_grads(0, mixed_0, dattn, grads)

    dh_0 = call(
        last_back_kernel,
        shape((tokens, width), F32),
        grads_0,
        attn_0,
        hidden_0,
        gains_all,
        dafter,
        in_specs=[in_vmem, in_hbm] + [in_vmem] * 3,
        scratch=held((fsdp, fsdp, tokens + 16, 256)),
    )
    expert_grads = call(expert_out_kernel, [shape(w_gate.shape, F32)] * 3, shard_0, shard_1)

    hidden_out, gate_grad_1 = call(
        final_kernel,
        [shape((tokens, width)), shape((8, tokens), F32)],
        after_1,
        returned,
        live_row,
        routes_t[1],
    )
    gate_grad_0 = call(
        gates_kernel, shape((8, tokens), F32), y_0, dh_1, live_col, pick[0], routes_t[0]
    )
    summed_0, beside = sum_ep(
        grads_0, part_0, ((dh_0, gate_grad_0), (hidden_out, gate_grad_1), tuple(expert_grads))
    )
    dh_0, gate_grad_0, hidden_out, gate_grad_1, *expert_grads = beside
    half = width // 2
    query_grad, key_grad, value_grad, output_grad, attn_gain_grad, mlp_gain_grad = call(
        functools.partial(attention_out_kernel, count=side),
        [shape((2, tokens, width), F32)]
        + [shape((2, tokens, half), F32)] * 2
        + [shape((2, tokens, width), F32)]
        + [shape((2, tokens), F32)] * 2,
        place,
        *summed_0,
        *summed_1,
        w_query,
        w_key,
        w_value,
        norm_attn.astype(F32).T,
        in_specs=[in_smem] + [in_vmem] * (2 * side + 4),
        scratch=[pltpu.VMEM((tokens, all_size), BF16)] * 2,
    )
    gates_grad = jnp.swapaxes(jnp.stack([gate_grad_0, gate_grad_1]), 1, 2)[:, None]

    return (
        hidden_out[None],
        dh_0[None],
        gates_grad,
        attn_gain_grad,
        query_grad,
        key_grad,
        value_grad,
        output_grad,
        mlp_gain_grad,
        *expert_grads,
    )


def solution(mesh):
    row = P(None, "fsdp", None)
    expert = P(None, "ep", "fsdp", None)
    hidden = P("ep", "fsdp", None)
    gain = P(None, "fsdp")
    return jax.shard_map(
        on_device,
        mesh=mesh,
        in_specs=(hidden, hidden, P("ep"), expert, expert, gain, row, row, row, row, gain, expert, expert, expert),
        out_specs=(hidden, hidden, expert, gain, row, row, row, row, gain, expert, expert, expert),
        check_vma=False,
    )
```

```python
import functools

import jax
import jax.numpy as jnp
import numpy as np
from jax import lax
from jax.experimental import pallas as pl
from jax.experimental.pallas import tpu as pltpu
from jax.sharding import PartitionSpec as P

HD = 64
EPS = 1e-06
THETA = 10000.0
NEG_FILL = -1e30
MOST = 40
MIB = 1024 * 1024
VMEM = 60
F32 = jnp.float32
BF16 = jnp.bfloat16


def dot(left, right):
    return lax.dot_general(left, right, (((1,), (0,)), ((), ())), preferred_element_type=F32)


def dot_nt(left, right):
    return lax.dot_general(left, right, (((1,), (1,)), ((), ())), preferred_element_type=F32)


def dot_tn(left, right):
    return lax.dot_general(left, right, (((0,), (0,)), ((), ())), preferred_element_type=F32)


def split_low(value):
    high = value.astype(BF16)
    return high, (value - high.astype(F32)).astype(BF16)


def rms_parts(hidden):
    scale = lax.rsqrt(jnp.mean(hidden * hidden, axis=-1, keepdims=True) + EPS)
    return hidden * scale, scale


def rms_back(hidden, gain, grad):
    unit, scale = rms_parts(hidden)
    scaled = grad * gain
    return scale * (scaled - unit * jnp.mean(scaled * unit, axis=-1, keepdims=True))


def swap_halves(value):
    lane = lax.broadcasted_iota(jnp.int32, value.shape, 1) % HD
    return jnp.where(lane < HD // 2, pltpu.roll(value, 128 - HD // 2, 1), pltpu.roll(value, HD // 2, 1))


def low_lanes(shape):
    return lax.broadcasted_iota(jnp.int32, shape, 1) < HD


def call(kernel, outs, *args, vmem=VMEM, scratch=(), **extra):
    return pl.pallas_call(
        kernel,
        out_shape=outs,
        scratch_shapes=scratch,
        compiler_params=pltpu.CompilerParams(vmem_limit_bytes=vmem * MIB),
        **extra,
    )(*args)


def shape(dims, dtype=BF16):
    return jax.ShapeDtypeStruct(dims, dtype)


def routing_kernel(routes_ref, gates_ref, live_ref, *out_refs):
    experts, tokens = out_refs[0].shape[0] // MOST, routes_ref.shape[2]
    earlier = lax.broadcasted_iota(jnp.int32, (tokens, tokens), 0) < lax.broadcasted_iota(
        jnp.int32, (tokens, tokens), 1
    )
    earlier = earlier.astype(F32).astype(BF16)
    expert_id = lax.broadcasted_iota(jnp.int32, (experts, tokens), 0)
    place_id = lax.broadcasted_iota(jnp.int32, (experts, MOST, tokens), 1).astype(F32)
    for layer in range(routes_ref.shape[0]):
        named = jnp.zeros((experts, tokens), F32)
        weight = jnp.zeros((experts, tokens), F32)
        for k in range(routes_ref.shape[1]):
            same = routes_ref[layer, k : k + 1, :] == expert_id
            named = named + jnp.where(same, 1.0, 0.0)
            weight = weight + jnp.where(same, gates_ref[layer, k : k + 1, :], 0.0)
        weight = weight * live_ref[0:1, :]
        rank = dot(named.astype(BF16), earlier)
        rank = jnp.where(named > 0.5, rank, -1.0)
        here = rank[:, None, :] == place_id
        pick = jnp.where(here, 1.0, 0.0).reshape(experts * MOST, tokens)
        weights = jnp.where(here, weight[:, None, :], 0.0).reshape(experts * MOST, tokens)
        high, low = split_low(weights)
        outs = out_refs[6 * layer : 6 * layer + 6]
        outs[0][...] = pick.astype(BF16)
        outs[1][...] = pick.T.astype(BF16)
        outs[2][...] = high
        outs[3][...] = low
        outs[4][...] = high.astype(F32).T.astype(BF16)
        outs[5][...] = low.astype(F32).T.astype(BF16)


def put_groups(wq_ref, wk_ref, wv_ref, out_ref):
    rows = wq_ref.shape[1]
    low_half = low_lanes((rows, 128))
    groups = wq_ref.shape[2] // 128
    for g in range(groups):
        out_ref[g, 0:rows, 0:128] = wq_ref[0, :, g * 128 : (g + 1) * 128]
    for j in range(groups // 2):
        key = wk_ref[0, :, j * 128 : (j + 1) * 128].astype(F32)
        value = wv_ref[0, :, j * 128 : (j + 1) * 128].astype(F32)
        out_ref[2 * j, 0:rows, 128:256] = jnp.where(low_half, key, pltpu.roll(value, HD, 1)).astype(BF16)
        out_ref[2 * j + 1, 0:rows, 128:256] = jnp.where(low_half, pltpu.roll(key, HD, 1), value).astype(BF16)


def group_kernel(wq_ref, wk_ref, wv_ref, wo_ref, attn_ref, mlp_ref, out_ref, wo_out_ref):
    gains = jnp.concatenate([attn_ref[...].astype(F32), mlp_ref[...].astype(F32)], axis=1)
    gains = jnp.concatenate([gains, jnp.zeros((14, 256), F32)], axis=0).astype(BF16)
    put_groups(wq_ref, wk_ref, wv_ref, out_ref)
    wo_out_ref[...] = wo_ref[0]
    for g in range(out_ref.shape[0]):
        out_ref[g, wq_ref.shape[1] :, :] = gains


def shards_kernel(wq_ref, wk_ref, wv_ref, wo_ref, gate_ref, up_ref, down_ref, attn_ref, *expert_refs):
    put_groups(wq_ref, wk_ref, wv_ref, attn_ref)
    groups = wq_ref.shape[2] // 128
    for j in range(attn_ref.shape[0] - groups):
        attn_ref[groups + j] = wo_ref[0, :, j * 256 : (j + 1) * 256]
    for layer, out_ref in enumerate(expert_refs):
        for e in range(2):
            out_ref[3 * e] = gate_ref[layer, e]
            out_ref[3 * e + 1] = up_ref[layer, e]
            out_ref[3 * e + 2] = down_ref[layer, e]


def fetch(source, held_ref, sem):
    copy = pltpu.make_async_copy(source, held_ref, sem)
    copy.start()
    return copy


def blocks_of(w_ref, groups):
    return w_ref if len(w_ref.shape) == 2 else w_ref.at[:, pl.ds(groups, w_ref.shape[1] - groups)]


def times_output(mixed, held_ref):
    if len(held_ref.shape) == 2:
        return dot(mixed, held_ref[...])
    return jnp.concatenate(
        [dot(mixed, held_ref[:, j].reshape(mixed.shape[1], 256)) for j in range(held_ref.shape[1])], axis=1
    )


def times_output_t(grad, held_ref):
    if len(held_ref.shape) == 2:
        return dot_nt(grad, held_ref[...])
    return sum(
        dot_nt(grad[:, j * 256 : (j + 1) * 256], held_ref[:, j].reshape(grad.shape[1], 256))
        for j in range(held_ref.shape[1])
    )


def relative(me, cores, count, step, flip):
    return lax.rem(me // cores - step + count, count) * cores + lax.rem(me % cores + flip, cores)


def turned(chunk, cos, sin):
    return chunk * cos + swap_halves(chunk) * sin


def attend(length, qkv_ref, rows, put):
    slot = qkv_ref.shape[0]
    keyval = qkv_ref[:, 128:256].astype(F32)
    low_half = low_lanes(keyval.shape)
    keyval_turned = pltpu.roll(keyval, HD, 1)
    zero = jnp.zeros_like(keyval)
    key_wide = (jnp.where(low_half, keyval, zero).astype(BF16), jnp.where(low_half, zero, keyval_turned).astype(BF16))
    value_wide = (jnp.where(low_half, keyval_turned, zero).astype(BF16), jnp.where(low_half, zero, keyval).astype(BF16))
    for block in range(slot // rows):
        span = (block + 1) * rows
        query = qkv_ref[pl.ds(block * rows, rows), 0:128]
        row_id = block * rows + lax.broadcasted_iota(jnp.int32, (rows, span), 0)
        col_id = lax.broadcasted_iota(jnp.int32, (rows, span), 1)
        allowed = (col_id <= row_id) & (col_id < length)
        mixed = jnp.zeros((rows, 128), F32)
        totals = []
        for head in range(2):
            scores = dot_nt(query, key_wide[head][:span]) * (HD**-0.5)
            scores = jnp.where(allowed, scores, NEG_FILL)
            top = jnp.max(scores, axis=-1, keepdims=True)
            expo = jnp.exp(scores - top)
            total = jnp.sum(expo, axis=-1, keepdims=True)
            probs = (expo * (1.0 / total)).astype(BF16)
            mixed = mixed + dot(probs, value_wide[head][:span])
            totals.append(top + jnp.log(total))
        put(block, mixed.astype(BF16), totals)


def put_moved(me, cores, moved_refs, owner, piece):
    chips = len(moved_refs)
    step = lax.rem(owner // cores - me // cores + chips, chips)
    flip = lax.rem(owner % cores + me % cores, cores)
    for k in range(chips):

        @pl.when(step == k)
        def _():
            moved_refs[k][flip] = piece


def place_moved(me, cores, steps, moved, mate_ref, out_ref, size, dim):
    for k, step in enumerate(steps):
        for flip, piece in ((0, moved[k][0]), (1, mate_ref[k])):
            at = pl.ds(pl.multiple_of(relative(me, cores, len(steps), step, flip) * size, size), size)
            if dim == 0:
                out_ref[at, :] = piece
            else:
                out_ref[:, at] = piece


def first_kernel(
    me_ref, length_ref, *refs, pieces, cores, rows
):
    moved = refs[: len(pieces)]
    w_ref, cos_ref, sin_ref, gains_ref, normed_ref, qkv_ref, mixed_ref, total_ref = refs[len(pieces) :]
    me = me_ref[0]
    shards, _, _ = w_ref.shape
    tokens = moved[0].shape[0]
    for row in range(2):
        for half in range(2):
            gains_ref[2 * row + half : 2 * row + half + 1, :] = jnp.concatenate(
                [w_ref[s, tokens + row : tokens + row + 1, half * 128 : (half + 1) * 128] for s in range(shards)], axis=1
            ).astype(F32)
    gain = gains_ref[0:1, :]
    for (step, flip), piece in zip(pieces, moved):
        at = relative(me, cores, shards // cores, step, flip) * tokens
        unit, _ = rms_parts(piece[...].astype(F32))
        normed_ref[pl.ds(pl.multiple_of(at, tokens), tokens), :] = (unit * gain).astype(BF16)
    weights = w_ref[:, :tokens, :].reshape(shards * tokens, 256)
    raw = dot(normed_ref[...], weights)
    cos, sin = cos_ref[...], sin_ref[...]
    qkv_ref[:, 0:128] = turned(raw[:, 0:128], cos, sin).astype(BF16)
    keyval = raw[:, 128:256]
    qkv_ref[:, 128:256] = jnp.where(low_lanes(keyval.shape), turned(keyval, cos, sin), keyval).astype(BF16)

    def put(block, mixed, totals):
        at = pl.ds(block * rows, rows)
        mixed_ref[at, :] = mixed
        for head in range(2):
            total_ref[at, head * HD : (head + 1) * HD] = jnp.broadcast_to(totals[head], (rows, HD))

    attend(length_ref[0], qkv_ref, rows, put)


def second_kernel(me_ref, length_ref, *refs, pieces, cores, rows):
    moved = refs[: len(pieces)]
    w_ref, cos_ref, sin_ref, normed_ref, qkv_ref, total_ref, mixed_ref = refs[len(pieces) : len(pieces) + 7]
    moved_refs = refs[len(pieces) + 7 :]
    me = me_ref[0]
    tokens = moved[0].shape[0]
    devices = normed_ref.shape[0] // tokens
    chips = devices // cores
    for (step, flip), piece in zip(pieces, moved):
        at = relative(me, cores, chips, step, flip) * tokens
        normed_ref[pl.ds(pl.multiple_of(at, tokens), tokens), :] = piece[...]
    normed = normed_ref[...]
    cos, sin = cos_ref[...], sin_ref[...]
    raw = dot(normed, w_ref[...].reshape(normed.shape[1], 256))
    qkv_ref[:, 0:128] = turned(raw[:, 0:128], cos, sin).astype(BF16)
    keyval = raw[:, 128:256]
    qkv_ref[:, 128:256] = jnp.where(low_lanes(keyval.shape), turned(keyval, cos, sin), keyval).astype(BF16)

    def put(block, mixed, totals):
        at = pl.ds(block * rows, rows)
        for head in range(2):
            total_ref[at, head * HD : (head + 1) * HD] = jnp.broadcast_to(totals[head], (rows, HD))
        mixed_ref[at, :] = mixed
        for part in range(rows // tokens):
            put_moved(me, cores, moved_refs, block * (rows // tokens) + part, mixed[part * tokens : (part + 1) * tokens])

    attend(length_ref[0], qkv_ref, rows, put)


def middle_kernel(after_ref, back_ref, high_ref, low_ref, gains_ref, hidden_ref, normed_ref):
    back = back_ref[...]
    hidden = after_ref[...] + (dot(high_ref[...], back) + dot(low_ref[...], back))
    hidden_ref[...] = hidden
    unit, _ = rms_parts(hidden)
    normed_ref[...] = (unit * gains_ref[2:3, :]).astype(BF16)


def attend_back_kernel(
    me_ref, length_ref, qkv_ref, total_ref, normed_ref, cos_ref, sin_ref, *refs, rows, cores, steps
):
    slot = qkv_ref.shape[0]
    if steps:
        count = len(steps)
        moved, mate_ref = refs[:count], refs[count]
        moved_refs = refs[count + 1 : 2 * count + 1]
        grads_ref, dk_ref, dv_ref, grad_ref, out_ref = refs[2 * count + 1 :]
        place_moved(me_ref[0], cores, steps, moved, mate_ref, grad_ref, slot // count // cores, 0)
    else:
        grad_ref, out_ref, grads_ref, dk_ref, dv_ref = refs
    length = length_ref[0]
    keyval = qkv_ref[:, 128:256].astype(F32)
    low_half = low_lanes(keyval.shape)
    keyval_turned = pltpu.roll(keyval, HD, 1)
    zero = jnp.zeros_like(keyval)
    key_wide = (jnp.where(low_half, keyval, zero).astype(BF16), jnp.where(low_half, zero, keyval_turned).astype(BF16))
    value_wide = (jnp.where(low_half, keyval_turned, zero).astype(BF16), jnp.where(low_half, zero, keyval).astype(BF16))
    dk_ref[...] = zero
    dv_ref[...] = zero
    low_row = low_lanes((rows, 128))
    zero_row = jnp.zeros((rows, 128), BF16)
    for block in range(slot // rows):
        span = (block + 1) * rows
        at = pl.ds(block * rows, rows)
        query = qkv_ref[at, 0:128]
        grad = grad_ref[at, :]
        row_id = block * rows + lax.broadcasted_iota(jnp.int32, (rows, span), 0)
        col_id = lax.broadcasted_iota(jnp.int32, (rows, span), 1)
        allowed = (col_id <= row_id) & (col_id < length)
        dq = jnp.zeros((rows, 128), F32)
        for head in range(2):
            keep = low_row if head == 0 else jnp.logical_not(low_row)
            scores = dot_nt(query, key_wide[head][:span]) * (HD**-0.5)
            scores = jnp.where(allowed, scores, NEG_FILL)
            probs = jnp.exp(scores - total_ref[at, head * HD : head * HD + 1])
            dprobs = dot_nt(grad, value_wide[head][:span])
            mean = jnp.sum(dprobs * probs, axis=-1, keepdims=True)
            dscores = (probs * (dprobs - mean)).astype(BF16)
            dq = dq + dot(dscores, key_wide[head][:span])
            dk_ref[:span, :] += dot_tn(dscores, jnp.where(keep, query, zero_row))
            dv_ref[:span, :] += dot_tn(probs.astype(BF16), jnp.where(keep, grad, zero_row))
        dq = dq * (HD**-0.5)
        out_ref[at, 0:128] = (dq * cos_ref[at, :] - swap_halves(dq) * sin_ref[at, :]).astype(BF16)
    dk = dk_ref[...]
    dk = (dk + pltpu.roll(dk, HD, 1)) * (HD**-0.5)
    dk = dk * cos_ref[...] - swap_halves(dk) * sin_ref[...]
    dv = dv_ref[...]
    dv = dv + pltpu.roll(dv, HD, 1)
    out_ref[:, 128:256] = jnp.where(low_half, dk, dv).astype(BF16)
    grads = dot_tn(normed_ref[...], out_ref[...])
    devices = slot // 128
    size = grads.shape[0] // devices
    for owner in range(devices):
        at = slice(owner * size, (owner + 1) * size)
        if steps:
            put_moved(me_ref[0], cores, moved_refs, owner, out_ref[owner * 128 : (owner + 1) * 128, :])
        parts, few = grads_ref.shape[0], grads_ref.shape[2]
        grads_ref[:, owner] = grads[at].reshape(parts, few, grads.shape[1]).astype(BF16)


def after_step(mixed, copy, held_ref, hidden_ref, gain, pick_ref, after_ref, send_ref):
    copy.wait()
    after = hidden_ref[...].astype(F32) + times_output(mixed, held_ref)
    after_ref[...] = after
    unit, _ = rms_parts(after)
    send_ref[...] = dot(pick_ref[...], (unit * gain).astype(BF16)).astype(BF16).reshape(send_ref.shape)


def after_first_kernel(
    mixed_ref, w_ref, hidden_ref, gains_ref, pick_ref, after_ref, send_ref, held_ref, sem
):
    copy = fetch(w_ref, held_ref, sem)
    mixed = jnp.concatenate([mixed_ref[g] for g in range(mixed_ref.shape[0])], axis=1)
    after_step(mixed, copy, held_ref, hidden_ref, gains_ref[1:2, :], pick_ref, after_ref, send_ref)


def after_second_kernel(me_ref, *refs, steps, cores, groups):
    moved, mate_ref = refs[: len(steps)], refs[len(steps)]
    w_ref, hidden_ref, gains_ref, pick_ref, after_ref, send_ref, mixed_out_ref, held_ref, sem = refs[len(steps) + 1 :]
    copy = fetch(blocks_of(w_ref, groups), held_ref, sem)
    place_moved(me_ref[0], cores, steps, moved, mate_ref, mixed_out_ref, 128, 1)
    after_step(mixed_out_ref[...], copy, held_ref, hidden_ref, gains_ref[3:4, :], pick_ref, after_ref, send_ref)


def pack(high, low, grad, send_ref):
    grad_high, grad_low = split_low(grad)
    rows = dot(high, grad_high) + (dot(low, grad_high) + dot(high, grad_low))
    send_ref[...] = rows.astype(BF16).reshape(send_ref.shape)


def cotangent_kernel(grad_ref, live_ref, high_ref, low_ref, dh_ref, send_ref):
    grad = grad_ref[...].astype(F32) * live_ref[...]
    dh_ref[...] = grad
    pack(high_ref[...], low_ref[...], grad, send_ref)


def after_back_kernel(
    me_ref, back_ref, place_ref, after_ref, gains_ref, dh_ref, w_ref, dafter_ref, dattn_ref, *refs, groups, cores, gain_row
):
    *dmixed_refs, held_ref, sem = refs
    copy = fetch(blocks_of(w_ref, groups), held_ref, sem)
    dmoe = dot(place_ref[...], back_ref[...])
    dafter = dh_ref[...] + rms_back(after_ref[...], gains_ref[gain_row : gain_row + 1, :], dmoe)
    dafter_ref[...] = dafter
    dattn = dafter.astype(BF16)
    dattn_ref[...] = dattn
    copy.wait()
    dmixed = times_output_t(dattn, held_ref).astype(BF16)
    for g in range(groups):
        if len(dmixed_refs) == 1:
            dmixed_refs[0][g] = dmixed[:, g * 128 : (g + 1) * 128]
        else:
            put_moved(me_ref[0], cores, dmixed_refs, g, dmixed[:, g * 128 : (g + 1) * 128])


def project_back(grads, copy, held_ref, hidden, gain, dafter):
    rows, groups = grads.shape[0], held_ref.shape[1]
    copy.wait()
    dnormed = [
        dot_nt(grads, jnp.concatenate([held_ref[s, g, 0:rows] for g in range(groups)], axis=1))
        for s in range(held_ref.shape[0])
    ]
    return dafter + rms_back(hidden, gain, jnp.concatenate(dnormed, axis=1))


def middle_back_kernel(me_ref, *refs, steps, cores):
    moved, mate_ref = refs[: len(steps)], refs[len(steps)]
    w_ref, hidden_ref, gains_ref, dafter_ref, high_ref, low_ref, dh_ref, send_ref, back_ref, held_ref, sem = refs[len(steps) + 1 :]
    copy = fetch(w_ref.at[:, pl.ds(0, held_ref.shape[1])], held_ref, sem)
    place_moved(me_ref[0], cores, steps, moved, mate_ref, back_ref, 256, 1)
    dh = project_back(back_ref[...], copy, held_ref, hidden_ref[...], gains_ref[2:3, :], dafter_ref[...])
    dh_ref[...] = dh
    pack(high_ref[...], low_ref[...], dh, send_ref)


def last_back_kernel(back_ref, w_ref, hidden_ref, gains_ref, dafter_ref, dh_ref, held_ref, sem):
    copy = fetch(w_ref.at[:, pl.ds(0, held_ref.shape[1])], held_ref, sem)
    grads = jnp.concatenate([back_ref[g] for g in range(back_ref.shape[0])], axis=1)
    dh_ref[...] = project_back(
        grads, copy, held_ref, hidden_ref[...].astype(F32), gains_ref[0:1, :], dafter_ref[...]
    )


def chunks_kernel(place_ref, *refs, count):
    *chunk_refs, whole_ref = refs[-count - 1 :]
    first = 0
    for part in refs[: -count - 1]:
        whole_ref[:, first : first + part.shape[1]] = part[...]
        first += part.shape[1]
    size = whole_ref.shape[0] // count
    for k, chunk_ref in enumerate(chunk_refs):
        at = lax.rem(place_ref[0] + k, count) * size
        chunk_ref[...] = whole_ref[pl.ds(pl.multiple_of(at, size), size), :]


def output_grads_kernel(me_ref, *refs, pieces, cores):
    moved, (mixed_ref, out_ref, all_ref) = refs[: len(pieces)], refs[len(pieces) :]
    tokens = moved[0].shape[0]
    chips = all_ref.shape[0] // tokens // cores
    for (step, flip), piece in zip(pieces, moved):
        at = relative(me_ref[0], cores, chips, step, flip) * tokens
        all_ref[pl.ds(pl.multiple_of(at, tokens), tokens), :] = piece[...]
    out_ref[...] = dot_tn(mixed_ref[...], all_ref[...]).astype(BF16)


def sum_slots_kernel(in_ref, out_ref):
    out_ref[...] = sum((in_ref[e].astype(F32) for e in range(1, in_ref.shape[0])), in_ref[0].astype(F32)).astype(BF16)


def sum_split_kernel(place_ref, *refs, count):
    arrived, chunk_refs, held_ref = refs[:count], refs[count:-1], refs[-1]
    held_ref[...] = sum((r[...].astype(F32) for r in arrived[1:]), arrived[0][...].astype(F32))
    size = held_ref.shape[0] // count
    for k, chunk_ref in enumerate(chunk_refs):
        at = lax.rem(place_ref[1] + k, count) * size
        chunk_ref[...] = held_ref[pl.ds(pl.multiple_of(at, size), size), :].astype(BF16)


def sum_kernel(*refs):
    refs[-1][...] = sum((r[...].astype(F32) for r in refs[1:-1]), refs[0][...].astype(F32)).astype(BF16)


def join_kernel(place_ref, *refs, count):
    arrived, out_ref, held_ref = refs[:count], refs[count], refs[count + 1]
    size = arrived[0].shape[0]
    for k, piece in enumerate(arrived):
        at = lax.rem(place_ref[1] - k + count, count) * size
        held_ref[pl.ds(pl.multiple_of(at, size), size), :] = piece[...].astype(F32)
    out_ref[...] = held_ref[...].astype(BF16)


def attention_out_kernel(place_ref, *refs, count):
    arrived, moved = refs[:count], refs[count : 2 * count]
    (wq_ref, wk_ref, wv_ref, gain_ref, query_ref, key_ref, value_ref, out_ref, attn_ref, mlp_ref, inner_ref, held_ref) = refs[2 * count :]
    width = wq_ref.shape[2]
    groups = width // 128
    size = arrived[0].shape[0]
    few = moved[0].shape[2] // 2
    for k, piece in enumerate(arrived):
        at = lax.rem(place_ref[0] - k + count, count) * size
        held_ref[pl.ds(pl.multiple_of(at, size), size), :] = piece[...]
    for k, piece in enumerate(moved):
        for j in range(count):
            came = lax.rem(place_ref[1] - j + count, count) * count + lax.rem(place_ref[0] - k + count, count)
            at = pl.ds(pl.multiple_of(came * few, few), few)
            for g in range(groups):
                both = piece[j, g].astype(F32)
                for layer in range(2):
                    inner_ref[layer, at, g * 256 : (g + 1) * 256] = both[layer * few : (layer + 1) * few]
    low_half = low_lanes((size * count, 128))
    for layer in range(2):
        ref, first = inner_ref.at[layer], 0
        total = jnp.zeros(low_half.shape, F32)
        for g in range(groups):
            query = ref[:, first + g * 256 : first + g * 256 + 128].astype(F32)
            query_ref[layer, :, g * 128 : (g + 1) * 128] = query
            total = total + query * wq_ref[layer, :, g * 128 : (g + 1) * 128].astype(F32)
        for j in range(groups // 2):
            even = ref[:, first + 512 * j + 128 : first + 512 * j + 256].astype(F32)
            odd = ref[:, first + 512 * j + 384 : first + 512 * j + 512].astype(F32)
            key = jnp.where(low_half, even, pltpu.roll(odd, HD, 1))
            value = jnp.where(low_half, pltpu.roll(even, HD, 1), odd)
            at = slice(j * 128, (j + 1) * 128)
            key_ref[layer, :, at] = key
            value_ref[layer, :, at] = value
            total = total + key * wk_ref[layer, :, at].astype(F32) + value * wv_ref[layer, :, at].astype(F32)
        out_ref[layer] = held_ref[:, layer * width : (layer + 1) * width].astype(F32)
        gain = jnp.sum(total, axis=1, keepdims=True) / gain_ref[:, layer : layer + 1]
        attn_ref[layer : layer + 1, :] = jnp.broadcast_to(gain, low_half.shape).T[0:1, :]
        column = held_ref[:, 2 * width + layer * 128 : 2 * width + (layer + 1) * 128]
        mlp_ref[layer : layer + 1, :] = column.astype(F32).T[0:1, :]


def part_kernel(shard_ref, gate_ref, up_ref, gain_ref, part_ref):
    total = jnp.zeros(gate_ref.shape[1:], F32)
    for e in range(2):
        total = total + shard_ref[3 * e].astype(F32) * gate_ref[e].astype(F32)
        total = total + shard_ref[3 * e + 1].astype(F32) * up_ref[e].astype(F32)
    gain = jnp.sum(total, axis=1, keepdims=True) / gain_ref[...]
    lane = lax.broadcasted_iota(jnp.int32, part_ref.shape, 1)
    part_ref[...] = jnp.where(lane == 0, gain, 0.0).astype(BF16)


def expert_out_kernel(first_ref, second_ref, gate_ref, up_ref, down_ref):
    for layer, ref in enumerate((first_ref, second_ref)):
        for e in range(2):
            gate_ref[layer, e] = ref[3 * e].astype(F32)
            up_ref[layer, e] = ref[3 * e + 1].astype(F32)
            down_ref[layer, e] = ref[3 * e + 2].astype(F32)


def gate_grads(back, dh, pick_ref, routes_ref, out_ref):
    high, low = split_low(dh)
    slots, tokens = pick_ref.shape
    product = dot_nt(back, high) + dot_nt(back, low)
    product = product * pick_ref[...].astype(F32)
    each = jnp.sum(product.reshape(slots // MOST, MOST, tokens), axis=1)
    expert_id = lax.broadcasted_iota(jnp.int32, each.shape, 0)
    for k in range(routes_ref.shape[0]):
        out_ref[k : k + 1, :] = jnp.sum(
            jnp.where(routes_ref[k : k + 1, :] == expert_id, each, 0.0), axis=0, keepdims=True
        )


def gates_kernel(back_ref, dh_ref, live_ref, pick_ref, routes_ref, out_ref):
    gate_grads(back_ref[...], dh_ref[...] * live_ref[...], pick_ref, routes_ref, out_ref)


def final_kernel(after_ref, back_ref, high_ref, low_ref, dh_ref, pick_ref, routes_ref, hidden_ref, out_ref):
    back = back_ref[...]
    hidden = after_ref[...] + (dot(high_ref[...], back) + dot(low_ref[...], back))
    hidden_ref[...] = hidden.astype(BF16)
    gate_grads(back, dh_ref[...], pick_ref, routes_ref, out_ref)


def rows_of(ref, expert):
    both = ref[...].astype(F32)
    rows = both[:, expert * MOST : (expert + 1) * MOST, :]
    return rows.reshape(rows.shape[0] * MOST, rows.shape[2]).astype(BF16)


def weights_of(w_ref, which):
    part = w_ref[:, which]
    return part.reshape(part.shape[0] * part.shape[1], part.shape[2])


def put_rows(rows, expert, held_ref, out_ref):
    sources = out_ref.shape[0]
    rows = rows.reshape(sources, MOST, rows.shape[1])
    if expert == 0:
        held_ref[...] = rows
    else:
        out_ref[...] = jnp.concatenate([held_ref[...], rows], axis=1).astype(BF16)


def expert_kernel(x_ref, w_ref, y_ref, rows_ref, gate_ref, up_ref, act_ref, held_ref):
    def one(expert):
        rows = rows_of(x_ref, expert)
        rows_ref[0] = rows
        gate = dot(rows, weights_of(w_ref, 0))
        up = dot(rows, weights_of(w_ref, 1))
        gate_ref[0] = gate.astype(BF16)
        up_ref[0] = up.astype(BF16)
        act = (gate * (1.0 / (1.0 + jnp.exp(-gate))) * up).astype(BF16)
        act_ref[0] = act
        put_rows(dot_nt(act, weights_of(w_ref, 2)), expert, held_ref, y_ref)

    for expert in range(2):
        pl.when(pl.program_id(0) == expert)(functools.partial(one, expert))


def expert_back_kernel(dy_ref, w_ref, gate_ref, up_ref, dx_ref, rows_ref, dgate_ref, dup_ref, held_ref):
    def one(expert):
        rows = rows_of(dy_ref, expert)
        rows_ref[0] = rows
        dact = dot(rows, weights_of(w_ref, 2))
        gate = gate_ref[0].astype(F32)
        up = up_ref[0].astype(F32)
        sigma = 1.0 / (1.0 + jnp.exp(-gate))
        dgate = (dact * up * (sigma * (1.0 + gate * (1.0 - sigma)))).astype(BF16)
        dup = (dact * (gate * sigma)).astype(BF16)
        dgate_ref[0] = dgate
        dup_ref[0] = dup
        dx = dot_nt(dgate, weights_of(w_ref, 0)) + dot_nt(dup, weights_of(w_ref, 1))
        put_rows(dx, expert, held_ref, dx_ref)

    for expert in range(2):
        pl.when(pl.program_id(0) == expert)(functools.partial(one, expert))


def expert_grads_kernel(x_ref, dy_ref, act_ref, dgate_ref, dup_ref, out_ref):
    shards, _, rows, hidden = out_ref.shape
    x = x_ref[0]
    out_ref[:, 0] = dot_tn(x, dgate_ref[0]).astype(BF16).reshape(shards, rows, hidden)
    out_ref[:, 1] = dot_tn(x, dup_ref[0]).astype(BF16).reshape(shards, rows, hidden)
    out_ref[:, 2] = dot_tn(dy_ref[0], act_ref[0]).astype(BF16).reshape(shards, rows, hidden)


def whole_block(dims):
    return pl.BlockSpec(dims, lambda e: (0,) * len(dims))


def expert_block(dims):
    return pl.BlockSpec((1,) + dims, lambda e: (e,) + (0,) * len(dims))


def weight_block(dims):
    return pl.BlockSpec((dims[0], 3) + dims[2:], lambda e: (0, e, 0, 0))


def expert_call(kernel, specs, out_specs, outs, *args, vmem=VMEM, scratch=()):
    return pl.pallas_call(
        kernel,
        grid=(2,),
        in_specs=specs,
        out_specs=out_specs,
        out_shape=outs,
        scratch_shapes=scratch,
        compiler_params=pltpu.CompilerParams(
            vmem_limit_bytes=vmem * MIB, dimension_semantics=("arbitrary",)
        ),
    )(*args)


def on_device(
    hidden_in,
    cotangent,
    lengths,
    routes,
    gates,
    norm_attn,
    w_query,
    w_key,
    w_value,
    w_output,
    norm_mlp,
    w_gate,
    w_up,
    w_down,
):
    _, tokens, width = hidden_in.shape
    hidden_units = w_gate.shape[3]
    ep = lax.axis_size("ep")
    fsdp = lax.axis_size("fsdp")
    slot = tokens * fsdp
    slots = ep * 2 * MOST
    pair = 2 * MOST
    me = lax.axis_index("fsdp")

    def exchange(value, axis):
        return lax.all_to_all(value, axis, 0, 0, tiled=True)

    def gather(value):
        return lax.all_gather(value, "fsdp", axis=0, tiled=True)

    cores = 2
    chips = fsdp // cores
    side = 4
    here = lax.axis_index("ep")
    place = jnp.stack([here % side, here // side, here, me]).astype(jnp.int32)
    me_arg = me.reshape(1).astype(jnp.int32)

    def along_fsdp(step, flip):
        return [
            (f, (f // cores + step) % chips * cores + (f % cores + flip) % cores) for f in range(fsdp)
        ]

    def along_ep(step_z, step_x):
        return [
            (e, (e // side + step_z) % (ep // side) * side + (e % side + step_x) % side) for e in range(ep)
        ]

    steps = (0, 1, 3, 2)
    pieces = [(step, flip) for flip in range(cores) for step in steps]

    def gather_slot(value):
        own = [value] + [lax.ppermute(value, "fsdp", along_fsdp(step, 0)) for step in steps[1:]]
        return own + [lax.ppermute(piece, "fsdp", along_fsdp(0, 1)) for piece in own]

    def layer_of(array, layer):
        dims = (1,) + array.shape[1:]
        return pl.BlockSpec(dims, lambda _: (layer,) + (0,) * (len(dims) - 1))

    hidden_0 = hidden_in[0]
    pieces_0 = gather_slot(hidden_0)
    mine = [w_query, w_key, w_value, w_output, w_gate, w_up, w_down]
    group_0, output_0 = pl.pallas_call(
        group_kernel,
        grid=(1,),
        in_specs=[layer_of(w, 0) for w in (w_query, w_key, w_value, w_output)]
        + [pl.BlockSpec((2, tokens), lambda _: (0, 0))] * 2,
        out_specs=[
            pl.BlockSpec((fsdp, tokens + 16, 256), lambda _: (0, 0, 0)),
            pl.BlockSpec((tokens, width), lambda _: (0, 0)),
        ],
        out_shape=[shape((fsdp, tokens + 16, 256)), shape((tokens, width))],
        compiler_params=pltpu.CompilerParams(vmem_limit_bytes=VMEM * MIB),
    )(*mine[:4], norm_attn, norm_mlp)
    attn_out = gather(output_0)
    expert_dims = (6,) + w_gate.shape[2:]
    blocks = fsdp + width // 256
    blocks = fsdp + width // 256
    group_back, group_0 = group_0, exchange(group_0, "fsdp")
    shard_1, *expert_shards = pl.pallas_call(
        shards_kernel,
        grid=(1,),
        in_specs=[layer_of(w, 1) for w in mine[:4]] + [pl.BlockSpec(w.shape, lambda _: (0,) * 4) for w in mine[4:]],
        out_specs=[pl.BlockSpec((blocks, tokens, 256), lambda _: (0, 0, 0))]
        + [pl.BlockSpec(expert_dims, lambda _: (0, 0, 0))] * 2,
        out_shape=[shape((blocks, tokens, 256)), shape(expert_dims), shape(expert_dims)],
        compiler_params=pltpu.CompilerParams(vmem_limit_bytes=VMEM * MIB),
    )(*mine)
    experts_0 = lax.all_gather(expert_shards[0], "fsdp", axis=0)
    attn_1 = lax.all_gather(shard_1, "fsdp", axis=0)
    experts_1 = lax.all_gather(expert_shards[1], "fsdp", axis=0)
    out_w = (attn_out, attn_1)
    expert_w = (experts_0, experts_1)


    lane = np.arange(128)
    frequency = np.float32(THETA) ** (np.float32(-2.0) * (lane % 32).astype(np.float32) / np.float32(HD))
    angles = np.arange(slot, dtype=np.float32)[:, None] * frequency.astype(np.float32)[None, :]
    cos_all = jnp.asarray(np.cos(angles).astype(np.float32))
    sin_all = jnp.asarray((np.sin(angles) * np.where(lane % HD < HD // 2, -1.0, 1.0)[None, :]).astype(np.float32))
    live = (me * tokens + jnp.arange(tokens, dtype=jnp.int32) < lengths[0]).astype(F32)
    live_col = live[:, None]
    live_row = jnp.broadcast_to(live[None, :], (8, tokens))
    routes_t = jnp.swapaxes(routes[:, 0], 1, 2)
    gates_t = jnp.swapaxes(gates[:, 0], 1, 2)

    by_row, by_token = shape((slots, tokens)), shape((tokens, slots))
    routing = call(
        routing_kernel, [by_row, by_token, by_row, by_row, by_token, by_token] * 2, routes_t, gates_t, live_row
    )
    pick, spread, high_t, low_t, high, low = zip(routing[:6], routing[6:])
    send_shape = shape((ep, pair, width))

    dh_2, send_cotangent = call(
        cotangent_kernel,
        [shape((tokens, width), F32), send_shape],
        cotangent[0],
        live_col,
        high_t[1],
        low_t[1],
    )

    in_smem = pl.BlockSpec(memory_space=pltpu.SMEM)
    in_vmem = pl.BlockSpec(memory_space=pltpu.VMEM)
    in_hbm = pl.BlockSpec(memory_space=pltpu.HBM)

    def held(dims):
        return [pltpu.VMEM(dims, BF16), pltpu.SemaphoreType.DMA(())]

    output_dims = ((width, width), (fsdp, blocks - fsdp, tokens, 256))

    rows_out = shape((2, ep * MOST, width))
    units_out = shape((2, ep * MOST, hidden_units))
    rows_spec, units_spec = expert_block((ep * MOST, width)), expert_block((ep * MOST, hidden_units))
    pair_spec = whole_block((ep, pair, width))
    held_rows = [pltpu.VMEM((ep, MOST, width), F32)]

    def run_experts(layer, received):
        return expert_call(
            expert_kernel,
            [pair_spec, weight_block(expert_w[layer].shape)],
            [pair_spec, rows_spec, units_spec, units_spec, units_spec],
            [send_shape, rows_out, units_out, units_out, units_out],
            received,
            expert_w[layer],
            scratch=held_rows,
        )

    def experts_back(layer, dy, kept, beside=()):
        _, x, gate, up, act = kept
        dx, dy_rows, dgate, dup = expert_call(
            expert_back_kernel,
            [pair_spec, weight_block(expert_w[layer].shape), units_spec, units_spec],
            [pair_spec, rows_spec, units_spec, units_spec],
            [send_shape, rows_out, units_out, units_out],
            dy,
            expert_w[layer],
            gate,
            up,
            scratch=held_rows,
        )
        back = exchange(dx, "ep").reshape(slots, width)
        (grads,) = expert_call(
            expert_grads_kernel,
            [rows_spec, rows_spec, units_spec, units_spec, units_spec],
            [weight_block(expert_w[layer].shape)],
            [shape(expert_w[layer].shape)],
            x,
            dy_rows,
            act,
            dgate,
            dup,
        )
        return lax.optimization_barrier((back, grads, beside))

    def scatter_grads(grads):
        return lax.psum_scatter(grads, "fsdp", scatter_dimension=0, tiled=False)

    def part_of(layer, shard):
        return call(
            part_kernel, shape((tokens, 128)), shard, w_gate[layer], w_up[layer], norm_mlp[layer].astype(F32)[:, None]
        )

    def move(parts):
        moved = [parts[0]] + [lax.ppermute(parts[step], "fsdp", along_fsdp(step, 0)) for step in steps[1:]]
        mates = jnp.concatenate([m[1:2] for m in moved], axis=0)
        return [*moved, lax.ppermute(mates, "fsdp", along_fsdp(0, 1))]

    def output_grads(mixed, gathered):
        return call(
            functools.partial(output_grads_kernel, pieces=pieces, cores=cores),
            shape((tokens, width)),
            me_arg,
            *gathered,
            mixed,
            in_specs=[in_smem] + [in_vmem] * (len(pieces) + 1),
            scratch=[pltpu.VMEM((slot, width), BF16)],
        )

    def attention_back(layer, back, after, dh, qkv, total, normed_all):
        w = out_w[layer]
        late = layer == 1
        dafter, dattn, *dmixed = call(
            functools.partial(after_back_kernel, groups=fsdp, cores=cores, gain_row=2 * layer + 1),
            [shape((tokens, width), F32), shape((tokens, width))]
            + ([shape((cores, tokens, 128))] * chips if late else [shape((fsdp, tokens, 128))]),
            me_arg,
            back,
            spread[layer],
            after,
            gains_all,
            dh,
            w,
            in_specs=[in_smem] + [in_vmem] * 5 + [in_hbm],
            scratch=held(output_dims[layer]),
        )
        dmixed = move(dmixed) if late else [exchange(dmixed[0], "fsdp").reshape(slot, 128)]
        gathered = None if late else gather_slot(dattn)
        if not late:
            start = len(steps)
            dmixed, gathered[1:start] = lax.optimization_barrier((dmixed, gathered[1:start]))
        whole = [pltpu.VMEM((slot, 128), BF16), pltpu.VMEM((slot, 256), BF16)]
        dqkv = [shape((cores, tokens, 256))] * chips if late else [shape((slot, 256))]
        grads = [shape((ep, fsdp, tokens // ep, 256))]
        outs = call(
            functools.partial(attend_back_kernel, rows=256, cores=cores, steps=steps if late else ()),
            dqkv + grads,
            me_arg,
            lengths,
            qkv,
            total,
            normed_all,
            cos_all,
            sin_all,
            *dmixed,
            in_specs=[in_smem] * 2 + [in_vmem] * (5 + len(dmixed)),
            scratch=[pltpu.VMEM((slot, 128), F32)] * 2 + (whole if late else []),
        )
        return dafter, dattn, gathered, outs[: len(dqkv)], outs[len(dqkv)]

    row_size = tokens // side

    def cut_rows(parts):
        all_size = sum(p.shape[1] for p in parts)
        return call(
            functools.partial(chunks_kernel, count=side),
            [shape((row_size, all_size))] * side,
            place,
            *parts,
            in_specs=[in_smem] + [in_vmem] * len(parts),
            scratch=[pltpu.VMEM((tokens, all_size), BF16)],
        )

    def sum_ep(chunks, beside):
        all_size = chunks[0].shape[1]
        arrived = [chunks[0]] + [lax.ppermute(chunks[k], "ep", along_ep(0, k)) for k in steps[1:]]
        chunks = call(
            functools.partial(sum_split_kernel, count=side),
            [shape((row_size // side, all_size))] * side,
            place,
            *arrived,
            in_specs=[in_smem] + [in_vmem] * side,
            scratch=[pltpu.VMEM((row_size, all_size), F32)],
        )
        arrived = [chunks[0]] + [lax.ppermute(chunks[k], "ep", along_ep(k, 0)) for k in steps[1:]]
        arrived[0], first = lax.optimization_barrier((arrived[0], beside[0]))
        piece = call(sum_kernel, shape((row_size // side, all_size)), *arrived)
        arrived = [piece] + [lax.ppermute(piece, "ep", along_ep(k, 0)) for k in (1, 2, 3)]
        arrived[0], second = lax.optimization_barrier((arrived[0], beside[1]))
        piece = call(
            functools.partial(join_kernel, count=side),
            shape((row_size, all_size)),
            place,
            *arrived,
            in_specs=[in_smem] + [in_vmem] * side,
            scratch=[pltpu.VMEM((row_size, all_size), F32)],
        )
        arrived = [piece] + [lax.ppermute(piece, "ep", along_ep(0, k)) for k in (1, 2, 3)]
        arrived[0], third = lax.optimization_barrier((arrived[0], beside[2]))
        return arrived, (*first, *second, *third)

    kept_out = [shape((slot, width)), shape((slot, 256))]

    gains_all, normed_0, qkv_0, mixed, total_0 = call(
        functools.partial(first_kernel, pieces=pieces, cores=cores, rows=256),
        [shape((8, width), F32)] + kept_out + [shape((slot, 128)), shape((slot, 128), F32)],
        me_arg,
        lengths,
        *pieces_0,
        group_0,
        cos_all,
        sin_all,
        in_specs=[in_smem] * 2 + [in_vmem] * (len(pieces) + 3),
    )
    mixed_0 = mixed
    mixed_back = exchange(mixed.reshape(fsdp, tokens, 128), "fsdp")
    after_0, send = call(
        after_first_kernel,
        [shape((tokens, width), F32), send_shape],
        mixed_back,
        attn_out,
        hidden_0,
        gains_all,
        pick[0],
        in_specs=[in_vmem, in_hbm] + [in_vmem] * 3,
        scratch=held(output_dims[0]),
    )
    kept_0 = run_experts(0, exchange(send, "ep"))
    y_0 = exchange(kept_0[0], "ep").reshape(slots, width)
    y_0, send_cotangent = lax.optimization_barrier((y_0, send_cotangent))
    dy_1 = exchange(send_cotangent, "ep")
    hidden_1, normed = call(
        middle_kernel,
        [shape((tokens, width), F32), shape((tokens, width))],
        after_0,
        y_0,
        high[0],
        low[0],
        gains_all,
    )
    normed_1, qkv_1, total_1, mixed_1, *mixed = call(
        functools.partial(second_kernel, pieces=pieces, cores=cores, rows=256),
        kept_out + [shape((slot, 128), F32), shape((slot, 128))] + [shape((cores, tokens, 128))] * chips,
        me_arg,
        lengths,
        *gather_slot(normed),
        lax.dynamic_index_in_dim(attn_1, me, 1, False),
        cos_all,
        sin_all,
        in_specs=[in_smem] * 2 + [in_vmem] * (len(pieces) + 3),
    )
    after_1, send = call(
        functools.partial(after_second_kernel, steps=steps, cores=cores, groups=fsdp),
        [shape((tokens, width), F32), send_shape],
        me_arg,
        *move(mixed),
        attn_1,
        hidden_1,
        gains_all,
        pick[1],
        in_specs=[in_smem] + [in_vmem] * (chips + 1) + [in_hbm] + [in_vmem] * 3,
        scratch=[pltpu.VMEM((tokens, width), BF16)] + held(output_dims[1]),
    )
    send, dy_1, group_back = lax.optimization_barrier((send, dy_1, group_back))
    attn_0 = lax.all_gather(group_back, "fsdp", axis=0)
    kept_1 = run_experts(1, exchange(send, "ep"))

    back, grads, _ = experts_back(1, dy_1, kept_1)
    shard_1 = scatter_grads(grads)
    back, attn_0 = lax.optimization_barrier((back, attn_0))
    y_late, back = lax.optimization_barrier((kept_1[0], back))
    y_1 = exchange(y_late, "ep").reshape(slots, width)
    dafter, dattn, _, dqkv, few_1 = attention_back(1, back, after_1, dh_2, qkv_1, total_1, normed_1)
    dh_1, send = call(
        functools.partial(middle_back_kernel, steps=steps, cores=cores),
        [shape((tokens, width), F32), send_shape],
        me_arg,
        *move(dqkv),
        attn_1,
        hidden_1,
        gains_all,
        dafter,
        high_t[0],
        low_t[0],
        in_specs=[in_smem] + [in_vmem] * (chips + 1) + [in_hbm] + [in_vmem] * 5,
        scratch=[pltpu.VMEM((tokens, 2 * width), BF16)] + held((fsdp, fsdp, tokens, 256)),
    )
    send, dattn, y_1 = lax.optimization_barrier((send, dattn, y_1))
    gate_grad_0 = call(
        gates_kernel, shape((8, tokens), F32), y_0, dh_1, live_col, pick[0], routes_t[0]
    )
    hidden_out, gate_grad_1 = call(
        final_kernel,
        [shape((tokens, width)), shape((8, tokens), F32)],
        after_1,
        y_1,
        high[1],
        low[1],
        dh_2,
        pick[1],
        routes_t[1],
    )
    dy_0, gathered, gate_grad_0, gate_grad_1, hidden_out = lax.optimization_barrier(
        (exchange(send, "ep"), gather_slot(dattn), gate_grad_0, gate_grad_1, hidden_out)
    )
    back, grads, (part_1, output_1) = experts_back(
        0, dy_0, kept_0, (part_of(1, shard_1), output_grads(mixed_1, gathered))
    )
    shard_0 = scatter_grads(grads)
    dafter, _, gathered, dqkv, few_0 = attention_back(0, back, after_0, dh_1, qkv_0, total_0, normed_0)

    output_0 = output_grads(mixed_0, gathered)
    part_0 = part_of(0, shard_0)
    few = jnp.concatenate([few_0, few_1], axis=2).reshape(ep * fsdp, 2 * tokens // ep, 256)
    few = lax.all_to_all(few, ("ep", "fsdp"), 0, 0, tiled=True).reshape(ep, fsdp, 2 * tokens // ep, 256)
    chunks = cut_rows([output_0, output_1, part_0, part_1])
    few, dqkv, chunks = lax.optimization_barrier((few, dqkv, chunks))
    few = call(sum_slots_kernel, shape(few.shape[1:]), few)[None]
    few = jnp.concatenate([few] + [lax.ppermute(few, "ep", along_ep(k, 0)) for k in (1, 2, 3)], axis=0)
    few = [few] + [lax.ppermute(few, "ep", along_ep(0, k)) for k in (1, 2, 3)]
    dh_0 = call(
        last_back_kernel,
        shape((tokens, width), F32),
        exchange(dqkv[0].reshape(fsdp, tokens, 256), "fsdp"),
        attn_0,
        hidden_0,
        gains_all,
        dafter,
        in_specs=[in_vmem, in_hbm] + [in_vmem] * 3,
        scratch=held((fsdp, fsdp, tokens + 16, 256)),
    )
    expert_grads = call(expert_out_kernel, [shape(w_gate.shape, F32)] * 3, shard_0, shard_1)
    summed, beside = sum_ep(chunks, (tuple(expert_grads), (dh_0,), ()))
    *expert_grads, dh_0 = beside
    half = width // 2
    query_grad, key_grad, value_grad, output_grad, attn_gain_grad, mlp_gain_grad = call(
        functools.partial(attention_out_kernel, count=side),
        [shape((2, tokens, width), F32)]
        + [shape((2, tokens, half), F32)] * 2
        + [shape((2, tokens, width), F32)]
        + [shape((2, tokens), F32)] * 2,
        place,
        *summed,
        *few,
        w_query,
        w_key,
        w_value,
        norm_attn.astype(F32).T,
        in_specs=[in_smem] + [in_vmem] * (2 * side + 4),
        scratch=[
            pltpu.VMEM((2, tokens, 2 * width), F32),
            pltpu.VMEM((tokens, 2 * width + 256), BF16),
        ],
    )
    gates_grad = jnp.swapaxes(jnp.stack([gate_grad_0, gate_grad_1]), 1, 2)[:, None]

    return (
        hidden_out[None],
        dh_0[None],
        gates_grad,
        attn_gain_grad,
        query_grad,
        key_grad,
        value_grad,
        output_grad,
        mlp_gain_grad,
        *expert_grads,
    )


def solution(mesh):
    row = P(None, "fsdp", None)
    expert = P(None, "ep", "fsdp", None)
    hidden = P("ep", "fsdp", None)
    gain = P(None, "fsdp")
    return jax.shard_map(
        on_device,
        mesh=mesh,
        in_specs=(hidden, hidden, P("ep"), expert, expert, gain, row, row, row, row, gain, expert, expert, expert),
        out_specs=(hidden, hidden, expert, gain, row, row, row, row, gain, expert, expert, expert),
        check_vma=False,
    )
```

```python
import functools

import jax
import jax.numpy as jnp
import numpy as np
from jax import lax
from jax.experimental import pallas as pl
from jax.experimental.pallas import tpu as pltpu
from jax.sharding import PartitionSpec as P

HD = 64
EPS = 1e-06
THETA = 10000.0
NEG_FILL = -1e30
MOST = 40
MIB = 1024 * 1024
VMEM = 62
F32 = jnp.float32
BF16 = jnp.bfloat16


def dot(left, right):
    return lax.dot_general(left, right, (((1,), (0,)), ((), ())), preferred_element_type=F32)


def dot_nt(left, right):
    return lax.dot_general(left, right, (((1,), (1,)), ((), ())), preferred_element_type=F32)


def dot_tn(left, right):
    return lax.dot_general(left, right, (((0,), (0,)), ((), ())), preferred_element_type=F32)


def split_low(value):
    high = value.astype(BF16)
    return high, (value - high.astype(F32)).astype(BF16)


def rms_parts(hidden):
    scale = lax.rsqrt(jnp.mean(hidden * hidden, axis=-1, keepdims=True) + EPS)
    return hidden * scale, scale


def rms_back(hidden, gain, grad):
    unit, scale = rms_parts(hidden)
    scaled = grad * gain
    return scale * (scaled - unit * jnp.mean(scaled * unit, axis=-1, keepdims=True))


def swap_halves(value):
    lane = lax.broadcasted_iota(jnp.int32, value.shape, 1) % HD
    return jnp.where(lane < HD // 2, pltpu.roll(value, 128 - HD // 2, 1), pltpu.roll(value, HD // 2, 1))


def low_lanes(shape):
    return lax.broadcasted_iota(jnp.int32, shape, 1) < HD


def call(kernel, outs, *args, vmem=VMEM, scratch=(), **extra):
    return pl.pallas_call(
        kernel,
        out_shape=outs,
        scratch_shapes=scratch,
        compiler_params=pltpu.CompilerParams(vmem_limit_bytes=vmem * MIB),
        **extra,
    )(*args)


def shape(dims, dtype=BF16):
    return jax.ShapeDtypeStruct(dims, dtype)


def routing_kernel(routes_ref, gates_ref, live_ref, *out_refs):
    experts, tokens = out_refs[0].shape[0] // MOST, routes_ref.shape[2]
    earlier = lax.broadcasted_iota(jnp.int32, (tokens, tokens), 0) < lax.broadcasted_iota(
        jnp.int32, (tokens, tokens), 1
    )
    earlier = earlier.astype(F32).astype(BF16)
    expert_id = lax.broadcasted_iota(jnp.int32, (experts, tokens), 0)
    place_id = lax.broadcasted_iota(jnp.int32, (experts, MOST, tokens), 1).astype(F32)
    for layer in range(routes_ref.shape[0]):
        named = jnp.zeros((experts, tokens), F32)
        weight = jnp.zeros((experts, tokens), F32)
        for k in range(routes_ref.shape[1]):
            same = routes_ref[layer, k : k + 1, :] == expert_id
            named = named + jnp.where(same, 1.0, 0.0)
            weight = weight + jnp.where(same, gates_ref[layer, k : k + 1, :], 0.0)
        weight = weight * live_ref[0:1, :]
        rank = dot(named.astype(BF16), earlier)
        rank = jnp.where(named > 0.5, rank, -1.0)
        here = rank[:, None, :] == place_id
        pick = jnp.where(here, 1.0, 0.0).reshape(experts * MOST, tokens)
        weights = jnp.where(here, weight[:, None, :], 0.0).reshape(experts * MOST, tokens)
        high, low = split_low(weights)
        outs = out_refs[5 * layer : 5 * layer + 5]
        outs[0][...] = pick.astype(BF16)
        outs[1][...] = pick.T.astype(BF16)
        outs[2][...] = high
        outs[3][...] = high.astype(F32).T.astype(BF16)
        outs[4][...] = low.astype(F32).T.astype(BF16)


def put_groups(wq_ref, wk_ref, wv_ref, out_ref):
    rows = wq_ref.shape[1]
    low_half = low_lanes((rows, 128))
    groups = wq_ref.shape[2] // 128
    for g in range(groups):
        out_ref[g, 0:rows, 0:128] = wq_ref[0, :, g * 128 : (g + 1) * 128]
    for j in range(groups // 2):
        key = wk_ref[0, :, j * 128 : (j + 1) * 128].astype(F32)
        value = wv_ref[0, :, j * 128 : (j + 1) * 128].astype(F32)
        out_ref[2 * j, 0:rows, 128:256] = jnp.where(low_half, key, pltpu.roll(value, HD, 1)).astype(BF16)
        out_ref[2 * j + 1, 0:rows, 128:256] = jnp.where(low_half, pltpu.roll(key, HD, 1), value).astype(BF16)


def group_kernel(wq_ref, wk_ref, wv_ref, wo_ref, attn_ref, mlp_ref, out_ref, wo_out_ref):
    gains = jnp.concatenate([attn_ref[...].astype(F32), mlp_ref[...].astype(F32)], axis=1)
    gains = jnp.concatenate([gains, jnp.zeros((14, 256), F32)], axis=0).astype(BF16)
    put_groups(wq_ref, wk_ref, wv_ref, out_ref)
    wo_out_ref[...] = wo_ref[0]
    for g in range(out_ref.shape[0]):
        out_ref[g, wq_ref.shape[1] :, :] = gains


def shards_kernel(wq_ref, wk_ref, wv_ref, wo_ref, gate_ref, up_ref, down_ref, attn_ref, *expert_refs):
    put_groups(wq_ref, wk_ref, wv_ref, attn_ref)
    groups = wq_ref.shape[2] // 128
    for j in range(attn_ref.shape[0] - groups):
        attn_ref[groups + j] = wo_ref[0, :, j * 256 : (j + 1) * 256]
    for layer, out_ref in enumerate(expert_refs):
        for e in range(2):
            out_ref[3 * e] = gate_ref[layer, e]
            out_ref[3 * e + 1] = up_ref[layer, e]
            out_ref[3 * e + 2] = down_ref[layer, e]


def fetch(source, held_ref, sem):
    copy = pltpu.make_async_copy(source, held_ref, sem)
    copy.start()
    return copy


def blocks_of(w_ref, groups):
    return w_ref if len(w_ref.shape) == 2 else w_ref.at[:, pl.ds(groups, w_ref.shape[1] - groups)]


def times_output(mixed, held_ref):
    if len(held_ref.shape) == 2:
        return dot(mixed, held_ref[...])
    return jnp.concatenate(
        [dot(mixed, held_ref[:, j].reshape(mixed.shape[1], 256)) for j in range(held_ref.shape[1])], axis=1
    )


def times_output_t(grad, held_ref):
    if len(held_ref.shape) == 2:
        return dot_nt(grad, held_ref[...])
    return sum(
        dot_nt(grad[:, j * 256 : (j + 1) * 256], held_ref[:, j].reshape(grad.shape[1], 256))
        for j in range(held_ref.shape[1])
    )


def relative(me, cores, count, step, flip):
    return lax.rem(me // cores - step + count, count) * cores + lax.rem(me % cores + flip, cores)


def turned(chunk, cos, sin):
    return chunk * cos + swap_halves(chunk) * sin


def wide(qkv_ref):
    keyval = qkv_ref[:, 128:256].astype(F32)
    low_half = low_lanes(keyval.shape)
    turn = pltpu.roll(keyval, HD, 1)
    zero = jnp.zeros_like(keyval)
    keys = (jnp.where(low_half, keyval, zero).astype(BF16), jnp.where(low_half, zero, turn).astype(BF16))
    return keys, (jnp.where(low_half, turn, zero).astype(BF16), jnp.where(low_half, zero, keyval).astype(BF16))


def masks(length, slot, rows):
    ahead = jnp.where(lax.broadcasted_iota(jnp.int32, (1, slot), 1) < length, 0.0, NEG_FILL)
    row_id = lax.broadcasted_iota(jnp.int32, (rows, rows), 0)
    return ahead, jnp.where(lax.broadcasted_iota(jnp.int32, (rows, rows), 1) <= row_id, 0.0, NEG_FILL)


def masked(scores, ahead, causal):
    rows, span = scores.shape
    own = scores[:, span - rows :] + (ahead[:, span - rows : span] + causal)
    if span == rows:
        return own
    return jnp.concatenate([scores[:, : span - rows] + ahead[:, : span - rows], own], axis=1)


def attend(length, qkv_ref, rows, put):
    slot = qkv_ref.shape[0]
    key_wide, value_wide = wide(qkv_ref)
    ahead, causal = masks(length, slot, rows)
    for block in range(slot // rows):
        span = (block + 1) * rows
        query = qkv_ref[pl.ds(block * rows, rows), 0:128] * jnp.asarray(HD**-0.5, BF16)
        mixed = jnp.zeros((rows, 128), F32)
        totals = []
        for head in range(2):
            scores = masked(dot_nt(query, key_wide[head][:span]), ahead, causal)
            top = jnp.max(scores, axis=-1, keepdims=True)
            expo = jnp.exp(scores - top)
            total = jnp.sum(expo, axis=-1, keepdims=True)
            probs = (expo * (1.0 / total)).astype(BF16)
            mixed = mixed + dot(probs, value_wide[head][:span])
            totals.append(top + jnp.log(total))
        put(block, mixed.astype(BF16), totals)


def put_moved(me, cores, moved_refs, owner, piece):
    chips = len(moved_refs)
    step = lax.rem(owner // cores - me // cores + chips, chips)
    flip = lax.rem(owner % cores + me % cores, cores)
    for k in range(chips):

        @pl.when(step == k)
        def _():
            moved_refs[k][flip] = piece


def place_moved(me, cores, steps, moved, mate_ref, out_ref, size, dim):
    for k, step in enumerate(steps):
        for flip, piece in ((0, moved[k][0]), (1, mate_ref[k])):
            at = pl.ds(pl.multiple_of(relative(me, cores, len(steps), step, flip) * size, size), size)
            if dim == 0:
                out_ref[at, :] = piece
            else:
                out_ref[:, at] = piece


def first_kernel(
    me_ref, length_ref, *refs, pieces, cores, rows
):
    moved = refs[: len(pieces)]
    w_ref, cos_ref, sin_ref, gains_ref, normed_ref, qkv_ref, mixed_ref, total_ref = refs[len(pieces) :]
    me = me_ref[0]
    shards, _, _ = w_ref.shape
    tokens = moved[0].shape[0]
    for row in range(2):
        for half in range(2):
            gains_ref[2 * row + half : 2 * row + half + 1, :] = jnp.concatenate(
                [w_ref[s, tokens + row : tokens + row + 1, half * 128 : (half + 1) * 128] for s in range(shards)], axis=1
            ).astype(F32)
    gain = gains_ref[0:1, :]
    for (step, flip), piece in zip(pieces, moved):
        at = relative(me, cores, shards // cores, step, flip) * tokens
        unit, _ = rms_parts(piece[...].astype(F32))
        normed_ref[pl.ds(pl.multiple_of(at, tokens), tokens), :] = (unit * gain).astype(BF16)
    weights = w_ref[:, :tokens, :].reshape(shards * tokens, 256)
    raw = dot(normed_ref[...], weights)
    cos, sin = cos_ref[...], sin_ref[...]
    qkv_ref[:, 0:128] = turned(raw[:, 0:128], cos, sin).astype(BF16)
    keyval = raw[:, 128:256]
    qkv_ref[:, 128:256] = jnp.where(low_lanes(keyval.shape), turned(keyval, cos, sin), keyval).astype(BF16)

    def put(block, mixed, totals):
        at = pl.ds(block * rows, rows)
        mixed_ref[at, :] = mixed
        for head in range(2):
            total_ref[at, head * HD : (head + 1) * HD] = jnp.broadcast_to(totals[head], (rows, HD))

    attend(length_ref[0], qkv_ref, rows, put)


def second_kernel(me_ref, length_ref, *refs, pieces, cores, rows):
    moved = refs[: len(pieces)]
    w_ref, cos_ref, sin_ref, normed_ref, qkv_ref, total_ref, mixed_ref = refs[len(pieces) : len(pieces) + 7]
    moved_refs = refs[len(pieces) + 7 :]
    me = me_ref[0]
    tokens = moved[0].shape[0]
    devices = normed_ref.shape[0] // tokens
    chips = devices // cores
    for (step, flip), piece in zip(pieces, moved):
        at = relative(me, cores, chips, step, flip) * tokens
        normed_ref[pl.ds(pl.multiple_of(at, tokens), tokens), :] = piece[...]
    normed = normed_ref[...]
    cos, sin = cos_ref[...], sin_ref[...]
    raw = dot(normed, w_ref[...].reshape(normed.shape[1], 256))
    qkv_ref[:, 0:128] = turned(raw[:, 0:128], cos, sin).astype(BF16)
    keyval = raw[:, 128:256]
    qkv_ref[:, 128:256] = jnp.where(low_lanes(keyval.shape), turned(keyval, cos, sin), keyval).astype(BF16)

    def put(block, mixed, totals):
        at = pl.ds(block * rows, rows)
        for head in range(2):
            total_ref[at, head * HD : (head + 1) * HD] = jnp.broadcast_to(totals[head], (rows, HD))
        mixed_ref[at, :] = mixed
        for part in range(rows // tokens):
            put_moved(me, cores, moved_refs, block * (rows // tokens) + part, mixed[part * tokens : (part + 1) * tokens])

    attend(length_ref[0], qkv_ref, rows, put)


def middle_kernel(after_ref, back_ref, high_ref, low_ref, gains_ref, hidden_ref, normed_ref):
    back = back_ref[...]
    hidden = after_ref[...] + (dot(high_ref[...], back) + dot(low_ref[...], back))
    hidden_ref[...] = hidden
    unit, _ = rms_parts(hidden)
    normed_ref[...] = (unit * gains_ref[2:3, :]).astype(BF16)


def attend_back_kernel(
    me_ref, length_ref, qkv_ref, total_ref, normed_ref, cos_ref, sin_ref, *refs, rows, cores, steps
):
    slot = qkv_ref.shape[0]
    if steps:
        count = len(steps)
        moved, mate_ref = refs[:count], refs[count]
        moved_refs = refs[count + 1 : 2 * count + 1]
        grads_ref, dk_ref, dv_ref, grad_ref, out_ref = refs[2 * count + 1 :]
        place_moved(me_ref[0], cores, steps, moved, mate_ref, grad_ref, slot // count // cores, 0)
    else:
        grad_ref, out_ref, grads_ref, dk_ref, dv_ref = refs
    length = length_ref[0]
    key_wide, value_wide = wide(qkv_ref)
    ahead, causal = masks(length, slot, rows)
    low_half = low_lanes((slot, 128))
    dk_ref[...] = jnp.zeros((slot, 128), F32)
    dv_ref[...] = jnp.zeros((slot, 128), F32)
    low_row = low_lanes((rows, 128))
    zero_row = jnp.zeros((rows, 128), BF16)
    for block in range(slot // rows):
        span = (block + 1) * rows
        at = pl.ds(block * rows, rows)
        query = qkv_ref[at, 0:128] * jnp.asarray(HD**-0.5, BF16)
        grad = grad_ref[at, :]
        dq = jnp.zeros((rows, 128), F32)
        for head in range(2):
            keep = low_row if head == 0 else jnp.logical_not(low_row)
            scores = masked(dot_nt(query, key_wide[head][:span]), ahead, causal)
            probs = jnp.exp(scores - total_ref[at, head * HD : head * HD + 1])
            dprobs = dot_nt(grad, value_wide[head][:span])
            mean = jnp.sum(dprobs * probs, axis=-1, keepdims=True)
            dscores = (probs * (dprobs - mean)).astype(BF16)
            dq = dq + dot(dscores, key_wide[head][:span])
            dk_ref[:span, :] += dot_tn(dscores, jnp.where(keep, query, zero_row))
            dv_ref[:span, :] += dot_tn(probs.astype(BF16), jnp.where(keep, grad, zero_row))
        dq = dq * (HD**-0.5)
        out_ref[at, 0:128] = (dq * cos_ref[at, :] - swap_halves(dq) * sin_ref[at, :]).astype(BF16)
    dk = dk_ref[...]
    dk = dk + pltpu.roll(dk, HD, 1)
    dk = dk * cos_ref[...] - swap_halves(dk) * sin_ref[...]
    dv = dv_ref[...]
    dv = dv + pltpu.roll(dv, HD, 1)
    out_ref[:, 128:256] = jnp.where(low_half, dk, dv).astype(BF16)
    grads = dot_tn(normed_ref[...], out_ref[...])
    devices = slot // 128
    size = grads.shape[0] // devices
    for owner in range(devices):
        at = slice(owner * size, (owner + 1) * size)
        if steps:
            put_moved(me_ref[0], cores, moved_refs, owner, out_ref[owner * 128 : (owner + 1) * 128, :])
        parts, few = grads_ref.shape[0], grads_ref.shape[2]
        grads_ref[:, owner] = grads[at].reshape(parts, few, grads.shape[1]).astype(BF16)


def after_step(mixed, copy, held_ref, hidden_ref, gain, pick_ref, after_ref, send_ref):
    copy.wait()
    after = hidden_ref[...].astype(F32) + times_output(mixed, held_ref)
    after_ref[...] = after
    unit, _ = rms_parts(after)
    send_ref[...] = dot(pick_ref[...], (unit * gain).astype(BF16)).astype(BF16).reshape(send_ref.shape)


def after_first_kernel(
    mixed_ref, w_ref, hidden_ref, gains_ref, pick_ref, after_ref, send_ref, held_ref, sem
):
    copy = fetch(w_ref, held_ref, sem)
    mixed = jnp.concatenate([mixed_ref[g] for g in range(mixed_ref.shape[0])], axis=1)
    after_step(mixed, copy, held_ref, hidden_ref, gains_ref[1:2, :], pick_ref, after_ref, send_ref)


def after_second_kernel(me_ref, *refs, steps, cores, groups):
    moved, mate_ref = refs[: len(steps)], refs[len(steps)]
    w_ref, hidden_ref, gains_ref, pick_ref, after_ref, send_ref, mixed_out_ref, held_ref, sem = refs[len(steps) + 1 :]
    copy = fetch(blocks_of(w_ref, groups), held_ref, sem)
    place_moved(me_ref[0], cores, steps, moved, mate_ref, mixed_out_ref, 128, 1)
    after_step(mixed_out_ref[...], copy, held_ref, hidden_ref, gains_ref[3:4, :], pick_ref, after_ref, send_ref)


def pack(weights, grad, send_ref):
    send_ref[...] = dot(weights, grad.astype(BF16)).astype(BF16).reshape(send_ref.shape)


def cotangent_kernel(grad_ref, live_ref, weights_ref, dh_ref, send_ref):
    grad = grad_ref[...].astype(F32) * live_ref[...]
    dh_ref[...] = grad
    pack(weights_ref[...], grad, send_ref)


def after_back_kernel(
    me_ref, back_ref, place_ref, after_ref, gains_ref, dh_ref, w_ref, dafter_ref, dattn_ref, gain_grad_ref, *refs, groups, cores, gain_row
):
    *dmixed_refs, held_ref, sem = refs
    copy = fetch(blocks_of(w_ref, groups), held_ref, sem)
    dmoe = dot(place_ref[...], back_ref[...])
    unit, _ = rms_parts(after_ref[...])
    gain_grad_ref[...] = jnp.broadcast_to(jnp.sum(dmoe * unit, axis=0, keepdims=True), gain_grad_ref.shape)
    dafter = dh_ref[...] + rms_back(after_ref[...], gains_ref[gain_row : gain_row + 1, :], dmoe)
    dafter_ref[...] = dafter
    dattn = dafter.astype(BF16)
    dattn_ref[...] = dattn
    copy.wait()
    dmixed = times_output_t(dattn, held_ref).astype(BF16)
    for g in range(groups):
        if len(dmixed_refs) == 1:
            dmixed_refs[0][g] = dmixed[:, g * 128 : (g + 1) * 128]
        else:
            put_moved(me_ref[0], cores, dmixed_refs, g, dmixed[:, g * 128 : (g + 1) * 128])


def project_back(grads, copy, held_ref, hidden, gain, dafter):
    rows, groups = grads.shape[0], held_ref.shape[1]
    copy.wait()
    dnormed = sum(
        dot_nt(grads[:, g * 256 : (g + 1) * 256], held_ref[:, g, 0:rows].reshape(hidden.shape[1], 256))
        for g in range(groups)
    )
    return dafter + rms_back(hidden, gain, dnormed)


def middle_back_kernel(me_ref, *refs, steps, cores):
    moved, mate_ref = refs[: len(steps)], refs[len(steps)]
    w_ref, hidden_ref, gains_ref, dafter_ref, weights_ref, dh_ref, send_ref, back_ref, held_ref, sem = refs[len(steps) + 1 :]
    copy = fetch(w_ref.at[:, pl.ds(0, held_ref.shape[1])], held_ref, sem)
    place_moved(me_ref[0], cores, steps, moved, mate_ref, back_ref, 256, 1)
    dh = project_back(back_ref[...], copy, held_ref, hidden_ref[...], gains_ref[2:3, :], dafter_ref[...])
    dh_ref[...] = dh
    pack(weights_ref[...], dh, send_ref)


def last_back_kernel(back_ref, w_ref, hidden_ref, gains_ref, dafter_ref, dh_ref, held_ref, sem):
    copy = fetch(w_ref.at[:, pl.ds(0, held_ref.shape[1])], held_ref, sem)
    grads = jnp.concatenate([back_ref[g] for g in range(back_ref.shape[0])], axis=1)
    dh_ref[...] = project_back(
        grads, copy, held_ref, hidden_ref[...].astype(F32), gains_ref[0:1, :], dafter_ref[...]
    )


def output_grads_kernel(me_ref, *refs, pieces, cores):
    moved, (mixed_ref, out_ref, all_ref) = refs[: len(pieces)], refs[len(pieces) :]
    tokens = moved[0].shape[0]
    chips = all_ref.shape[0] // tokens // cores
    for (step, flip), piece in zip(pieces, moved):
        at = relative(me_ref[0], cores, chips, step, flip) * tokens
        all_ref[pl.ds(pl.multiple_of(at, tokens), tokens), :] = piece[...]
    out_ref[...] = dot_tn(mixed_ref[...], all_ref[...]).astype(BF16)


def output_part_kernel(mixed_ref, dattn_ref, gain_grad_ref, out_ref):
    shards, rows, _ = out_ref.shape
    mixed = jnp.concatenate([mixed_ref[g] for g in range(mixed_ref.shape[0])], axis=1)
    width = mixed.shape[1]
    out_ref[:, :, 0:width] = dot_tn(mixed, dattn_ref[...]).astype(BF16).reshape(shards, rows, width)
    gain = jnp.broadcast_to(gain_grad_ref[0:1, :], (128, width)).T
    lane = lax.broadcasted_iota(jnp.int32, gain.shape, 1)
    out_ref[:, :, width:] = jnp.where(lane == 0, gain, 0.0).astype(BF16).reshape(shards, rows, 128)


def sum_slots_kernel(few_ref, rows_ref, out_ref):
    count, groups, _, lanes = few_ref.shape
    size, first = rows_ref.shape[1:]
    out_ref[:, 0:first] = sum(rows_ref[e].astype(F32) for e in range(count)).astype(BF16)
    few = sum(few_ref[e].astype(F32) for e in range(count))
    for layer in range(2):
        for g in range(groups):
            at = first + (layer * groups + g) * lanes
            out_ref[:, at : at + lanes] = few[g, layer * size : (layer + 1) * size].astype(BF16)


def join_kernel(place_ref, *refs, count):
    arrived, out_ref, held_ref = refs[:count], refs[count], refs[count + 1]
    size = arrived[0].shape[0]
    for k, piece in enumerate(arrived):
        at = lax.rem(place_ref[0] - k + count, count) * size
        held_ref[pl.ds(pl.multiple_of(at, size), size), :] = piece[...].astype(F32)
    out_ref[...] = held_ref[...].astype(BF16)


def attention_out_kernel(place_ref, *refs, count):
    arrived = refs[:count]
    (wq_ref, wk_ref, wv_ref, gain_ref, query_ref, key_ref, value_ref, out_ref, attn_ref, mlp_ref, ref) = refs[count:]
    width = wq_ref.shape[2]
    groups = width // 128
    size = arrived[0].shape[0]
    for k, piece in enumerate(arrived):
        at = lax.rem(place_ref[1] - k + count, count) * size
        ref[pl.ds(pl.multiple_of(at, size), size), :] = piece[...]
    low_half = low_lanes((size * count, 128))
    for layer in range(2):
        first = 2 * width + 256 + layer * 2 * width
        total = jnp.zeros(low_half.shape, F32)
        for g in range(groups):
            query = ref[:, first + g * 256 : first + g * 256 + 128].astype(F32)
            query_ref[layer, :, g * 128 : (g + 1) * 128] = query
            total = total + query * wq_ref[layer, :, g * 128 : (g + 1) * 128].astype(F32)
        for j in range(groups // 2):
            even = ref[:, first + 512 * j + 128 : first + 512 * j + 256].astype(F32)
            odd = ref[:, first + 512 * j + 384 : first + 512 * j + 512].astype(F32)
            key = jnp.where(low_half, even, pltpu.roll(odd, HD, 1))
            value = jnp.where(low_half, pltpu.roll(even, HD, 1), odd)
            at = slice(j * 128, (j + 1) * 128)
            key_ref[layer, :, at] = key
            value_ref[layer, :, at] = value
            total = total + key * wk_ref[layer, :, at].astype(F32) + value * wv_ref[layer, :, at].astype(F32)
        out_ref[layer] = ref[:, layer * width : (layer + 1) * width].astype(F32)
        gain = jnp.sum(total, axis=1, keepdims=True) / gain_ref[:, layer : layer + 1]
        attn_ref[layer : layer + 1, :] = jnp.broadcast_to(gain, low_half.shape).T[0:1, :]
        column = ref[:, 2 * width + layer * 128 : 2 * width + (layer + 1) * 128]
        mlp_ref[layer : layer + 1, :] = column.astype(F32).T[0:1, :]


def part_kernel(shard_ref, gate_ref, up_ref, gain_ref, part_ref):
    total = jnp.zeros(gate_ref.shape[1:], F32)
    for e in range(2):
        total = total + shard_ref[3 * e].astype(F32) * gate_ref[e].astype(F32)
        total = total + shard_ref[3 * e + 1].astype(F32) * up_ref[e].astype(F32)
    gain = jnp.sum(total, axis=1, keepdims=True) / gain_ref[...]
    lane = lax.broadcasted_iota(jnp.int32, (total.shape[0], 128), 1)
    part_ref[...] = jnp.where(lane == 0, gain, 0.0).astype(BF16)


def rows_kernel(first_ref, second_ref, part_ref, out_ref):
    width = second_ref.shape[1]
    out_ref[:, 0:width] = first_ref[:, 0:width]
    out_ref[:, width : 2 * width] = second_ref[...]
    out_ref[:, 2 * width : 2 * width + 128] = first_ref[:, width:]
    out_ref[:, 2 * width + 128 :] = part_ref[...]


def expert_out_kernel(first_ref, second_ref, gate_ref, up_ref, down_ref):
    for layer, ref in enumerate((first_ref, second_ref)):
        for e in range(2):
            gate_ref[layer, e] = ref[3 * e].astype(F32)
            up_ref[layer, e] = ref[3 * e + 1].astype(F32)
            down_ref[layer, e] = ref[3 * e + 2].astype(F32)


def gate_grads(back, dh, pick_ref, routes_ref, out_ref):
    high, low = split_low(dh)
    slots, tokens = pick_ref.shape
    product = dot_nt(back, high) + dot_nt(back, low)
    product = product * pick_ref[...].astype(F32)
    each = jnp.sum(product.reshape(slots // MOST, MOST, tokens), axis=1)
    expert_id = lax.broadcasted_iota(jnp.int32, each.shape, 0)
    for k in range(routes_ref.shape[0]):
        out_ref[k : k + 1, :] = jnp.sum(
            jnp.where(routes_ref[k : k + 1, :] == expert_id, each, 0.0), axis=0, keepdims=True
        )


def gates_kernel(back_ref, dh_ref, live_ref, pick_ref, routes_ref, out_ref):
    gate_grads(back_ref[...], dh_ref[...] * live_ref[...], pick_ref, routes_ref, out_ref)


def final_kernel(after_ref, back_ref, high_ref, low_ref, dh_ref, pick_ref, routes_ref, hidden_ref, out_ref):
    back = back_ref[...]
    hidden = after_ref[...] + (dot(high_ref[...], back) + dot(low_ref[...], back))
    hidden_ref[...] = hidden.astype(BF16)
    gate_grads(back, dh_ref[...], pick_ref, routes_ref, out_ref)


def rows_of(ref, expert):
    both = ref[...].astype(F32)
    rows = both[:, expert * MOST : (expert + 1) * MOST, :]
    return rows.reshape(rows.shape[0] * MOST, rows.shape[2]).astype(BF16)


def weights_of(w_ref, which):
    part = w_ref[:, which]
    return part.reshape(part.shape[0] * part.shape[1], part.shape[2])


def put_rows(rows, expert, held_ref, out_ref):
    sources = out_ref.shape[0]
    rows = rows.reshape(sources, MOST, rows.shape[1])
    if expert == 0:
        held_ref[...] = rows
    else:
        out_ref[...] = jnp.concatenate([held_ref[...], rows], axis=1).astype(BF16)


def expert_kernel(x_ref, w_ref, y_ref, gate_ref, up_ref, held_ref):
    def one(expert):
        rows = rows_of(x_ref, expert)
        gate = dot(rows, weights_of(w_ref, 0))
        up = dot(rows, weights_of(w_ref, 1))
        gate_ref[0] = gate.astype(BF16)
        up_ref[0] = up.astype(BF16)
        act = (gate * (1.0 / (1.0 + jnp.exp(-gate))) * up).astype(BF16)
        put_rows(dot_nt(act, weights_of(w_ref, 2)), expert, held_ref, y_ref)

    for expert in range(2):
        pl.when(pl.program_id(0) == expert)(functools.partial(one, expert))


def expert_back_kernel(dy_ref, w_ref, gate_ref, up_ref, dx_ref, dgate_ref, dup_ref, held_ref):
    def one(expert):
        rows = rows_of(dy_ref, expert)
        dact = dot(rows, weights_of(w_ref, 2))
        gate = gate_ref[0].astype(F32)
        up = up_ref[0].astype(F32)
        sigma = 1.0 / (1.0 + jnp.exp(-gate))
        dgate = (dact * up * (sigma * (1.0 + gate * (1.0 - sigma)))).astype(BF16)
        dup = (dact * (gate * sigma)).astype(BF16)
        dgate_ref[0] = dgate
        dup_ref[0] = dup
        dx = dot_nt(dgate, weights_of(w_ref, 0)) + dot_nt(dup, weights_of(w_ref, 1))
        put_rows(dx, expert, held_ref, dx_ref)

    for expert in range(2):
        pl.when(pl.program_id(0) == expert)(functools.partial(one, expert))


def expert_grads_kernel(x_ref, dy_ref, gate_ref, up_ref, dgate_ref, dup_ref, out_ref):
    shards, _, rows, hidden = out_ref.shape

    def one(expert):
        x = rows_of(x_ref, expert)
        gate = gate_ref[0].astype(F32)
        act = (gate * (1.0 / (1.0 + jnp.exp(-gate))) * up_ref[0].astype(F32)).astype(BF16)
        out_ref[:, 0] = dot_tn(x, dgate_ref[0]).astype(BF16).reshape(shards, rows, hidden)
        out_ref[:, 1] = dot_tn(x, dup_ref[0]).astype(BF16).reshape(shards, rows, hidden)
        out_ref[:, 2] = dot_tn(rows_of(dy_ref, expert), act).astype(BF16).reshape(shards, rows, hidden)

    for expert in range(2):
        pl.when(pl.program_id(0) == expert)(functools.partial(one, expert))


def whole_block(dims):
    return pl.BlockSpec(dims, lambda e: (0,) * len(dims))


def expert_block(dims):
    return pl.BlockSpec((1,) + dims, lambda e: (e,) + (0,) * len(dims))


def weight_block(dims):
    return pl.BlockSpec((dims[0], 3) + dims[2:], lambda e: (0, e, 0, 0))


def expert_call(kernel, specs, out_specs, outs, *args, vmem=VMEM, scratch=()):
    return pl.pallas_call(
        kernel,
        grid=(2,),
        in_specs=specs,
        out_specs=out_specs,
        out_shape=outs,
        scratch_shapes=scratch,
        compiler_params=pltpu.CompilerParams(
            vmem_limit_bytes=vmem * MIB, dimension_semantics=("arbitrary",)
        ),
    )(*args)


def on_device(
    hidden_in,
    cotangent,
    lengths,
    routes,
    gates,
    norm_attn,
    w_query,
    w_key,
    w_value,
    w_output,
    norm_mlp,
    w_gate,
    w_up,
    w_down,
):
    _, tokens, width = hidden_in.shape
    hidden_units = w_gate.shape[3]
    ep = lax.axis_size("ep")
    fsdp = lax.axis_size("fsdp")
    slot = tokens * fsdp
    slots = ep * 2 * MOST
    pair = 2 * MOST
    me = lax.axis_index("fsdp")

    def exchange(value, axis):
        return lax.all_to_all(value, axis, 0, 0, tiled=True)

    def gather(value):
        return lax.all_gather(value, "fsdp", axis=0, tiled=True)

    cores = 2
    chips = fsdp // cores
    side = 4
    here = lax.axis_index("ep")
    place = jnp.stack([here % side, here // side, here, me]).astype(jnp.int32)
    me_arg = me.reshape(1).astype(jnp.int32)

    def along_fsdp(step, flip):
        return [
            (f, (f // cores + step) % chips * cores + (f % cores + flip) % cores) for f in range(fsdp)
        ]

    def along_ep(step_z, step_x):
        return [
            (e, (e // side + step_z) % (ep // side) * side + (e % side + step_x) % side) for e in range(ep)
        ]

    steps = (0, 1, 3, 2)
    pieces = [(step, flip) for flip in range(cores) for step in steps]

    def gather_slot(value):
        own = [value] + [lax.ppermute(value, "fsdp", along_fsdp(step, 0)) for step in steps[1:]]
        return own + [lax.ppermute(piece, "fsdp", along_fsdp(0, 1)) for piece in own]

    def layer_of(array, layer):
        dims = (1,) + array.shape[1:]
        return pl.BlockSpec(dims, lambda _: (layer,) + (0,) * (len(dims) - 1))

    hidden_0 = hidden_in[0]
    pieces_0 = gather_slot(hidden_0)
    mine = [w_query, w_key, w_value, w_output, w_gate, w_up, w_down]
    group_0, output_0 = pl.pallas_call(
        group_kernel,
        grid=(1,),
        in_specs=[layer_of(w, 0) for w in (w_query, w_key, w_value, w_output)]
        + [pl.BlockSpec((2, tokens), lambda _: (0, 0))] * 2,
        out_specs=[
            pl.BlockSpec((fsdp, tokens + 16, 256), lambda _: (0, 0, 0)),
            pl.BlockSpec((tokens, width), lambda _: (0, 0)),
        ],
        out_shape=[shape((fsdp, tokens + 16, 256)), shape((tokens, width))],
        compiler_params=pltpu.CompilerParams(vmem_limit_bytes=VMEM * MIB),
    )(*mine[:4], norm_attn, norm_mlp)
    expert_dims = (6,) + w_gate.shape[2:]
    blocks = fsdp + width // 256
    blocks = fsdp + width // 256
    group_back, group_0 = group_0, exchange(group_0, "fsdp")
    shard_1, *expert_shards = pl.pallas_call(
        shards_kernel,
        grid=(1,),
        in_specs=[layer_of(w, 1) for w in mine[:4]] + [pl.BlockSpec(w.shape, lambda _: (0,) * 4) for w in mine[4:]],
        out_specs=[pl.BlockSpec((blocks, tokens, 256), lambda _: (0, 0, 0))]
        + [pl.BlockSpec(expert_dims, lambda _: (0, 0, 0))] * 2,
        out_shape=[shape((blocks, tokens, 256)), shape(expert_dims), shape(expert_dims)],
        compiler_params=pltpu.CompilerParams(vmem_limit_bytes=VMEM * MIB),
    )(*mine)
    attn_out = gather(output_0)
    experts_0 = lax.all_gather(expert_shards[0], "fsdp", axis=0)
    attn_1 = lax.all_gather(shard_1, "fsdp", axis=0)
    experts_1 = lax.all_gather(expert_shards[1], "fsdp", axis=0)
    out_w = (attn_out, attn_1)
    expert_w = (experts_0, experts_1)


    lane = np.arange(128)
    frequency = np.float32(THETA) ** (np.float32(-2.0) * (lane % 32).astype(np.float32) / np.float32(HD))
    angles = np.arange(slot, dtype=np.float32)[:, None] * frequency.astype(np.float32)[None, :]
    cos_all = jnp.asarray(np.cos(angles).astype(np.float32))
    sin_all = jnp.asarray((np.sin(angles) * np.where(lane % HD < HD // 2, -1.0, 1.0)[None, :]).astype(np.float32))
    live = (me * tokens + jnp.arange(tokens, dtype=jnp.int32) < lengths[0]).astype(F32)
    live_col = live[:, None]
    live_row = jnp.broadcast_to(live[None, :], (8, tokens))
    routes_t = jnp.swapaxes(routes[:, 0], 1, 2)
    gates_t = jnp.swapaxes(gates[:, 0], 1, 2)

    by_row, by_token = shape((slots, tokens)), shape((tokens, slots))
    routing = call(
        routing_kernel, [by_row, by_token, by_row, by_token, by_token] * 2, routes_t, gates_t, live_row
    )
    pick, spread, high_t, high, low = zip(routing[:5], routing[5:])
    send_shape = shape((ep, pair, width))

    dh_2, send_cotangent = call(
        cotangent_kernel,
        [shape((tokens, width), F32), send_shape],
        cotangent[0],
        live_col,
        high_t[1],
    )

    in_smem = pl.BlockSpec(memory_space=pltpu.SMEM)
    in_vmem = pl.BlockSpec(memory_space=pltpu.VMEM)
    in_hbm = pl.BlockSpec(memory_space=pltpu.HBM)

    def held(dims):
        return [pltpu.VMEM(dims, BF16), pltpu.SemaphoreType.DMA(())]

    output_dims = ((width, width), (fsdp, blocks - fsdp, tokens, 256))

    units_out = shape((2, ep * MOST, hidden_units))
    units_spec = expert_block((ep * MOST, hidden_units))
    pair_spec = whole_block((ep, pair, width))
    held_rows = [pltpu.VMEM((ep, MOST, width), F32)]

    def run_experts(layer, received):
        return received, *expert_call(
            expert_kernel,
            [pair_spec, weight_block(expert_w[layer].shape)],
            [pair_spec, units_spec, units_spec],
            [send_shape, units_out, units_out],
            received,
            expert_w[layer],
            scratch=held_rows,
        )

    def experts_back(layer, dy, kept, beside=()):
        x, _, gate, up = kept
        dx, dgate, dup = expert_call(
            expert_back_kernel,
            [pair_spec, weight_block(expert_w[layer].shape), units_spec, units_spec],
            [pair_spec, units_spec, units_spec],
            [send_shape, units_out, units_out],
            dy,
            expert_w[layer],
            gate,
            up,
            scratch=held_rows,
        )
        back = exchange(dx, "ep").reshape(slots, width)
        (grads,) = expert_call(
            expert_grads_kernel,
            [pair_spec, pair_spec, units_spec, units_spec, units_spec, units_spec],
            [weight_block(expert_w[layer].shape)],
            [shape(expert_w[layer].shape)],
            x,
            dy,
            gate,
            up,
            dgate,
            dup,
        )
        return lax.optimization_barrier((back, grads, beside))

    def scatter_grads(grads):
        return lax.psum_scatter(grads, "fsdp", scatter_dimension=0, tiled=False)

    def part_of(layer, shard):
        return call(
            part_kernel, shape((tokens, 128)), shard, w_gate[layer], w_up[layer], norm_mlp[layer].astype(F32)[:, None]
        )

    def move(parts):
        moved = [parts[0]] + [lax.ppermute(parts[step], "fsdp", along_fsdp(step, 0)) for step in steps[1:]]
        mates = jnp.concatenate([m[1:2] for m in moved], axis=0)
        return [*moved, lax.ppermute(mates, "fsdp", along_fsdp(0, 1))]

    def output_grads(mixed, gathered):
        return call(
            functools.partial(output_grads_kernel, pieces=pieces, cores=cores),
            shape((tokens, width)),
            me_arg,
            *gathered,
            mixed,
            in_specs=[in_smem] + [in_vmem] * (len(pieces) + 1),
            scratch=[pltpu.VMEM((slot, width), BF16)],
        )

    def attention_back(layer, back, after, dh, qkv, total, normed_all):
        w = out_w[layer]
        late = layer == 1
        dafter, dattn, gain_grad, *dmixed = call(
            functools.partial(after_back_kernel, groups=fsdp, cores=cores, gain_row=2 * layer + 1),
            [shape((tokens, width), F32), shape((tokens, width)), shape((8, width), F32)]
            + ([shape((cores, tokens, 128))] * chips if late else [shape((fsdp, tokens, 128))]),
            me_arg,
            back,
            spread[layer],
            after,
            gains_all,
            dh,
            w,
            in_specs=[in_smem] + [in_vmem] * 5 + [in_hbm],
            scratch=held(output_dims[layer]),
        )
        dmixed = move(dmixed) if late else [exchange(dmixed[0], "fsdp").reshape(slot, 128)]
        whole = [pltpu.VMEM((slot, 128), BF16), pltpu.VMEM((slot, 256), BF16)]
        dqkv = [shape((cores, tokens, 256))] * chips if late else [shape((slot, 256))]
        grads = [shape((ep, fsdp, tokens // ep, 256))]
        outs = call(
            functools.partial(attend_back_kernel, rows=256, cores=cores, steps=steps if late else ()),
            dqkv + grads,
            me_arg,
            lengths,
            qkv,
            total,
            normed_all,
            cos_all,
            sin_all,
            *dmixed,
            in_specs=[in_smem] * 2 + [in_vmem] * (5 + len(dmixed)),
            scratch=[pltpu.VMEM((slot, 128), F32)] * 2 + (whole if late else []),
        )
        return dafter, dattn, gain_grad, outs[: len(dqkv)], outs[len(dqkv)]

    kept_out = [shape((slot, width)), shape((slot, 256))]

    gains_all, normed_0, qkv_0, mixed, total_0 = call(
        functools.partial(first_kernel, pieces=pieces, cores=cores, rows=256),
        [shape((8, width), F32)] + kept_out + [shape((slot, 128)), shape((slot, 128), F32)],
        me_arg,
        lengths,
        *pieces_0,
        group_0,
        cos_all,
        sin_all,
        in_specs=[in_smem] * 2 + [in_vmem] * (len(pieces) + 3),
    )
    mixed_0 = exchange(mixed.reshape(fsdp, tokens, 128), "fsdp")
    after_0, send = call(
        after_first_kernel,
        [shape((tokens, width), F32), send_shape],
        mixed_0,
        attn_out,
        hidden_0,
        gains_all,
        pick[0],
        in_specs=[in_vmem, in_hbm] + [in_vmem] * 3,
        scratch=held(output_dims[0]),
    )
    kept_0 = run_experts(0, exchange(send, "ep"))
    y_0 = exchange(kept_0[1], "ep").reshape(slots, width)
    y_0, send_cotangent = lax.optimization_barrier((y_0, send_cotangent))
    dy_1 = exchange(send_cotangent, "ep")
    hidden_1, normed = call(
        middle_kernel,
        [shape((tokens, width), F32), shape((tokens, width))],
        after_0,
        y_0,
        high[0],
        low[0],
        gains_all,
    )
    normed_1, qkv_1, total_1, mixed_1, *mixed = call(
        functools.partial(second_kernel, pieces=pieces, cores=cores, rows=256),
        kept_out + [shape((slot, 128), F32), shape((slot, 128))] + [shape((cores, tokens, 128))] * chips,
        me_arg,
        lengths,
        *gather_slot(normed),
        lax.dynamic_index_in_dim(attn_1, me, 1, False),
        cos_all,
        sin_all,
        in_specs=[in_smem] * 2 + [in_vmem] * (len(pieces) + 3),
    )
    after_1, send = call(
        functools.partial(after_second_kernel, steps=steps, cores=cores, groups=fsdp),
        [shape((tokens, width), F32), send_shape],
        me_arg,
        *move(mixed),
        attn_1,
        hidden_1,
        gains_all,
        pick[1],
        in_specs=[in_smem] + [in_vmem] * (chips + 1) + [in_hbm] + [in_vmem] * 3,
        scratch=[pltpu.VMEM((tokens, width), BF16)] + held(output_dims[1]),
    )
    send, dy_1, group_back = lax.optimization_barrier((send, dy_1, group_back))
    attn_0 = lax.all_gather(group_back, "fsdp", axis=0)
    kept_1 = run_experts(1, exchange(send, "ep"))

    back, grads, _ = experts_back(1, dy_1, kept_1)
    shard_1 = scatter_grads(grads)
    back, attn_0 = lax.optimization_barrier((back, attn_0))
    y_late, back = lax.optimization_barrier((kept_1[1], back))
    y_1 = exchange(y_late, "ep").reshape(slots, width)
    dafter, dattn, _, dqkv, few_1 = attention_back(1, back, after_1, dh_2, qkv_1, total_1, normed_1)
    dh_1, send = call(
        functools.partial(middle_back_kernel, steps=steps, cores=cores),
        [shape((tokens, width), F32), send_shape],
        me_arg,
        *move(dqkv),
        attn_1,
        hidden_1,
        gains_all,
        dafter,
        high_t[0],
        in_specs=[in_smem] + [in_vmem] * (chips + 1) + [in_hbm] + [in_vmem] * 4,
        scratch=[pltpu.VMEM((tokens, 2 * width), BF16)] + held((fsdp, fsdp, tokens, 256)),
    )
    send, dattn, y_1 = lax.optimization_barrier((send, dattn, y_1))
    gate_grad_0 = call(
        gates_kernel, shape((8, tokens), F32), y_0, dh_1, live_col, pick[0], routes_t[0]
    )
    hidden_out, gate_grad_1 = call(
        final_kernel,
        [shape((tokens, width)), shape((8, tokens), F32)],
        after_1,
        y_1,
        high[1],
        low[1],
        dh_2,
        pick[1],
        routes_t[1],
    )
    dy_0, gathered, gate_grad_0, gate_grad_1, hidden_out = lax.optimization_barrier(
        (exchange(send, "ep"), gather_slot(dattn), gate_grad_0, gate_grad_1, hidden_out)
    )
    back, grads, (part_1, output_1) = experts_back(
        0, dy_0, kept_0, (part_of(1, shard_1), output_grads(mixed_1, gathered))
    )
    dafter, dattn, gain_grad, dqkv, few_0 = attention_back(0, back, after_0, dh_1, qkv_0, total_0, normed_0)

    output_0 = scatter_grads(
        call(output_part_kernel, shape((fsdp, tokens, width + 128)), mixed_0, dattn, gain_grad)
    )
    rows = call(rows_kernel, shape((tokens, 2 * width + 256)), output_0, output_1, part_1)
    few = jnp.concatenate([few_0, few_1], axis=2).reshape(ep * fsdp, 2 * tokens // ep, 256)
    few = lax.all_to_all(few, ("ep", "fsdp"), 0, 0, tiled=True).reshape(ep, fsdp, 2 * tokens // ep, 256)
    few, grads, rows = lax.optimization_barrier((few, grads, rows))
    shard_0 = scatter_grads(grads)
    rows = exchange(rows.reshape(ep, tokens // ep, rows.shape[1]), "ep")
    few, rows, dqkv = lax.optimization_barrier((few, rows, dqkv))
    piece = call(sum_slots_kernel, shape((tokens // ep, rows.shape[2] + 4 * width)), few, rows)
    arrived = [piece] + [lax.ppermute(piece, "ep", along_ep(0, k)) for k in (1, 2, 3)]
    dh_0 = call(
        last_back_kernel,
        shape((tokens, width), F32),
        exchange(dqkv[0].reshape(fsdp, tokens, 256), "fsdp"),
        attn_0,
        hidden_0,
        gains_all,
        dafter,
        in_specs=[in_vmem, in_hbm] + [in_vmem] * 3,
        scratch=held((fsdp, fsdp, tokens + 16, 256)),
    )
    expert_grads = call(expert_out_kernel, [shape(w_gate.shape, F32)] * 3, shard_0, shard_1)
    arrived[0], expert_grads = lax.optimization_barrier((arrived[0], expert_grads))
    piece = call(
        functools.partial(join_kernel, count=side),
        shape((side * piece.shape[0], piece.shape[1])),
        place,
        *arrived,
        in_specs=[in_smem] + [in_vmem] * side,
        scratch=[pltpu.VMEM((side * piece.shape[0], piece.shape[1]), F32)],
    )
    arrived = [piece] + [lax.ppermute(piece, "ep", along_ep(k, 0)) for k in (1, 2, 3)]
    arrived[0], dh_0 = lax.optimization_barrier((arrived[0], dh_0))
    half = width // 2
    query_grad, key_grad, value_grad, output_grad, attn_gain_grad, mlp_gain_grad = call(
        functools.partial(attention_out_kernel, count=side),
        [shape((2, tokens, width), F32)]
        + [shape((2, tokens, half), F32)] * 2
        + [shape((2, tokens, width), F32)]
        + [shape((2, tokens), F32)] * 2,
        place,
        *arrived,
        w_query,
        w_key,
        w_value,
        norm_attn.astype(F32).T,
        in_specs=[in_smem] + [in_vmem] * (side + 4),
        scratch=[pltpu.VMEM((tokens, piece.shape[1]), BF16)],
    )
    gates_grad = jnp.swapaxes(jnp.stack([gate_grad_0, gate_grad_1]), 1, 2)[:, None]

    return (
        hidden_out[None],
        dh_0[None],
        gates_grad,
        attn_gain_grad,
        query_grad,
        key_grad,
        value_grad,
        output_grad,
        mlp_gain_grad,
        *expert_grads,
    )


def solution(mesh):
    row = P(None, "fsdp", None)
    expert = P(None, "ep", "fsdp", None)
    hidden = P("ep", "fsdp", None)
    gain = P(None, "fsdp")
    return jax.shard_map(
        on_device,
        mesh=mesh,
        in_specs=(hidden, hidden, P("ep"), expert, expert, gain, row, row, row, row, gain, expert, expert, expert),
        out_specs=(hidden, hidden, expert, gain, row, row, row, row, gain, expert, expert, expert),
        check_vma=False,
    )
```

```python
import functools

import jax
import jax.numpy as jnp
import numpy as np
from jax import lax
from jax.experimental import pallas as pl
from jax.experimental.pallas import tpu as pltpu
from jax.sharding import PartitionSpec as P

HD = 64
EPS = 1e-06
THETA = 10000.0
NEG_FILL = -1e30
MOST = 40
MIB = 1024 * 1024
VMEM = 62
F32 = jnp.float32
BF16 = jnp.bfloat16


def dot(left, right):
    return lax.dot_general(left, right, (((1,), (0,)), ((), ())), preferred_element_type=F32)


def dot_nt(left, right):
    return lax.dot_general(left, right, (((1,), (1,)), ((), ())), preferred_element_type=F32)


def dot_tn(left, right):
    return lax.dot_general(left, right, (((0,), (0,)), ((), ())), preferred_element_type=F32)


def split_low(value):
    high = value.astype(BF16)
    return high, (value - high.astype(F32)).astype(BF16)


def rms_parts(hidden):
    scale = lax.rsqrt(jnp.mean(hidden * hidden, axis=-1, keepdims=True) + EPS)
    return hidden * scale, scale


def rms_back(hidden, gain, grad):
    unit, scale = rms_parts(hidden)
    scaled = grad * gain
    return scale * (scaled - unit * jnp.mean(scaled * unit, axis=-1, keepdims=True))


def swap_halves(value):
    lane = lax.broadcasted_iota(jnp.int32, value.shape, 1) % HD
    return jnp.where(lane < HD // 2, pltpu.roll(value, 128 - HD // 2, 1), pltpu.roll(value, HD // 2, 1))


def low_lanes(shape):
    return lax.broadcasted_iota(jnp.int32, shape, 1) < HD


def call(kernel, outs, *args, vmem=VMEM, scratch=(), **extra):
    return pl.pallas_call(
        kernel,
        out_shape=outs,
        scratch_shapes=scratch,
        compiler_params=pltpu.CompilerParams(vmem_limit_bytes=vmem * MIB),
        **extra,
    )(*args)


def shape(dims, dtype=BF16):
    return jax.ShapeDtypeStruct(dims, dtype)


def routing_kernel(routes_ref, gates_ref, live_ref, *out_refs):
    experts, tokens = out_refs[0].shape[0] // MOST, routes_ref.shape[2]
    earlier = lax.broadcasted_iota(jnp.int32, (tokens, tokens), 0) < lax.broadcasted_iota(
        jnp.int32, (tokens, tokens), 1
    )
    earlier = earlier.astype(F32).astype(BF16)
    expert_id = lax.broadcasted_iota(jnp.int32, (experts, tokens), 0)
    place_id = lax.broadcasted_iota(jnp.int32, (experts, MOST, tokens), 1).astype(F32)
    for layer in range(routes_ref.shape[0]):
        named = jnp.zeros((experts, tokens), F32)
        weight = jnp.zeros((experts, tokens), F32)
        for k in range(routes_ref.shape[1]):
            same = routes_ref[layer, k : k + 1, :] == expert_id
            named = named + jnp.where(same, 1.0, 0.0)
            weight = weight + jnp.where(same, gates_ref[layer, k : k + 1, :], 0.0)
        weight = weight * live_ref[0:1, :]
        rank = dot(named.astype(BF16), earlier)
        rank = jnp.where(named > 0.5, rank, -1.0)
        here = rank[:, None, :] == place_id
        pick = jnp.where(here, 1.0, 0.0).reshape(experts * MOST, tokens)
        weights = jnp.where(here, weight[:, None, :], 0.0).reshape(experts * MOST, tokens)
        high, low = split_low(weights)
        outs = out_refs[5 * layer : 5 * layer + 5]
        outs[0][...] = pick.astype(BF16)
        outs[1][...] = pick.T.astype(BF16)
        outs[2][...] = high
        outs[3][...] = high.astype(F32).T.astype(BF16)
        outs[4][...] = low.astype(F32).T.astype(BF16)


def put_groups(wq_ref, wk_ref, wv_ref, out_ref):
    rows = wq_ref.shape[1]
    low_half = low_lanes((rows, 128))
    groups = wq_ref.shape[2] // 128
    for g in range(groups):
        out_ref[g, 0:rows, 0:128] = wq_ref[0, :, g * 128 : (g + 1) * 128]
    for j in range(groups // 2):
        key = wk_ref[0, :, j * 128 : (j + 1) * 128].astype(F32)
        value = wv_ref[0, :, j * 128 : (j + 1) * 128].astype(F32)
        out_ref[2 * j, 0:rows, 128:256] = jnp.where(low_half, key, pltpu.roll(value, HD, 1)).astype(BF16)
        out_ref[2 * j + 1, 0:rows, 128:256] = jnp.where(low_half, pltpu.roll(key, HD, 1), value).astype(BF16)


def group_kernel(wq_ref, wk_ref, wv_ref, wo_ref, attn_ref, mlp_ref, out_ref, wo_out_ref):
    gains = jnp.concatenate([attn_ref[...].astype(F32), mlp_ref[...].astype(F32)], axis=1)
    gains = jnp.concatenate([gains, jnp.zeros((14, 256), F32)], axis=0).astype(BF16)
    put_groups(wq_ref, wk_ref, wv_ref, out_ref)
    wo_out_ref[...] = wo_ref[0]
    for g in range(out_ref.shape[0]):
        out_ref[g, wq_ref.shape[1] :, :] = gains


def shards_kernel(wq_ref, wk_ref, wv_ref, wo_ref, gate_ref, up_ref, down_ref, attn_ref, *expert_refs):
    put_groups(wq_ref, wk_ref, wv_ref, attn_ref)
    groups = wq_ref.shape[2] // 128
    for j in range(attn_ref.shape[0] - groups):
        attn_ref[groups + j] = wo_ref[0, :, j * 256 : (j + 1) * 256]
    for layer, out_ref in enumerate(expert_refs):
        for e in range(2):
            out_ref[3 * e] = gate_ref[layer, e]
            out_ref[3 * e + 1] = up_ref[layer, e]
            out_ref[3 * e + 2] = down_ref[layer, e]


def fetch(source, held_ref, sem):
    copy = pltpu.make_async_copy(source, held_ref, sem)
    copy.start()
    return copy


def blocks_of(w_ref, groups):
    return w_ref if len(w_ref.shape) == 2 else w_ref.at[:, pl.ds(groups, w_ref.shape[1] - groups)]


def times_output(mixed, held_ref):
    if len(held_ref.shape) == 2:
        return dot(mixed, held_ref[...])
    return jnp.concatenate(
        [dot(mixed, held_ref[:, j].reshape(mixed.shape[1], 256)) for j in range(held_ref.shape[1])], axis=1
    )


def times_output_t(grad, held_ref):
    if len(held_ref.shape) == 2:
        return dot_nt(grad, held_ref[...])
    return sum(
        dot_nt(grad[:, j * 256 : (j + 1) * 256], held_ref[:, j].reshape(grad.shape[1], 256))
        for j in range(held_ref.shape[1])
    )


def relative(me, cores, count, step, flip):
    return lax.rem(me // cores - step + count, count) * cores + lax.rem(me % cores + flip, cores)


def turned(chunk, cos, sin):
    return chunk * cos + swap_halves(chunk) * sin


def wide(qkv_ref):
    keyval = qkv_ref[:, 128:256].astype(F32)
    low_half = low_lanes(keyval.shape)
    turn = pltpu.roll(keyval, HD, 1)
    zero = jnp.zeros_like(keyval)
    keys = (jnp.where(low_half, keyval, zero).astype(BF16), jnp.where(low_half, zero, turn).astype(BF16))
    return keys, (jnp.where(low_half, turn, zero).astype(BF16), jnp.where(low_half, zero, keyval).astype(BF16))


def masks(length, slot, rows):
    ahead = jnp.where(lax.broadcasted_iota(jnp.int32, (1, slot), 1) < length, 0.0, NEG_FILL)
    row_id = lax.broadcasted_iota(jnp.int32, (rows, rows), 0)
    return ahead, jnp.where(lax.broadcasted_iota(jnp.int32, (rows, rows), 1) <= row_id, 0.0, NEG_FILL)


def masked(scores, ahead, causal):
    rows, span = scores.shape
    own = scores[:, span - rows :] + (ahead[:, span - rows : span] + causal)
    if span == rows:
        return own
    return jnp.concatenate([scores[:, : span - rows] + ahead[:, : span - rows], own], axis=1)


def attend(length, qkv_ref, rows, put):
    slot = qkv_ref.shape[0]
    key_wide, value_wide = wide(qkv_ref)
    ahead, causal = masks(length, slot, rows)
    for block in range(slot // rows):
        span = (block + 1) * rows
        query = qkv_ref[pl.ds(block * rows, rows), 0:128] * jnp.asarray(HD**-0.5, BF16)
        mixed = jnp.zeros((rows, 128), F32)
        totals = []
        for head in range(2):
            scores = masked(dot_nt(query, key_wide[head][:span]), ahead, causal)
            top = jnp.max(scores, axis=-1, keepdims=True)
            expo = jnp.exp(scores - top)
            total = jnp.sum(expo, axis=-1, keepdims=True)
            probs = (expo * (1.0 / total)).astype(BF16)
            mixed = mixed + dot(probs, value_wide[head][:span])
            totals.append(top + jnp.log(total))
        put(block, mixed.astype(BF16), totals)


def put_moved(me, cores, moved_refs, owner, piece):
    chips = len(moved_refs)
    step = lax.rem(owner // cores - me // cores + chips, chips)
    flip = lax.rem(owner % cores + me % cores, cores)
    for k in range(chips):

        @pl.when(step == k)
        def _():
            moved_refs[k][flip] = piece


def place_moved(me, cores, steps, moved, mate_ref, out_ref, size, dim):
    for k, step in enumerate(steps):
        for flip, piece in ((0, moved[k][0]), (1, mate_ref[k])):
            at = pl.ds(pl.multiple_of(relative(me, cores, len(steps), step, flip) * size, size), size)
            if dim == 0:
                out_ref[at, :] = piece
            else:
                out_ref[:, at] = piece


def first_kernel(
    me_ref, length_ref, *refs, pieces, cores, rows
):
    moved = refs[: len(pieces)]
    w_ref, cos_ref, sin_ref, gains_ref, normed_ref, qkv_ref, mixed_ref, total_ref = refs[len(pieces) :]
    me = me_ref[0]
    shards, _, _ = w_ref.shape
    tokens = moved[0].shape[0]
    for row in range(2):
        for half in range(2):
            gains_ref[2 * row + half : 2 * row + half + 1, :] = jnp.concatenate(
                [w_ref[s, tokens + row : tokens + row + 1, half * 128 : (half + 1) * 128] for s in range(shards)], axis=1
            ).astype(F32)
    gain = gains_ref[0:1, :]
    for (step, flip), piece in zip(pieces, moved):
        at = relative(me, cores, shards // cores, step, flip) * tokens
        unit, _ = rms_parts(piece[...].astype(F32))
        normed_ref[pl.ds(pl.multiple_of(at, tokens), tokens), :] = (unit * gain).astype(BF16)
    weights = w_ref[:, :tokens, :].reshape(shards * tokens, 256)
    raw = dot(normed_ref[...], weights)
    cos, sin = cos_ref[...], sin_ref[...]
    qkv_ref[:, 0:128] = turned(raw[:, 0:128], cos, sin).astype(BF16)
    keyval = raw[:, 128:256]
    qkv_ref[:, 128:256] = jnp.where(low_lanes(keyval.shape), turned(keyval, cos, sin), keyval).astype(BF16)

    def put(block, mixed, totals):
        at = pl.ds(block * rows, rows)
        mixed_ref[at, :] = mixed
        for head in range(2):
            total_ref[at, head * HD : (head + 1) * HD] = jnp.broadcast_to(totals[head], (rows, HD))

    attend(length_ref[0], qkv_ref, rows, put)


def second_kernel(me_ref, length_ref, *refs, pieces, cores, rows):
    moved = refs[: len(pieces)]
    w_ref, cos_ref, sin_ref, normed_ref, qkv_ref, total_ref, mixed_ref = refs[len(pieces) : len(pieces) + 7]
    moved_refs = refs[len(pieces) + 7 :]
    me = me_ref[0]
    tokens = moved[0].shape[0]
    devices = normed_ref.shape[0] // tokens
    chips = devices // cores
    for (step, flip), piece in zip(pieces, moved):
        at = relative(me, cores, chips, step, flip) * tokens
        normed_ref[pl.ds(pl.multiple_of(at, tokens), tokens), :] = piece[...]
    normed = normed_ref[...]
    cos, sin = cos_ref[...], sin_ref[...]
    raw = dot(normed, w_ref[...].reshape(normed.shape[1], 256))
    qkv_ref[:, 0:128] = turned(raw[:, 0:128], cos, sin).astype(BF16)
    keyval = raw[:, 128:256]
    qkv_ref[:, 128:256] = jnp.where(low_lanes(keyval.shape), turned(keyval, cos, sin), keyval).astype(BF16)

    def put(block, mixed, totals):
        at = pl.ds(block * rows, rows)
        for head in range(2):
            total_ref[at, head * HD : (head + 1) * HD] = jnp.broadcast_to(totals[head], (rows, HD))
        mixed_ref[at, :] = mixed
        for part in range(rows // tokens):
            put_moved(me, cores, moved_refs, block * (rows // tokens) + part, mixed[part * tokens : (part + 1) * tokens])

    attend(length_ref[0], qkv_ref, rows, put)


def middle_kernel(after_ref, back_ref, high_ref, low_ref, gains_ref, hidden_ref, normed_ref):
    back = back_ref[...]
    hidden = after_ref[...] + (dot(high_ref[...], back) + dot(low_ref[...], back))
    hidden_ref[...] = hidden
    unit, _ = rms_parts(hidden)
    normed_ref[...] = (unit * gains_ref[2:3, :]).astype(BF16)


def attend_back_kernel(
    me_ref, length_ref, qkv_ref, total_ref, normed_ref, cos_ref, sin_ref, *refs, rows, cores, steps
):
    slot = qkv_ref.shape[0]
    if steps:
        count = len(steps)
        moved, mate_ref = refs[:count], refs[count]
        moved_refs = refs[count + 1 : 2 * count + 1]
        grads_ref, dk_ref, dv_ref, grad_ref, out_ref = refs[2 * count + 1 :]
        place_moved(me_ref[0], cores, steps, moved, mate_ref, grad_ref, slot // count // cores, 0)
    else:
        grad_ref, out_ref, grads_ref, dk_ref, dv_ref = refs
    length = length_ref[0]
    key_wide, value_wide = wide(qkv_ref)
    ahead, causal = masks(length, slot, rows)
    low_half = low_lanes((slot, 128))
    dk_ref[...] = jnp.zeros((slot, 128), F32)
    dv_ref[...] = jnp.zeros((slot, 128), F32)
    low_row = low_lanes((rows, 128))
    zero_row = jnp.zeros((rows, 128), BF16)
    for block in range(slot // rows):
        span = (block + 1) * rows
        at = pl.ds(block * rows, rows)
        query = qkv_ref[at, 0:128] * jnp.asarray(HD**-0.5, BF16)
        grad = grad_ref[at, :]
        dq = jnp.zeros((rows, 128), F32)
        for head in range(2):
            keep = low_row if head == 0 else jnp.logical_not(low_row)
            scores = masked(dot_nt(query, key_wide[head][:span]), ahead, causal)
            probs = jnp.exp(scores - total_ref[at, head * HD : head * HD + 1])
            dprobs = dot_nt(grad, value_wide[head][:span])
            mean = jnp.sum(dprobs * probs, axis=-1, keepdims=True)
            dscores = (probs * (dprobs - mean)).astype(BF16)
            dq = dq + dot(dscores, key_wide[head][:span])
            dk_ref[:span, :] += dot_tn(dscores, jnp.where(keep, query, zero_row))
            dv_ref[:span, :] += dot_tn(probs.astype(BF16), jnp.where(keep, grad, zero_row))
        dq = dq * (HD**-0.5)
        out_ref[at, 0:128] = (dq * cos_ref[at, :] - swap_halves(dq) * sin_ref[at, :]).astype(BF16)
    dk = dk_ref[...]
    dk = dk + pltpu.roll(dk, HD, 1)
    dk = dk * cos_ref[...] - swap_halves(dk) * sin_ref[...]
    dv = dv_ref[...]
    dv = dv + pltpu.roll(dv, HD, 1)
    out_ref[:, 128:256] = jnp.where(low_half, dk, dv).astype(BF16)
    grads = dot_tn(normed_ref[...], out_ref[...])
    devices = slot // 128
    size = grads.shape[0] // devices
    for owner in range(devices):
        at = slice(owner * size, (owner + 1) * size)
        if steps:
            put_moved(me_ref[0], cores, moved_refs, owner, out_ref[owner * 128 : (owner + 1) * 128, :])
        parts, few = grads_ref.shape[0], grads_ref.shape[2]
        grads_ref[:, owner] = grads[at].reshape(parts, few, grads.shape[1]).astype(BF16)


def after_step(mixed, copy, held_ref, hidden_ref, gain, pick_ref, after_ref, send_ref):
    copy.wait()
    after = hidden_ref[...].astype(F32) + times_output(mixed, held_ref)
    after_ref[...] = after
    unit, _ = rms_parts(after)
    send_ref[...] = dot(pick_ref[...], (unit * gain).astype(BF16)).astype(BF16).reshape(send_ref.shape)


def after_first_kernel(
    mixed_ref, w_ref, hidden_ref, gains_ref, pick_ref, after_ref, send_ref, held_ref, sem
):
    copy = fetch(w_ref, held_ref, sem)
    mixed = jnp.concatenate([mixed_ref[g] for g in range(mixed_ref.shape[0])], axis=1)
    after_step(mixed, copy, held_ref, hidden_ref, gains_ref[1:2, :], pick_ref, after_ref, send_ref)


def after_second_kernel(me_ref, *refs, steps, cores, groups):
    moved, mate_ref = refs[: len(steps)], refs[len(steps)]
    w_ref, hidden_ref, gains_ref, pick_ref, after_ref, send_ref, mixed_out_ref, held_ref, sem = refs[len(steps) + 1 :]
    copy = fetch(blocks_of(w_ref, groups), held_ref, sem)
    place_moved(me_ref[0], cores, steps, moved, mate_ref, mixed_out_ref, 128, 1)
    after_step(mixed_out_ref[...], copy, held_ref, hidden_ref, gains_ref[3:4, :], pick_ref, after_ref, send_ref)


def pack(weights, grad, send_ref):
    send_ref[...] = dot(weights, grad.astype(BF16)).astype(BF16).reshape(send_ref.shape)


def cotangent_kernel(grad_ref, live_ref, weights_ref, dh_ref, send_ref):
    grad = grad_ref[...].astype(F32) * live_ref[...]
    dh_ref[...] = grad
    pack(weights_ref[...], grad, send_ref)


def after_back_kernel(
    me_ref, back_ref, place_ref, after_ref, gains_ref, dh_ref, w_ref, dafter_ref, dattn_ref, gain_grad_ref, *refs, groups, cores, gain_row
):
    *dmixed_refs, held_ref, sem = refs
    copy = fetch(blocks_of(w_ref, groups), held_ref, sem)
    dmoe = dot(place_ref[...], back_ref[...])
    unit, _ = rms_parts(after_ref[...])
    gain_grad_ref[...] = jnp.broadcast_to(jnp.sum(dmoe * unit, axis=0, keepdims=True), gain_grad_ref.shape)
    dafter = dh_ref[...] + rms_back(after_ref[...], gains_ref[gain_row : gain_row + 1, :], dmoe)
    dafter_ref[...] = dafter
    dattn = dafter.astype(BF16)
    dattn_ref[...] = dattn
    copy.wait()
    dmixed = times_output_t(dattn, held_ref).astype(BF16)
    for g in range(groups):
        if len(dmixed_refs) == 1:
            dmixed_refs[0][g] = dmixed[:, g * 128 : (g + 1) * 128]
        else:
            put_moved(me_ref[0], cores, dmixed_refs, g, dmixed[:, g * 128 : (g + 1) * 128])


def project_back(grads, copy, held_ref, hidden, gain, dafter):
    rows, groups = grads.shape[0], held_ref.shape[1]
    copy.wait()
    dnormed = sum(
        dot_nt(grads[:, g * 256 : (g + 1) * 256], held_ref[:, g, 0:rows].reshape(hidden.shape[1], 256))
        for g in range(groups)
    )
    return dafter + rms_back(hidden, gain, dnormed)


def middle_back_kernel(me_ref, *refs, steps, cores):
    moved, mate_ref = refs[: len(steps)], refs[len(steps)]
    w_ref, hidden_ref, gains_ref, dafter_ref, weights_ref, dh_ref, send_ref, back_ref, held_ref, sem = refs[len(steps) + 1 :]
    copy = fetch(w_ref.at[:, pl.ds(0, held_ref.shape[1])], held_ref, sem)
    place_moved(me_ref[0], cores, steps, moved, mate_ref, back_ref, 256, 1)
    dh = project_back(back_ref[...], copy, held_ref, hidden_ref[...], gains_ref[2:3, :], dafter_ref[...])
    dh_ref[...] = dh
    pack(weights_ref[...], dh, send_ref)


def last_back_kernel(back_ref, w_ref, hidden_ref, gains_ref, dafter_ref, dh_ref, held_ref, sem):
    copy = fetch(w_ref.at[:, pl.ds(0, held_ref.shape[1])], held_ref, sem)
    grads = jnp.concatenate([back_ref[g] for g in range(back_ref.shape[0])], axis=1)
    dh_ref[...] = project_back(
        grads, copy, held_ref, hidden_ref[...].astype(F32), gains_ref[0:1, :], dafter_ref[...]
    )


def output_grads_kernel(me_ref, *refs, pieces, cores):
    moved, (mixed_ref, out_ref, all_ref) = refs[: len(pieces)], refs[len(pieces) :]
    tokens = moved[0].shape[0]
    chips = all_ref.shape[0] // tokens // cores
    for (step, flip), piece in zip(pieces, moved):
        at = relative(me_ref[0], cores, chips, step, flip) * tokens
        all_ref[pl.ds(pl.multiple_of(at, tokens), tokens), :] = piece[...]
    out_ref[...] = dot_tn(mixed_ref[...], all_ref[...]).astype(BF16)


def output_part_kernel(mixed_ref, dattn_ref, gain_grad_ref, out_ref):
    shards, rows, _ = out_ref.shape
    mixed = jnp.concatenate([mixed_ref[g] for g in range(mixed_ref.shape[0])], axis=1)
    width = mixed.shape[1]
    out_ref[:, :, 0:width] = dot_tn(mixed, dattn_ref[...]).astype(BF16).reshape(shards, rows, width)
    gain = jnp.broadcast_to(gain_grad_ref[0:1, :], (128, width)).T
    lane = lax.broadcasted_iota(jnp.int32, gain.shape, 1)
    out_ref[:, :, width:] = jnp.where(lane == 0, gain, 0.0).astype(BF16).reshape(shards, rows, 128)


def sum_slots_kernel(few_ref, rows_ref, out_ref):
    count, groups, _, lanes = few_ref.shape
    size, first = rows_ref.shape[1:]
    out_ref[:, 0:first] = sum(rows_ref[e].astype(F32) for e in range(count)).astype(BF16)
    few = sum(few_ref[e].astype(F32) for e in range(count))
    for layer in range(2):
        for g in range(groups):
            at = first + (layer * groups + g) * lanes
            out_ref[:, at : at + lanes] = few[g, layer * size : (layer + 1) * size].astype(BF16)


def join_kernel(place_ref, *refs, count):
    arrived, out_ref, held_ref = refs[:count], refs[count], refs[count + 1]
    size = arrived[0].shape[0]
    for k, piece in enumerate(arrived):
        at = lax.rem(place_ref[0] - k + count, count) * size
        held_ref[pl.ds(pl.multiple_of(at, size), size), :] = piece[...].astype(F32)
    out_ref[...] = held_ref[...].astype(BF16)


def attention_out_kernel(place_ref, *refs, count):
    arrived = refs[:count]
    (wq_ref, wk_ref, wv_ref, gain_ref, query_ref, key_ref, value_ref, out_ref, attn_ref, mlp_ref, ref) = refs[count:]
    width = wq_ref.shape[2]
    groups = width // 128
    size = arrived[0].shape[0]
    for k, piece in enumerate(arrived):
        at = lax.rem(place_ref[1] - k + count, count) * size
        ref[pl.ds(pl.multiple_of(at, size), size), :] = piece[...]
    low_half = low_lanes((size * count, 128))
    for layer in range(2):
        first = 2 * width + 256 + layer * 2 * width
        total = jnp.zeros(low_half.shape, F32)
        for g in range(groups):
            query = ref[:, first + g * 256 : first + g * 256 + 128].astype(F32)
            query_ref[layer, :, g * 128 : (g + 1) * 128] = query
            total = total + query * wq_ref[layer, :, g * 128 : (g + 1) * 128].astype(F32)
        for j in range(groups // 2):
            even = ref[:, first + 512 * j + 128 : first + 512 * j + 256].astype(F32)
            odd = ref[:, first + 512 * j + 384 : first + 512 * j + 512].astype(F32)
            key = jnp.where(low_half, even, pltpu.roll(odd, HD, 1))
            value = jnp.where(low_half, pltpu.roll(even, HD, 1), odd)
            at = slice(j * 128, (j + 1) * 128)
            key_ref[layer, :, at] = key
            value_ref[layer, :, at] = value
            total = total + key * wk_ref[layer, :, at].astype(F32) + value * wv_ref[layer, :, at].astype(F32)
        out_ref[layer] = ref[:, layer * width : (layer + 1) * width].astype(F32)
        gain = jnp.sum(total, axis=1, keepdims=True) / gain_ref[:, layer : layer + 1]
        attn_ref[layer : layer + 1, :] = jnp.broadcast_to(gain, low_half.shape).T[0:1, :]
        column = ref[:, 2 * width + layer * 128 : 2 * width + (layer + 1) * 128]
        mlp_ref[layer : layer + 1, :] = column.astype(F32).T[0:1, :]


def part_kernel(shard_ref, gate_ref, up_ref, gain_ref, part_ref):
    total = jnp.zeros(gate_ref.shape[1:], F32)
    for e in range(2):
        total = total + shard_ref[3 * e].astype(F32) * gate_ref[e].astype(F32)
        total = total + shard_ref[3 * e + 1].astype(F32) * up_ref[e].astype(F32)
    gain = jnp.sum(total, axis=1, keepdims=True) / gain_ref[...]
    lane = lax.broadcasted_iota(jnp.int32, (total.shape[0], 128), 1)
    part_ref[...] = jnp.where(lane == 0, gain, 0.0).astype(BF16)


def rows_kernel(first_ref, second_ref, part_ref, out_ref):
    width = second_ref.shape[1]
    out_ref[:, 0:width] = first_ref[:, 0:width]
    out_ref[:, width : 2 * width] = second_ref[...]
    out_ref[:, 2 * width : 2 * width + 128] = first_ref[:, width:]
    out_ref[:, 2 * width + 128 :] = part_ref[...]


def expert_out_kernel(first_ref, second_ref, gate_ref, up_ref, down_ref):
    for layer, ref in enumerate((first_ref, second_ref)):
        for e in range(2):
            gate_ref[layer, e] = ref[3 * e].astype(F32)
            up_ref[layer, e] = ref[3 * e + 1].astype(F32)
            down_ref[layer, e] = ref[3 * e + 2].astype(F32)


def gate_grads(back, dh, pick_ref, routes_ref, out_ref):
    high, low = split_low(dh)
    slots, tokens = pick_ref.shape
    product = dot_nt(back, high) + dot_nt(back, low)
    product = product * pick_ref[...].astype(F32)
    each = jnp.sum(product.reshape(slots // MOST, MOST, tokens), axis=1)
    expert_id = lax.broadcasted_iota(jnp.int32, each.shape, 0)
    for k in range(routes_ref.shape[0]):
        out_ref[k : k + 1, :] = jnp.sum(
            jnp.where(routes_ref[k : k + 1, :] == expert_id, each, 0.0), axis=0, keepdims=True
        )


def gates_kernel(back_ref, dh_ref, live_ref, pick_ref, routes_ref, out_ref):
    gate_grads(back_ref[...], dh_ref[...] * live_ref[...], pick_ref, routes_ref, out_ref)


def final_kernel(after_ref, back_ref, high_ref, low_ref, dh_ref, pick_ref, routes_ref, hidden_ref, out_ref):
    back = back_ref[...]
    hidden = after_ref[...] + (dot(high_ref[...], back) + dot(low_ref[...], back))
    hidden_ref[...] = hidden.astype(BF16)
    gate_grads(back, dh_ref[...], pick_ref, routes_ref, out_ref)


def rows_of(ref, expert):
    both = ref[...].astype(F32)
    rows = both[:, expert * MOST : (expert + 1) * MOST, :]
    return rows.reshape(rows.shape[0] * MOST, rows.shape[2]).astype(BF16)


def weights_of(w_ref, which):
    part = w_ref[:, which]
    return part.reshape(part.shape[0] * part.shape[1], part.shape[2])


def put_rows(rows, expert, held_ref, out_ref):
    sources = out_ref.shape[0]
    rows = rows.reshape(sources, MOST, rows.shape[1])
    if expert == 0:
        held_ref[...] = rows
    else:
        out_ref[...] = jnp.concatenate([held_ref[...], rows], axis=1).astype(BF16)


def expert_kernel(x_ref, w_ref, y_ref, gate_ref, up_ref, held_ref):
    def one(expert):
        rows = rows_of(x_ref, expert)
        gate = dot(rows, weights_of(w_ref, 0))
        up = dot(rows, weights_of(w_ref, 1))
        gate_ref[0] = gate.astype(BF16)
        up_ref[0] = up.astype(BF16)
        act = (gate * (1.0 / (1.0 + jnp.exp(-gate))) * up).astype(BF16)
        put_rows(dot_nt(act, weights_of(w_ref, 2)), expert, held_ref, y_ref)

    for expert in range(2):
        pl.when(pl.program_id(0) == expert)(functools.partial(one, expert))


def expert_back_kernel(dy_ref, w_ref, gate_ref, up_ref, dx_ref, dgate_ref, dup_ref, held_ref):
    def one(expert):
        rows = rows_of(dy_ref, expert)
        dact = dot(rows, weights_of(w_ref, 2))
        gate = gate_ref[0].astype(F32)
        up = up_ref[0].astype(F32)
        sigma = 1.0 / (1.0 + jnp.exp(-gate))
        dgate = (dact * up * (sigma * (1.0 + gate * (1.0 - sigma)))).astype(BF16)
        dup = (dact * (gate * sigma)).astype(BF16)
        dgate_ref[0] = dgate
        dup_ref[0] = dup
        dx = dot_nt(dgate, weights_of(w_ref, 0)) + dot_nt(dup, weights_of(w_ref, 1))
        put_rows(dx, expert, held_ref, dx_ref)

    for expert in range(2):
        pl.when(pl.program_id(0) == expert)(functools.partial(one, expert))


def expert_grads_kernel(x_ref, dy_ref, gate_ref, up_ref, dgate_ref, dup_ref, out_ref):
    shards, _, rows, hidden = out_ref.shape

    def one(expert):
        x = rows_of(x_ref, expert)
        gate = gate_ref[0].astype(F32)
        act = (gate * (1.0 / (1.0 + jnp.exp(-gate))) * up_ref[0].astype(F32)).astype(BF16)
        out_ref[:, 0] = dot_tn(x, dgate_ref[0]).astype(BF16).reshape(shards, rows, hidden)
        out_ref[:, 1] = dot_tn(x, dup_ref[0]).astype(BF16).reshape(shards, rows, hidden)
        out_ref[:, 2] = dot_tn(rows_of(dy_ref, expert), act).astype(BF16).reshape(shards, rows, hidden)

    for expert in range(2):
        pl.when(pl.program_id(0) == expert)(functools.partial(one, expert))


def whole_block(dims):
    return pl.BlockSpec(dims, lambda e: (0,) * len(dims))


def expert_block(dims):
    return pl.BlockSpec((1,) + dims, lambda e: (e,) + (0,) * len(dims))


def weight_block(dims):
    return pl.BlockSpec((dims[0], 3) + dims[2:], lambda e: (0, e, 0, 0))


def expert_call(kernel, specs, out_specs, outs, *args, vmem=VMEM, scratch=()):
    return pl.pallas_call(
        kernel,
        grid=(2,),
        in_specs=specs,
        out_specs=out_specs,
        out_shape=outs,
        scratch_shapes=scratch,
        compiler_params=pltpu.CompilerParams(
            vmem_limit_bytes=vmem * MIB, dimension_semantics=("arbitrary",)
        ),
    )(*args)


def on_device(
    hidden_in,
    cotangent,
    lengths,
    routes,
    gates,
    norm_attn,
    w_query,
    w_key,
    w_value,
    w_output,
    norm_mlp,
    w_gate,
    w_up,
    w_down,
):
    _, tokens, width = hidden_in.shape
    hidden_units = w_gate.shape[3]
    ep = lax.axis_size("ep")
    fsdp = lax.axis_size("fsdp")
    slot = tokens * fsdp
    slots = ep * 2 * MOST
    pair = 2 * MOST
    me = lax.axis_index("fsdp")

    def exchange(value, axis):
        return lax.all_to_all(value, axis, 0, 0, tiled=True)

    def gather(value):
        return lax.all_gather(value, "fsdp", axis=0, tiled=True)

    cores = 2
    chips = fsdp // cores
    side = 4
    here = lax.axis_index("ep")
    place = jnp.stack([here % side, here // side, here, me]).astype(jnp.int32)
    me_arg = me.reshape(1).astype(jnp.int32)

    def along_fsdp(step, flip):
        return [
            (f, (f // cores + step) % chips * cores + (f % cores + flip) % cores) for f in range(fsdp)
        ]

    def along_ep(step_z, step_x):
        return [
            (e, (e // side + step_z) % (ep // side) * side + (e % side + step_x) % side) for e in range(ep)
        ]

    steps = (0, 1, 3, 2)
    pieces = [(step, flip) for flip in range(cores) for step in steps]

    def gather_slot(value):
        own = [value] + [lax.ppermute(value, "fsdp", along_fsdp(step, 0)) for step in steps[1:]]
        return own + [lax.ppermute(piece, "fsdp", along_fsdp(0, 1)) for piece in own]

    def layer_of(array, layer):
        dims = (1,) + array.shape[1:]
        return pl.BlockSpec(dims, lambda _: (layer,) + (0,) * (len(dims) - 1))

    hidden_0 = hidden_in[0]
    pieces_0 = gather_slot(hidden_0)
    mine = [w_query, w_key, w_value, w_output, w_gate, w_up, w_down]
    group_0, output_0 = pl.pallas_call(
        group_kernel,
        grid=(1,),
        in_specs=[layer_of(w, 0) for w in (w_query, w_key, w_value, w_output)]
        + [pl.BlockSpec((2, tokens), lambda _: (0, 0))] * 2,
        out_specs=[
            pl.BlockSpec((fsdp, tokens + 16, 256), lambda _: (0, 0, 0)),
            pl.BlockSpec((tokens, width), lambda _: (0, 0)),
        ],
        out_shape=[shape((fsdp, tokens + 16, 256)), shape((tokens, width))],
        compiler_params=pltpu.CompilerParams(vmem_limit_bytes=VMEM * MIB),
    )(*mine[:4], norm_attn, norm_mlp)
    expert_dims = (6,) + w_gate.shape[2:]
    blocks = fsdp + width // 256
    blocks = fsdp + width // 256
    group_back, group_0 = group_0, exchange(group_0, "fsdp")
    shard_1, *expert_shards = pl.pallas_call(
        shards_kernel,
        grid=(1,),
        in_specs=[layer_of(w, 1) for w in mine[:4]] + [pl.BlockSpec(w.shape, lambda _: (0,) * 4) for w in mine[4:]],
        out_specs=[pl.BlockSpec((blocks, tokens, 256), lambda _: (0, 0, 0))]
        + [pl.BlockSpec(expert_dims, lambda _: (0, 0, 0))] * 2,
        out_shape=[shape((blocks, tokens, 256)), shape(expert_dims), shape(expert_dims)],
        compiler_params=pltpu.CompilerParams(vmem_limit_bytes=VMEM * MIB),
    )(*mine)
    attn_out = gather(output_0)
    experts_0 = lax.all_gather(expert_shards[0], "fsdp", axis=0)
    attn_1 = lax.all_gather(shard_1, "fsdp", axis=0)
    experts_1 = lax.all_gather(expert_shards[1], "fsdp", axis=0)
    out_w = (attn_out, attn_1)
    expert_w = (experts_0, experts_1)


    lane = np.arange(128)
    frequency = np.float32(THETA) ** (np.float32(-2.0) * (lane % 32).astype(np.float32) / np.float32(HD))
    angles = np.arange(slot, dtype=np.float32)[:, None] * frequency.astype(np.float32)[None, :]
    cos_all = jnp.asarray(np.cos(angles).astype(np.float32))
    sin_all = jnp.asarray((np.sin(angles) * np.where(lane % HD < HD // 2, -1.0, 1.0)[None, :]).astype(np.float32))
    live = (me * tokens + jnp.arange(tokens, dtype=jnp.int32) < lengths[0]).astype(F32)
    live_col = live[:, None]
    live_row = jnp.broadcast_to(live[None, :], (8, tokens))
    routes_t = jnp.swapaxes(routes[:, 0], 1, 2)
    gates_t = jnp.swapaxes(gates[:, 0], 1, 2)

    by_row, by_token = shape((slots, tokens)), shape((tokens, slots))
    routing = call(
        routing_kernel, [by_row, by_token, by_row, by_token, by_token] * 2, routes_t, gates_t, live_row
    )
    pick, spread, high_t, high, low = zip(routing[:5], routing[5:])
    send_shape = shape((ep, pair, width))

    dh_2, send_cotangent = call(
        cotangent_kernel,
        [shape((tokens, width), F32), send_shape],
        cotangent[0],
        live_col,
        high_t[1],
    )

    in_smem = pl.BlockSpec(memory_space=pltpu.SMEM)
    in_vmem = pl.BlockSpec(memory_space=pltpu.VMEM)
    in_hbm = pl.BlockSpec(memory_space=pltpu.HBM)

    def held(dims):
        return [pltpu.VMEM(dims, BF16), pltpu.SemaphoreType.DMA(())]

    output_dims = ((width, width), (fsdp, blocks - fsdp, tokens, 256))

    units_out = shape((2, ep * MOST, hidden_units))
    units_spec = expert_block((ep * MOST, hidden_units))
    pair_spec = whole_block((ep, pair, width))
    held_rows = [pltpu.VMEM((ep, MOST, width), F32)]

    def run_experts(layer, received):
        return received, *expert_call(
            expert_kernel,
            [pair_spec, weight_block(expert_w[layer].shape)],
            [pair_spec, units_spec, units_spec],
            [send_shape, units_out, units_out],
            received,
            expert_w[layer],
            scratch=held_rows,
        )

    def experts_back(layer, dy, kept, beside=()):
        x, _, gate, up = kept
        dx, dgate, dup = expert_call(
            expert_back_kernel,
            [pair_spec, weight_block(expert_w[layer].shape), units_spec, units_spec],
            [pair_spec, units_spec, units_spec],
            [send_shape, units_out, units_out],
            dy,
            expert_w[layer],
            gate,
            up,
            scratch=held_rows,
        )
        back = exchange(dx, "ep").reshape(slots, width)
        (grads,) = expert_call(
            expert_grads_kernel,
            [pair_spec, pair_spec, units_spec, units_spec, units_spec, units_spec],
            [weight_block(expert_w[layer].shape)],
            [shape(expert_w[layer].shape)],
            x,
            dy,
            gate,
            up,
            dgate,
            dup,
        )
        return lax.optimization_barrier((back, grads, beside))

    def scatter_grads(grads):
        return lax.psum_scatter(grads, "fsdp", scatter_dimension=0, tiled=False)

    def part_of(layer, shard):
        return call(
            part_kernel, shape((tokens, 128)), shard, w_gate[layer], w_up[layer], norm_mlp[layer].astype(F32)[:, None]
        )

    def move(parts):
        moved = [parts[0]] + [lax.ppermute(parts[step], "fsdp", along_fsdp(step, 0)) for step in steps[1:]]
        mates = jnp.concatenate([m[1:2] for m in moved], axis=0)
        return [*moved, lax.ppermute(mates, "fsdp", along_fsdp(0, 1))]

    def output_grads(mixed, gathered):
        return call(
            functools.partial(output_grads_kernel, pieces=pieces, cores=cores),
            shape((tokens, width)),
            me_arg,
            *gathered,
            mixed,
            in_specs=[in_smem] + [in_vmem] * (len(pieces) + 1),
            scratch=[pltpu.VMEM((slot, width), BF16)],
        )

    def attention_back(layer, back, after, dh, qkv, total, normed_all):
        w = out_w[layer]
        late = layer == 1
        dafter, dattn, gain_grad, *dmixed = call(
            functools.partial(after_back_kernel, groups=fsdp, cores=cores, gain_row=2 * layer + 1),
            [shape((tokens, width), F32), shape((tokens, width)), shape((8, width), F32)]
            + ([shape((cores, tokens, 128))] * chips if late else [shape((fsdp, tokens, 128))]),
            me_arg,
            back,
            spread[layer],
            after,
            gains_all,
            dh,
            w,
            in_specs=[in_smem] + [in_vmem] * 5 + [in_hbm],
            scratch=held(output_dims[layer]),
        )
        dmixed = move(dmixed) if late else [exchange(dmixed[0], "fsdp").reshape(slot, 128)]
        whole = [pltpu.VMEM((slot, 128), BF16), pltpu.VMEM((slot, 256), BF16)]
        dqkv = [shape((cores, tokens, 256))] * chips if late else [shape((slot, 256))]
        grads = [shape((ep, fsdp, tokens // ep, 256))]
        outs = call(
            functools.partial(attend_back_kernel, rows=512, cores=cores, steps=steps if late else ()),
            dqkv + grads,
            me_arg,
            lengths,
            qkv,
            total,
            normed_all,
            cos_all,
            sin_all,
            *dmixed,
            in_specs=[in_smem] * 2 + [in_vmem] * (5 + len(dmixed)),
            scratch=[pltpu.VMEM((slot, 128), F32)] * 2 + (whole if late else []),
        )
        return dafter, dattn, gain_grad, outs[: len(dqkv)], outs[len(dqkv)]

    kept_out = [shape((slot, width)), shape((slot, 256))]

    gains_all, normed_0, qkv_0, mixed, total_0 = call(
        functools.partial(first_kernel, pieces=pieces, cores=cores, rows=512),
        [shape((8, width), F32)] + kept_out + [shape((slot, 128)), shape((slot, 128), F32)],
        me_arg,
        lengths,
        *pieces_0,
        group_0,
        cos_all,
        sin_all,
        in_specs=[in_smem] * 2 + [in_vmem] * (len(pieces) + 3),
    )
    mixed_0 = exchange(mixed.reshape(fsdp, tokens, 128), "fsdp")
    after_0, send = call(
        after_first_kernel,
        [shape((tokens, width), F32), send_shape],
        mixed_0,
        attn_out,
        hidden_0,
        gains_all,
        pick[0],
        in_specs=[in_vmem, in_hbm] + [in_vmem] * 3,
        scratch=held(output_dims[0]),
    )
    kept_0 = run_experts(0, exchange(send, "ep"))
    y_0 = exchange(kept_0[1], "ep").reshape(slots, width)
    group_1 = lax.dynamic_index_in_dim(attn_1, me, 1, False)
    y_0, send_cotangent, group_1 = lax.optimization_barrier((y_0, send_cotangent, group_1))
    dy_1 = exchange(send_cotangent, "ep")
    hidden_1, normed = call(
        middle_kernel,
        [shape((tokens, width), F32), shape((tokens, width))],
        after_0,
        y_0,
        high[0],
        low[0],
        gains_all,
    )
    normed_1, qkv_1, total_1, mixed_1, *mixed = call(
        functools.partial(second_kernel, pieces=pieces, cores=cores, rows=512),
        kept_out + [shape((slot, 128), F32), shape((slot, 128))] + [shape((cores, tokens, 128))] * chips,
        me_arg,
        lengths,
        *gather_slot(normed),
        group_1,
        cos_all,
        sin_all,
        in_specs=[in_smem] * 2 + [in_vmem] * (len(pieces) + 3),
    )
    after_1, send = call(
        functools.partial(after_second_kernel, steps=steps, cores=cores, groups=fsdp),
        [shape((tokens, width), F32), send_shape],
        me_arg,
        *move(mixed),
        attn_1,
        hidden_1,
        gains_all,
        pick[1],
        in_specs=[in_smem] + [in_vmem] * (chips + 1) + [in_hbm] + [in_vmem] * 3,
        scratch=[pltpu.VMEM((tokens, width), BF16)] + held(output_dims[1]),
    )
    send, dy_1, group_back = lax.optimization_barrier((send, dy_1, group_back))
    attn_0 = lax.all_gather(group_back, "fsdp", axis=0)
    kept_1 = run_experts(1, exchange(send, "ep"))

    back, grads, _ = experts_back(1, dy_1, kept_1)
    shard_1 = scatter_grads(grads)
    back, attn_0 = lax.optimization_barrier((back, attn_0))
    y_late, back = lax.optimization_barrier((kept_1[1], back))
    y_1 = exchange(y_late, "ep").reshape(slots, width)
    dafter, dattn, _, dqkv, few_1 = attention_back(1, back, after_1, dh_2, qkv_1, total_1, normed_1)
    dh_1, send = call(
        functools.partial(middle_back_kernel, steps=steps, cores=cores),
        [shape((tokens, width), F32), send_shape],
        me_arg,
        *move(dqkv),
        attn_1,
        hidden_1,
        gains_all,
        dafter,
        high_t[0],
        in_specs=[in_smem] + [in_vmem] * (chips + 1) + [in_hbm] + [in_vmem] * 4,
        scratch=[pltpu.VMEM((tokens, 2 * width), BF16)] + held((fsdp, fsdp, tokens, 256)),
    )
    send, dattn, y_1 = lax.optimization_barrier((send, dattn, y_1))
    gate_grad_0 = call(
        gates_kernel, shape((8, tokens), F32), y_0, dh_1, live_col, pick[0], routes_t[0]
    )
    hidden_out, gate_grad_1 = call(
        final_kernel,
        [shape((tokens, width)), shape((8, tokens), F32)],
        after_1,
        y_1,
        high[1],
        low[1],
        dh_2,
        pick[1],
        routes_t[1],
    )
    dy_0, gathered, gate_grad_0, gate_grad_1, hidden_out = lax.optimization_barrier(
        (exchange(send, "ep"), gather_slot(dattn), gate_grad_0, gate_grad_1, hidden_out)
    )
    back, grads, (part_1, output_1) = experts_back(
        0, dy_0, kept_0, (part_of(1, shard_1), output_grads(mixed_1, gathered))
    )
    dafter, dattn, gain_grad, dqkv, few_0 = attention_back(0, back, after_0, dh_1, qkv_0, total_0, normed_0)

    output_0 = scatter_grads(
        call(output_part_kernel, shape((fsdp, tokens, width + 128)), mixed_0, dattn, gain_grad)
    )
    rows = call(rows_kernel, shape((tokens, 2 * width + 256)), output_0, output_1, part_1)
    few = jnp.concatenate([few_0, few_1], axis=2).reshape(ep * fsdp, 2 * tokens // ep, 256)
    few = lax.all_to_all(few, ("ep", "fsdp"), 0, 0, tiled=True).reshape(ep, fsdp, 2 * tokens // ep, 256)
    few, grads, rows = lax.optimization_barrier((few, grads, rows))
    shard_0 = scatter_grads(grads)
    rows = exchange(rows.reshape(ep, tokens // ep, rows.shape[1]), "ep")
    few, rows, dqkv = lax.optimization_barrier((few, rows, dqkv))
    piece = call(sum_slots_kernel, shape((tokens // ep, rows.shape[2] + 4 * width)), few, rows)
    arrived = [piece] + [lax.ppermute(piece, "ep", along_ep(0, k)) for k in (1, 2, 3)]
    dh_0 = call(
        last_back_kernel,
        shape((tokens, width), F32),
        exchange(dqkv[0].reshape(fsdp, tokens, 256), "fsdp"),
        attn_0,
        hidden_0,
        gains_all,
        dafter,
        in_specs=[in_vmem, in_hbm] + [in_vmem] * 3,
        scratch=held((fsdp, fsdp, tokens + 16, 256)),
    )
    expert_grads = call(expert_out_kernel, [shape(w_gate.shape, F32)] * 3, shard_0, shard_1)
    piece = call(
        functools.partial(join_kernel, count=side),
        shape((side * piece.shape[0], piece.shape[1])),
        place,
        *arrived,
        in_specs=[in_smem] + [in_vmem] * side,
        scratch=[pltpu.VMEM((side * piece.shape[0], piece.shape[1]), F32)],
    )
    arrived = [piece] + [lax.ppermute(piece, "ep", along_ep(k, 0)) for k in (1, 2, 3)]
    arrived[0], dh_0, expert_grads = lax.optimization_barrier((arrived[0], dh_0, expert_grads))
    half = width // 2
    query_grad, key_grad, value_grad, output_grad, attn_gain_grad, mlp_gain_grad = call(
        functools.partial(attention_out_kernel, count=side),
        [shape((2, tokens, width), F32)]
        + [shape((2, tokens, half), F32)] * 2
        + [shape((2, tokens, width), F32)]
        + [shape((2, tokens), F32)] * 2,
        place,
        *arrived,
        w_query,
        w_key,
        w_value,
        norm_attn.astype(F32).T,
        in_specs=[in_smem] + [in_vmem] * (side + 4),
        scratch=[pltpu.VMEM((tokens, piece.shape[1]), BF16)],
    )
    gates_grad = jnp.swapaxes(jnp.stack([gate_grad_0, gate_grad_1]), 1, 2)[:, None]

    return (
        hidden_out[None],
        dh_0[None],
        gates_grad,
        attn_gain_grad,
        query_grad,
        key_grad,
        value_grad,
        output_grad,
        mlp_gain_grad,
        *expert_grads,
    )


def solution(mesh):
    row = P(None, "fsdp", None)
    expert = P(None, "ep", "fsdp", None)
    hidden = P("ep", "fsdp", None)
    gain = P(None, "fsdp")
    return jax.shard_map(
        on_device,
        mesh=mesh,
        in_specs=(hidden, hidden, P("ep"), expert, expert, gain, row, row, row, row, gain, expert, expert, expert),
        out_specs=(hidden, hidden, expert, gain, row, row, row, row, gain, expert, expert, expert),
        check_vma=False,
    )
```

```python
import functools

import jax
import jax.numpy as jnp
import numpy as np
from jax import lax
from jax.experimental import pallas as pl
from jax.experimental.pallas import tpu as pltpu
from jax.sharding import PartitionSpec as P

HD = 64
EPS = 1e-06
THETA = 10000.0
NEG_FILL = -1e30
MOST = 40
MIB = 1024 * 1024
VMEM = 62
F32 = jnp.float32
BF16 = jnp.bfloat16


def dot(left, right):
    return lax.dot_general(left, right, (((1,), (0,)), ((), ())), preferred_element_type=F32)


def dot_nt(left, right):
    return lax.dot_general(left, right, (((1,), (1,)), ((), ())), preferred_element_type=F32)


def dot_tn(left, right):
    return lax.dot_general(left, right, (((0,), (0,)), ((), ())), preferred_element_type=F32)


def split_low(value):
    high = value.astype(BF16)
    return high, (value - high.astype(F32)).astype(BF16)


def rms_parts(hidden):
    scale = lax.rsqrt(jnp.mean(hidden * hidden, axis=-1, keepdims=True) + EPS)
    return hidden * scale, scale


def rms_back(hidden, gain, grad):
    unit, scale = rms_parts(hidden)
    scaled = grad * gain
    return scale * (scaled - unit * jnp.mean(scaled * unit, axis=-1, keepdims=True))


def swap_halves(value):
    lane = lax.broadcasted_iota(jnp.int32, value.shape, 1) % HD
    return jnp.where(lane < HD // 2, pltpu.roll(value, 128 - HD // 2, 1), pltpu.roll(value, HD // 2, 1))


def low_lanes(shape):
    return lax.broadcasted_iota(jnp.int32, shape, 1) < HD


def call(kernel, outs, *args, vmem=VMEM, scratch=(), **extra):
    return pl.pallas_call(
        kernel,
        out_shape=outs,
        scratch_shapes=scratch,
        compiler_params=pltpu.CompilerParams(vmem_limit_bytes=vmem * MIB),
        **extra,
    )(*args)


def shape(dims, dtype=BF16):
    return jax.ShapeDtypeStruct(dims, dtype)


def routing_kernel(routes_ref, gates_ref, live_ref, *out_refs):
    experts, tokens = out_refs[0].shape[0] // MOST, routes_ref.shape[2]
    earlier = lax.broadcasted_iota(jnp.int32, (tokens, tokens), 0) < lax.broadcasted_iota(
        jnp.int32, (tokens, tokens), 1
    )
    earlier = earlier.astype(F32).astype(BF16)
    expert_id = lax.broadcasted_iota(jnp.int32, (experts, tokens), 0)
    place_id = lax.broadcasted_iota(jnp.int32, (experts, MOST, tokens), 1).astype(F32)
    for layer in range(routes_ref.shape[0]):
        named = jnp.zeros((experts, tokens), F32)
        weight = jnp.zeros((experts, tokens), F32)
        for k in range(routes_ref.shape[1]):
            same = routes_ref[layer, k : k + 1, :] == expert_id
            named = named + jnp.where(same, 1.0, 0.0)
            weight = weight + jnp.where(same, gates_ref[layer, k : k + 1, :], 0.0)
        weight = weight * live_ref[0:1, :]
        rank = dot(named.astype(BF16), earlier)
        rank = jnp.where(named > 0.5, rank, -1.0)
        here = rank[:, None, :] == place_id
        pick = jnp.where(here, 1.0, 0.0).reshape(experts * MOST, tokens)
        weights = jnp.where(here, weight[:, None, :], 0.0).reshape(experts * MOST, tokens)
        high, low = split_low(weights)
        outs = out_refs[5 * layer : 5 * layer + 5]
        outs[0][...] = pick.astype(BF16)
        outs[1][...] = pick.T.astype(BF16)
        outs[2][...] = high
        outs[3][...] = high.astype(F32).T.astype(BF16)
        outs[4][...] = low.astype(F32).T.astype(BF16)


def put_groups(wq_ref, wk_ref, wv_ref, out_ref):
    rows = wq_ref.shape[1]
    low_half = low_lanes((rows, 128))
    groups = wq_ref.shape[2] // 128
    for g in range(groups):
        out_ref[g, 0:rows, 0:128] = wq_ref[0, :, g * 128 : (g + 1) * 128]
    for j in range(groups // 2):
        key = wk_ref[0, :, j * 128 : (j + 1) * 128].astype(F32)
        value = wv_ref[0, :, j * 128 : (j + 1) * 128].astype(F32)
        out_ref[2 * j, 0:rows, 128:256] = jnp.where(low_half, key, pltpu.roll(value, HD, 1)).astype(BF16)
        out_ref[2 * j + 1, 0:rows, 128:256] = jnp.where(low_half, pltpu.roll(key, HD, 1), value).astype(BF16)


def group_kernel(wq_ref, wk_ref, wv_ref, wo_ref, attn_ref, mlp_ref, out_ref, wo_out_ref):
    gains = jnp.concatenate([attn_ref[...].astype(F32), mlp_ref[...].astype(F32)], axis=1)
    gains = jnp.concatenate([gains, jnp.zeros((14, 256), F32)], axis=0).astype(BF16)
    put_groups(wq_ref, wk_ref, wv_ref, out_ref)
    wo_out_ref[...] = wo_ref[0]
    for g in range(out_ref.shape[0]):
        out_ref[g, wq_ref.shape[1] :, :] = gains


def shards_kernel(wq_ref, wk_ref, wv_ref, wo_ref, gate_ref, up_ref, down_ref, attn_ref, *expert_refs):
    put_groups(wq_ref, wk_ref, wv_ref, attn_ref)
    groups = wq_ref.shape[2] // 128
    for j in range(attn_ref.shape[0] - groups):
        attn_ref[groups + j] = wo_ref[0, :, j * 256 : (j + 1) * 256]
    for layer, out_ref in enumerate(expert_refs):
        for e in range(2):
            out_ref[3 * e] = gate_ref[layer, e]
            out_ref[3 * e + 1] = up_ref[layer, e]
            out_ref[3 * e + 2] = down_ref[layer, e]


def fetch(source, held_ref, sem):
    copy = pltpu.make_async_copy(source, held_ref, sem)
    copy.start()
    return copy


def blocks_of(w_ref, groups):
    return w_ref if len(w_ref.shape) == 2 else w_ref.at[:, pl.ds(groups, w_ref.shape[1] - groups)]


def times_output(mixed, held_ref):
    if len(held_ref.shape) == 2:
        return dot(mixed, held_ref[...])
    return jnp.concatenate(
        [dot(mixed, held_ref[:, j].reshape(mixed.shape[1], 256)) for j in range(held_ref.shape[1])], axis=1
    )


def times_output_t(grad, held_ref):
    if len(held_ref.shape) == 2:
        return dot_nt(grad, held_ref[...])
    return sum(
        dot_nt(grad[:, j * 256 : (j + 1) * 256], held_ref[:, j].reshape(grad.shape[1], 256))
        for j in range(held_ref.shape[1])
    )


def relative(me, cores, count, step, flip):
    return lax.rem(me // cores - step + count, count) * cores + lax.rem(me % cores + flip, cores)


def turned(chunk, cos, sin):
    return chunk * cos + swap_halves(chunk) * sin


def wide(qkv_ref):
    keyval = qkv_ref[:, 128:256].astype(F32)
    low_half = low_lanes(keyval.shape)
    turn = pltpu.roll(keyval, HD, 1)
    zero = jnp.zeros_like(keyval)
    keys = (jnp.where(low_half, keyval, zero).astype(BF16), jnp.where(low_half, zero, turn).astype(BF16))
    return keys, (jnp.where(low_half, turn, zero).astype(BF16), jnp.where(low_half, zero, keyval).astype(BF16))


def masks(length, slot, rows):
    ahead = jnp.where(lax.broadcasted_iota(jnp.int32, (1, slot), 1) < length, 0.0, NEG_FILL)
    row_id = lax.broadcasted_iota(jnp.int32, (rows, rows), 0)
    return ahead, jnp.where(lax.broadcasted_iota(jnp.int32, (rows, rows), 1) <= row_id, 0.0, NEG_FILL)


def masked(scores, ahead, causal):
    rows, span = scores.shape
    own = scores[:, span - rows :] + (ahead[:, span - rows : span] + causal)
    if span == rows:
        return own
    return jnp.concatenate([scores[:, : span - rows] + ahead[:, : span - rows], own], axis=1)


def attend(length, qkv_ref, rows, put):
    slot = qkv_ref.shape[0]
    key_wide, value_wide = wide(qkv_ref)
    ahead, causal = masks(length, slot, rows)
    for block in range(slot // rows):
        span = (block + 1) * rows
        query = qkv_ref[pl.ds(block * rows, rows), 0:128] * jnp.asarray(HD**-0.5, BF16)
        mixed = jnp.zeros((rows, 128), F32)
        totals = []
        for head in range(2):
            scores = masked(dot_nt(query, key_wide[head][:span]), ahead, causal)
            top = jnp.max(scores, axis=-1, keepdims=True)
            expo = jnp.exp(scores - top)
            total = jnp.sum(expo, axis=-1, keepdims=True)
            probs = (expo * (1.0 / total)).astype(BF16)
            mixed = mixed + dot(probs, value_wide[head][:span])
            totals.append(top + jnp.log(total))
        put(block, mixed.astype(BF16), totals)


def put_moved(me, cores, moved_refs, owner, piece):
    chips = len(moved_refs)
    step = lax.rem(owner // cores - me // cores + chips, chips)
    flip = lax.rem(owner % cores + me % cores, cores)
    for k in range(chips):

        @pl.when(step == k)
        def _():
            moved_refs[k][flip] = piece


def place_moved(me, cores, steps, moved, mate_ref, out_ref, size, dim):
    for k, step in enumerate(steps):
        for flip, piece in ((0, moved[k][0]), (1, mate_ref[k])):
            at = pl.ds(pl.multiple_of(relative(me, cores, len(steps), step, flip) * size, size), size)
            if dim == 0:
                out_ref[at, :] = piece
            else:
                out_ref[:, at] = piece


def first_kernel(
    me_ref, length_ref, *refs, pieces, cores, rows
):
    moved = refs[: len(pieces)]
    w_ref, cos_ref, sin_ref, gains_ref, normed_ref, qkv_ref, mixed_ref, total_ref = refs[len(pieces) :]
    me = me_ref[0]
    shards, _, _ = w_ref.shape
    tokens = moved[0].shape[0]
    for row in range(2):
        for half in range(2):
            gains_ref[2 * row + half : 2 * row + half + 1, :] = jnp.concatenate(
                [w_ref[s, tokens + row : tokens + row + 1, half * 128 : (half + 1) * 128] for s in range(shards)], axis=1
            ).astype(F32)
    gain = gains_ref[0:1, :]
    for (step, flip), piece in zip(pieces, moved):
        at = relative(me, cores, shards // cores, step, flip) * tokens
        unit, _ = rms_parts(piece[...].astype(F32))
        normed_ref[pl.ds(pl.multiple_of(at, tokens), tokens), :] = (unit * gain).astype(BF16)
    weights = w_ref[:, :tokens, :].reshape(shards * tokens, 256)
    raw = dot(normed_ref[...], weights)
    cos, sin = cos_ref[...], sin_ref[...]
    qkv_ref[:, 0:128] = turned(raw[:, 0:128], cos, sin).astype(BF16)
    keyval = raw[:, 128:256]
    qkv_ref[:, 128:256] = jnp.where(low_lanes(keyval.shape), turned(keyval, cos, sin), keyval).astype(BF16)

    def put(block, mixed, totals):
        at = pl.ds(block * rows, rows)
        mixed_ref[at, :] = mixed
        for head in range(2):
            total_ref[at, head * HD : (head + 1) * HD] = jnp.broadcast_to(totals[head], (rows, HD))

    attend(length_ref[0], qkv_ref, rows, put)


def second_kernel(me_ref, length_ref, *refs, pieces, cores, rows):
    moved = refs[: len(pieces)]
    w_ref, cos_ref, sin_ref, normed_ref, qkv_ref, total_ref, mixed_ref = refs[len(pieces) : len(pieces) + 7]
    moved_refs = refs[len(pieces) + 7 :]
    me = me_ref[0]
    tokens = moved[0].shape[0]
    devices = normed_ref.shape[0] // tokens
    chips = devices // cores
    for (step, flip), piece in zip(pieces, moved):
        at = relative(me, cores, chips, step, flip) * tokens
        normed_ref[pl.ds(pl.multiple_of(at, tokens), tokens), :] = piece[...]
    normed = normed_ref[...]
    cos, sin = cos_ref[...], sin_ref[...]
    raw = dot(normed, w_ref[...].reshape(normed.shape[1], 256))
    qkv_ref[:, 0:128] = turned(raw[:, 0:128], cos, sin).astype(BF16)
    keyval = raw[:, 128:256]
    qkv_ref[:, 128:256] = jnp.where(low_lanes(keyval.shape), turned(keyval, cos, sin), keyval).astype(BF16)

    def put(block, mixed, totals):
        at = pl.ds(block * rows, rows)
        for head in range(2):
            total_ref[at, head * HD : (head + 1) * HD] = jnp.broadcast_to(totals[head], (rows, HD))
        mixed_ref[at, :] = mixed
        for part in range(rows // tokens):
            put_moved(me, cores, moved_refs, block * (rows // tokens) + part, mixed[part * tokens : (part + 1) * tokens])

    attend(length_ref[0], qkv_ref, rows, put)


def middle_kernel(after_ref, back_ref, high_ref, low_ref, gains_ref, hidden_ref, normed_ref):
    back = back_ref[...]
    hidden = after_ref[...] + (dot(high_ref[...], back) + dot(low_ref[...], back))
    hidden_ref[...] = hidden
    unit, _ = rms_parts(hidden)
    normed_ref[...] = (unit * gains_ref[2:3, :]).astype(BF16)


def attend_back_kernel(
    me_ref, length_ref, qkv_ref, total_ref, normed_ref, cos_ref, sin_ref, *refs, rows, cores, steps
):
    slot = qkv_ref.shape[0]
    if steps:
        count = len(steps)
        moved, mate_ref = refs[:count], refs[count]
        moved_refs = refs[count + 1 : 2 * count + 1]
        grads_ref, dk_ref, dv_ref, grad_ref, out_ref = refs[2 * count + 1 :]
        place_moved(me_ref[0], cores, steps, moved, mate_ref, grad_ref, slot // count // cores, 0)
    else:
        grad_ref, other_ref, out_ref, grads_ref, dk_ref, dv_ref = refs
    length = length_ref[0]
    key_wide, value_wide = wide(qkv_ref)
    ahead, causal = masks(length, slot, rows)
    low_half = low_lanes((slot, 128))
    dk_ref[...] = jnp.zeros((slot, 128), F32)
    dv_ref[...] = jnp.zeros((slot, 128), F32)
    low_row = low_lanes((rows, 128))
    zero_row = jnp.zeros((rows, 128), BF16)
    for block in range(slot // rows):
        span = (block + 1) * rows
        at = pl.ds(block * rows, rows)
        query = qkv_ref[at, 0:128] * jnp.asarray(HD**-0.5, BF16)
        grad = grad_ref[at, :]
        dq = jnp.zeros((rows, 128), F32)
        for head in range(2):
            keep = low_row if head == 0 else jnp.logical_not(low_row)
            scores = masked(dot_nt(query, key_wide[head][:span]), ahead, causal)
            probs = jnp.exp(scores - total_ref[at, head * HD : head * HD + 1])
            dprobs = dot_nt(grad, value_wide[head][:span])
            mean = jnp.sum(dprobs * probs, axis=-1, keepdims=True)
            dscores = (probs * (dprobs - mean)).astype(BF16)
            dq = dq + dot(dscores, key_wide[head][:span])
            dk_ref[:span, :] += dot_tn(dscores, jnp.where(keep, query, zero_row))
            dv_ref[:span, :] += dot_tn(probs.astype(BF16), jnp.where(keep, grad, zero_row))
        dq = dq * (HD**-0.5)
        out_ref[at, 0:128] = (dq * cos_ref[at, :] - swap_halves(dq) * sin_ref[at, :]).astype(BF16)
    dk = dk_ref[...]
    dk = dk + pltpu.roll(dk, HD, 1)
    dk = dk * cos_ref[...] - swap_halves(dk) * sin_ref[...]
    dv = dv_ref[...]
    dv = dv + pltpu.roll(dv, HD, 1)
    out_ref[:, 128:256] = jnp.where(low_half, dk, dv).astype(BF16)
    grads = dot_tn(normed_ref[...], out_ref[...])
    devices = slot // 128
    size = grads.shape[0] // devices
    for owner in range(devices):
        at = slice(owner * size, (owner + 1) * size)
        if steps:
            put_moved(me_ref[0], cores, moved_refs, owner, out_ref[owner * 128 : (owner + 1) * 128, :])
        parts = grads_ref.shape[0]
        few = grads[at].reshape(parts, size // parts, grads.shape[1])
        if not steps:
            few = jnp.concatenate([few, other_ref[:, owner].astype(F32)], axis=1)
        grads_ref[:, owner] = few.astype(BF16)


def after_step(mixed, copy, held_ref, hidden_ref, gain, pick_ref, after_ref, send_ref):
    copy.wait()
    after = hidden_ref[...].astype(F32) + times_output(mixed, held_ref)
    after_ref[...] = after
    unit, _ = rms_parts(after)
    send_ref[...] = dot(pick_ref[...], (unit * gain).astype(BF16)).astype(BF16).reshape(send_ref.shape)


def after_first_kernel(
    mixed_ref, w_ref, hidden_ref, gains_ref, pick_ref, after_ref, send_ref, held_ref, sem
):
    copy = fetch(w_ref, held_ref, sem)
    mixed = jnp.concatenate([mixed_ref[g] for g in range(mixed_ref.shape[0])], axis=1)
    after_step(mixed, copy, held_ref, hidden_ref, gains_ref[1:2, :], pick_ref, after_ref, send_ref)


def after_second_kernel(me_ref, *refs, steps, cores, groups):
    moved, mate_ref = refs[: len(steps)], refs[len(steps)]
    w_ref, hidden_ref, gains_ref, pick_ref, after_ref, send_ref, mixed_out_ref, held_ref, sem = refs[len(steps) + 1 :]
    copy = fetch(blocks_of(w_ref, groups), held_ref, sem)
    place_moved(me_ref[0], cores, steps, moved, mate_ref, mixed_out_ref, 128, 1)
    after_step(mixed_out_ref[...], copy, held_ref, hidden_ref, gains_ref[3:4, :], pick_ref, after_ref, send_ref)


def pack(weights, grad, send_ref):
    send_ref[...] = dot(weights, grad.astype(BF16)).astype(BF16).reshape(send_ref.shape)


def cotangent_kernel(grad_ref, live_ref, weights_ref, dh_ref, send_ref):
    grad = grad_ref[...].astype(F32) * live_ref[...]
    dh_ref[...] = grad
    pack(weights_ref[...], grad, send_ref)


def after_back_kernel(
    me_ref, back_ref, place_ref, after_ref, gains_ref, dh_ref, w_ref, dafter_ref, dattn_ref, gain_grad_ref, *refs, groups, cores, gain_row
):
    *dmixed_refs, held_ref, sem = refs
    copy = fetch(blocks_of(w_ref, groups), held_ref, sem)
    dmoe = dot(place_ref[...], back_ref[...])
    unit, _ = rms_parts(after_ref[...])
    gain_grad_ref[...] = jnp.broadcast_to(jnp.sum(dmoe * unit, axis=0, keepdims=True), gain_grad_ref.shape)
    dafter = dh_ref[...] + rms_back(after_ref[...], gains_ref[gain_row : gain_row + 1, :], dmoe)
    dafter_ref[...] = dafter
    dattn = dafter.astype(BF16)
    dattn_ref[...] = dattn
    copy.wait()
    dmixed = times_output_t(dattn, held_ref).astype(BF16)
    for g in range(groups):
        if len(dmixed_refs) == 1:
            dmixed_refs[0][g] = dmixed[:, g * 128 : (g + 1) * 128]
        else:
            put_moved(me_ref[0], cores, dmixed_refs, g, dmixed[:, g * 128 : (g + 1) * 128])


def project_back(grads, copy, held_ref, hidden, gain, dafter):
    rows, groups = grads.shape[0], held_ref.shape[1]
    copy.wait()
    dnormed = sum(
        dot_nt(grads[:, g * 256 : (g + 1) * 256], held_ref[:, g, 0:rows].reshape(hidden.shape[1], 256))
        for g in range(groups)
    )
    return dafter + rms_back(hidden, gain, dnormed)


def middle_back_kernel(me_ref, *refs, steps, cores):
    moved, mate_ref = refs[: len(steps)], refs[len(steps)]
    w_ref, hidden_ref, gains_ref, dafter_ref, weights_ref, dh_ref, send_ref, back_ref, held_ref, sem = refs[len(steps) + 1 :]
    copy = fetch(w_ref.at[:, pl.ds(0, held_ref.shape[1])], held_ref, sem)
    place_moved(me_ref[0], cores, steps, moved, mate_ref, back_ref, 256, 1)
    dh = project_back(back_ref[...], copy, held_ref, hidden_ref[...], gains_ref[2:3, :], dafter_ref[...])
    dh_ref[...] = dh
    pack(weights_ref[...], dh, send_ref)


def last_back_kernel(back_ref, w_ref, hidden_ref, gains_ref, dafter_ref, dh_ref, held_ref, sem):
    copy = fetch(w_ref.at[:, pl.ds(0, held_ref.shape[1])], held_ref, sem)
    grads = jnp.concatenate([back_ref[g] for g in range(back_ref.shape[0])], axis=1)
    dh_ref[...] = project_back(
        grads, copy, held_ref, hidden_ref[...].astype(F32), gains_ref[0:1, :], dafter_ref[...]
    )


def output_grads_kernel(me_ref, *refs, pieces, cores):
    moved, (mixed_ref, out_ref, all_ref) = refs[: len(pieces)], refs[len(pieces) :]
    tokens = moved[0].shape[0]
    chips = all_ref.shape[0] // tokens // cores
    for (step, flip), piece in zip(pieces, moved):
        at = relative(me_ref[0], cores, chips, step, flip) * tokens
        all_ref[pl.ds(pl.multiple_of(at, tokens), tokens), :] = piece[...]
    out_ref[...] = dot_tn(mixed_ref[...], all_ref[...]).astype(BF16)


def output_part_kernel(mixed_ref, dattn_ref, gain_grad_ref, out_ref):
    shards, rows, _ = out_ref.shape
    mixed = jnp.concatenate([mixed_ref[g] for g in range(mixed_ref.shape[0])], axis=1)
    width = mixed.shape[1]
    out_ref[:, :, 0:width] = dot_tn(mixed, dattn_ref[...]).astype(BF16).reshape(shards, rows, width)
    gain = jnp.broadcast_to(gain_grad_ref[0:1, :], (128, width)).T
    lane = lax.broadcasted_iota(jnp.int32, gain.shape, 1)
    out_ref[:, :, width:] = jnp.where(lane == 0, gain, 0.0).astype(BF16).reshape(shards, rows, 128)


def sum_slots_kernel(few_ref, rows_ref, out_ref):
    count, groups, _, lanes = few_ref.shape
    size, first = rows_ref.shape[1:]
    out_ref[:, 0:first] = sum(rows_ref[e].astype(F32) for e in range(count)).astype(BF16)
    few = sum(few_ref[e].astype(F32) for e in range(count))
    for layer in range(2):
        for g in range(groups):
            at = first + (layer * groups + g) * lanes
            out_ref[:, at : at + lanes] = few[g, layer * size : (layer + 1) * size].astype(BF16)


def join_kernel(place_ref, *refs, count):
    arrived, out_ref, held_ref = refs[:count], refs[count], refs[count + 1]
    size = arrived[0].shape[0]
    for k, piece in enumerate(arrived):
        at = lax.rem(place_ref[0] - k + count, count) * size
        held_ref[pl.ds(pl.multiple_of(at, size), size), :] = piece[...].astype(F32)
    out_ref[...] = held_ref[...].astype(BF16)


def attention_out_kernel(place_ref, *refs, count):
    arrived = refs[:count]
    (wq_ref, wk_ref, wv_ref, gain_ref, query_ref, key_ref, value_ref, out_ref, attn_ref, mlp_ref, ref) = refs[count:]
    width = wq_ref.shape[2]
    groups = width // 128
    size = arrived[0].shape[0]
    for k, piece in enumerate(arrived):
        at = lax.rem(place_ref[1] - k + count, count) * size
        ref[pl.ds(pl.multiple_of(at, size), size), :] = piece[...]
    low_half = low_lanes((size * count, 128))
    for layer in range(2):
        first = 2 * width + 256 + layer * 2 * width
        total = jnp.zeros(low_half.shape, F32)
        for g in range(groups):
            query = ref[:, first + g * 256 : first + g * 256 + 128].astype(F32)
            query_ref[layer, :, g * 128 : (g + 1) * 128] = query
            total = total + query * wq_ref[layer, :, g * 128 : (g + 1) * 128].astype(F32)
        for j in range(groups // 2):
            even = ref[:, first + 512 * j + 128 : first + 512 * j + 256].astype(F32)
            odd = ref[:, first + 512 * j + 384 : first + 512 * j + 512].astype(F32)
            key = jnp.where(low_half, even, pltpu.roll(odd, HD, 1))
            value = jnp.where(low_half, pltpu.roll(even, HD, 1), odd)
            at = slice(j * 128, (j + 1) * 128)
            key_ref[layer, :, at] = key
            value_ref[layer, :, at] = value
            total = total + key * wk_ref[layer, :, at].astype(F32) + value * wv_ref[layer, :, at].astype(F32)
        out_ref[layer] = ref[:, layer * width : (layer + 1) * width].astype(F32)
        gain = jnp.sum(total, axis=1, keepdims=True) / gain_ref[:, layer : layer + 1]
        attn_ref[layer : layer + 1, :] = jnp.broadcast_to(gain, low_half.shape).T[0:1, :]
        column = ref[:, 2 * width + layer * 128 : 2 * width + (layer + 1) * 128]
        mlp_ref[layer : layer + 1, :] = column.astype(F32).T[0:1, :]


def part_kernel(shard_ref, gate_ref, up_ref, gain_ref, part_ref):
    total = jnp.zeros(gate_ref.shape[1:], F32)
    for e in range(2):
        total = total + shard_ref[3 * e].astype(F32) * gate_ref[e].astype(F32)
        total = total + shard_ref[3 * e + 1].astype(F32) * up_ref[e].astype(F32)
    gain = jnp.sum(total, axis=1, keepdims=True) / gain_ref[...]
    lane = lax.broadcasted_iota(jnp.int32, (total.shape[0], 128), 1)
    part_ref[...] = jnp.where(lane == 0, gain, 0.0).astype(BF16)


def rows_kernel(first_ref, second_ref, part_ref, out_ref):
    width = second_ref.shape[1]
    out_ref[:, 0:width] = first_ref[:, 0:width]
    out_ref[:, width : 2 * width] = second_ref[...]
    out_ref[:, 2 * width : 2 * width + 128] = first_ref[:, width:]
    out_ref[:, 2 * width + 128 :] = part_ref[...]


def expert_out_kernel(first_ref, second_ref, gate_ref, up_ref, down_ref):
    for layer, ref in enumerate((first_ref, second_ref)):
        for e in range(2):
            gate_ref[layer, e] = ref[3 * e].astype(F32)
            up_ref[layer, e] = ref[3 * e + 1].astype(F32)
            down_ref[layer, e] = ref[3 * e + 2].astype(F32)


def gate_grads(back, dh, pick_ref, routes_ref, out_ref):
    high, low = split_low(dh)
    slots, tokens = pick_ref.shape
    product = dot_nt(back, high) + dot_nt(back, low)
    product = product * pick_ref[...].astype(F32)
    each = jnp.sum(product.reshape(slots // MOST, MOST, tokens), axis=1)
    expert_id = lax.broadcasted_iota(jnp.int32, each.shape, 0)
    for k in range(routes_ref.shape[0]):
        out_ref[k : k + 1, :] = jnp.sum(
            jnp.where(routes_ref[k : k + 1, :] == expert_id, each, 0.0), axis=0, keepdims=True
        )


def gates_kernel(back_ref, dh_ref, live_ref, pick_ref, routes_ref, out_ref):
    gate_grads(back_ref[...], dh_ref[...] * live_ref[...], pick_ref, routes_ref, out_ref)


def final_kernel(after_ref, back_ref, high_ref, low_ref, dh_ref, pick_ref, routes_ref, hidden_ref, out_ref):
    back = back_ref[...]
    hidden = after_ref[...] + (dot(high_ref[...], back) + dot(low_ref[...], back))
    hidden_ref[...] = hidden.astype(BF16)
    gate_grads(back, dh_ref[...], pick_ref, routes_ref, out_ref)


def rows_of(ref, expert):
    both = ref[...].astype(F32)
    rows = both[:, expert * MOST : (expert + 1) * MOST, :]
    return rows.reshape(rows.shape[0] * MOST, rows.shape[2]).astype(BF16)


def weights_of(w_ref, which):
    part = w_ref[:, which]
    return part.reshape(part.shape[0] * part.shape[1], part.shape[2])


def put_rows(rows, expert, held_ref, out_ref):
    sources = out_ref.shape[0]
    rows = rows.reshape(sources, MOST, rows.shape[1])
    if expert == 0:
        held_ref[...] = rows
    else:
        out_ref[...] = jnp.concatenate([held_ref[...], rows], axis=1).astype(BF16)


def expert_kernel(x_ref, w_ref, y_ref, gate_ref, up_ref, held_ref):
    def one(expert):
        rows = rows_of(x_ref, expert)
        gate = dot(rows, weights_of(w_ref, 0))
        up = dot(rows, weights_of(w_ref, 1))
        gate_ref[0] = gate.astype(BF16)
        up_ref[0] = up.astype(BF16)
        act = (gate * (1.0 / (1.0 + jnp.exp(-gate))) * up).astype(BF16)
        put_rows(dot_nt(act, weights_of(w_ref, 2)), expert, held_ref, y_ref)

    for expert in range(2):
        pl.when(pl.program_id(0) == expert)(functools.partial(one, expert))


def expert_back_kernel(dy_ref, w_ref, gate_ref, up_ref, dx_ref, dgate_ref, dup_ref, held_ref):
    def one(expert):
        rows = rows_of(dy_ref, expert)
        dact = dot(rows, weights_of(w_ref, 2))
        gate = gate_ref[0].astype(F32)
        up = up_ref[0].astype(F32)
        sigma = 1.0 / (1.0 + jnp.exp(-gate))
        dgate = (dact * up * (sigma * (1.0 + gate * (1.0 - sigma)))).astype(BF16)
        dup = (dact * (gate * sigma)).astype(BF16)
        dgate_ref[0] = dgate
        dup_ref[0] = dup
        dx = dot_nt(dgate, weights_of(w_ref, 0)) + dot_nt(dup, weights_of(w_ref, 1))
        put_rows(dx, expert, held_ref, dx_ref)

    for expert in range(2):
        pl.when(pl.program_id(0) == expert)(functools.partial(one, expert))


def expert_grads_kernel(x_ref, dy_ref, gate_ref, up_ref, dgate_ref, dup_ref, out_ref):
    shards, _, rows, hidden = out_ref.shape

    def one(expert):
        x = rows_of(x_ref, expert)
        gate = gate_ref[0].astype(F32)
        act = (gate * (1.0 / (1.0 + jnp.exp(-gate))) * up_ref[0].astype(F32)).astype(BF16)
        out_ref[:, 0] = dot_tn(x, dgate_ref[0]).astype(BF16).reshape(shards, rows, hidden)
        out_ref[:, 1] = dot_tn(x, dup_ref[0]).astype(BF16).reshape(shards, rows, hidden)
        out_ref[:, 2] = dot_tn(rows_of(dy_ref, expert), act).astype(BF16).reshape(shards, rows, hidden)

    for expert in range(2):
        pl.when(pl.program_id(0) == expert)(functools.partial(one, expert))


def whole_block(dims):
    return pl.BlockSpec(dims, lambda e: (0,) * len(dims))


def expert_block(dims):
    return pl.BlockSpec((1,) + dims, lambda e: (e,) + (0,) * len(dims))


def weight_block(dims):
    return pl.BlockSpec((dims[0], 3) + dims[2:], lambda e: (0, e, 0, 0))


def expert_call(kernel, specs, out_specs, outs, *args, vmem=VMEM, scratch=()):
    return pl.pallas_call(
        kernel,
        grid=(2,),
        in_specs=specs,
        out_specs=out_specs,
        out_shape=outs,
        scratch_shapes=scratch,
        compiler_params=pltpu.CompilerParams(
            vmem_limit_bytes=vmem * MIB, dimension_semantics=("arbitrary",)
        ),
    )(*args)


def on_device(
    hidden_in,
    cotangent,
    lengths,
    routes,
    gates,
    norm_attn,
    w_query,
    w_key,
    w_value,
    w_output,
    norm_mlp,
    w_gate,
    w_up,
    w_down,
):
    _, tokens, width = hidden_in.shape
    hidden_units = w_gate.shape[3]
    ep = lax.axis_size("ep")
    fsdp = lax.axis_size("fsdp")
    slot = tokens * fsdp
    slots = ep * 2 * MOST
    pair = 2 * MOST
    me = lax.axis_index("fsdp")

    def exchange(value, axis):
        return lax.all_to_all(value, axis, 0, 0, tiled=True)

    def gather(value):
        return lax.all_gather(value, "fsdp", axis=0, tiled=True)

    cores = 2
    chips = fsdp // cores
    side = 4
    here = lax.axis_index("ep")
    place = jnp.stack([here % side, here // side, here, me]).astype(jnp.int32)
    me_arg = me.reshape(1).astype(jnp.int32)

    def along_fsdp(step, flip):
        return [
            (f, (f // cores + step) % chips * cores + (f % cores + flip) % cores) for f in range(fsdp)
        ]

    def along_ep(step_z, step_x):
        return [
            (e, (e // side + step_z) % (ep // side) * side + (e % side + step_x) % side) for e in range(ep)
        ]

    steps = (0, 1, 3, 2)
    pieces = [(step, flip) for flip in range(cores) for step in steps]

    def gather_slot(value):
        own = [value] + [lax.ppermute(value, "fsdp", along_fsdp(step, 0)) for step in steps[1:]]
        return own + [lax.ppermute(piece, "fsdp", along_fsdp(0, 1)) for piece in own]

    def layer_of(array, layer):
        dims = (1,) + array.shape[1:]
        return pl.BlockSpec(dims, lambda _: (layer,) + (0,) * (len(dims) - 1))

    hidden_0 = hidden_in[0]
    pieces_0 = gather_slot(hidden_0)
    mine = [w_query, w_key, w_value, w_output, w_gate, w_up, w_down]
    group_0, output_0 = pl.pallas_call(
        group_kernel,
        grid=(1,),
        in_specs=[layer_of(w, 0) for w in (w_query, w_key, w_value, w_output)]
        + [pl.BlockSpec((2, tokens), lambda _: (0, 0))] * 2,
        out_specs=[
            pl.BlockSpec((fsdp, tokens + 16, 256), lambda _: (0, 0, 0)),
            pl.BlockSpec((tokens, width), lambda _: (0, 0)),
        ],
        out_shape=[shape((fsdp, tokens + 16, 256)), shape((tokens, width))],
        compiler_params=pltpu.CompilerParams(vmem_limit_bytes=VMEM * MIB),
    )(*mine[:4], norm_attn, norm_mlp)
    expert_dims = (6,) + w_gate.shape[2:]
    blocks = fsdp + width // 256
    blocks = fsdp + width // 256
    group_back, group_0 = group_0, exchange(group_0, "fsdp")
    shard_1, *expert_shards = pl.pallas_call(
        shards_kernel,
        grid=(1,),
        in_specs=[layer_of(w, 1) for w in mine[:4]] + [pl.BlockSpec(w.shape, lambda _: (0,) * 4) for w in mine[4:]],
        out_specs=[pl.BlockSpec((blocks, tokens, 256), lambda _: (0, 0, 0))]
        + [pl.BlockSpec(expert_dims, lambda _: (0, 0, 0))] * 2,
        out_shape=[shape((blocks, tokens, 256)), shape(expert_dims), shape(expert_dims)],
        compiler_params=pltpu.CompilerParams(vmem_limit_bytes=VMEM * MIB),
    )(*mine)
    attn_out = gather(output_0)
    experts_0 = lax.all_gather(expert_shards[0], "fsdp", axis=0)
    attn_1 = lax.all_gather(shard_1, "fsdp", axis=0)
    experts_1 = lax.all_gather(expert_shards[1], "fsdp", axis=0)
    out_w = (attn_out, attn_1)
    expert_w = (experts_0, experts_1)


    lane = np.arange(128)
    frequency = np.float32(THETA) ** (np.float32(-2.0) * (lane % 32).astype(np.float32) / np.float32(HD))
    angles = np.arange(slot, dtype=np.float32)[:, None] * frequency.astype(np.float32)[None, :]
    cos_all = jnp.asarray(np.cos(angles).astype(np.float32))
    sin_all = jnp.asarray((np.sin(angles) * np.where(lane % HD < HD // 2, -1.0, 1.0)[None, :]).astype(np.float32))
    live = (me * tokens + jnp.arange(tokens, dtype=jnp.int32) < lengths[0]).astype(F32)
    live_col = live[:, None]
    live_row = jnp.broadcast_to(live[None, :], (8, tokens))
    routes_t = jnp.swapaxes(routes[:, 0], 1, 2)
    gates_t = jnp.swapaxes(gates[:, 0], 1, 2)

    by_row, by_token = shape((slots, tokens)), shape((tokens, slots))
    routing = call(
        routing_kernel, [by_row, by_token, by_row, by_token, by_token] * 2, routes_t, gates_t, live_row
    )
    pick, spread, high_t, high, low = zip(routing[:5], routing[5:])
    send_shape = shape((ep, pair, width))

    dh_2, send_cotangent = call(
        cotangent_kernel,
        [shape((tokens, width), F32), send_shape],
        cotangent[0],
        live_col,
        high_t[1],
    )

    in_smem = pl.BlockSpec(memory_space=pltpu.SMEM)
    in_vmem = pl.BlockSpec(memory_space=pltpu.VMEM)
    in_hbm = pl.BlockSpec(memory_space=pltpu.HBM)

    def held(dims):
        return [pltpu.VMEM(dims, BF16), pltpu.SemaphoreType.DMA(())]

    output_dims = ((width, width), (fsdp, blocks - fsdp, tokens, 256))

    units_out = shape((2, ep * MOST, hidden_units))
    units_spec = expert_block((ep * MOST, hidden_units))
    pair_spec = whole_block((ep, pair, width))
    held_rows = [pltpu.VMEM((ep, MOST, width), F32)]

    def run_experts(layer, received):
        return received, *expert_call(
            expert_kernel,
            [pair_spec, weight_block(expert_w[layer].shape)],
            [pair_spec, units_spec, units_spec],
            [send_shape, units_out, units_out],
            received,
            expert_w[layer],
            scratch=held_rows,
        )

    def experts_back(layer, dy, kept, beside=()):
        x, _, gate, up = kept
        dx, dgate, dup = expert_call(
            expert_back_kernel,
            [pair_spec, weight_block(expert_w[layer].shape), units_spec, units_spec],
            [pair_spec, units_spec, units_spec],
            [send_shape, units_out, units_out],
            dy,
            expert_w[layer],
            gate,
            up,
            scratch=held_rows,
        )
        back = exchange(dx, "ep").reshape(slots, width)
        (grads,) = expert_call(
            expert_grads_kernel,
            [pair_spec, pair_spec, units_spec, units_spec, units_spec, units_spec],
            [weight_block(expert_w[layer].shape)],
            [shape(expert_w[layer].shape)],
            x,
            dy,
            gate,
            up,
            dgate,
            dup,
        )
        return lax.optimization_barrier((back, grads, beside))

    def scatter_grads(grads):
        return lax.psum_scatter(grads, "fsdp", scatter_dimension=0, tiled=False)

    def part_of(layer, shard):
        return call(
            part_kernel, shape((tokens, 128)), shard, w_gate[layer], w_up[layer], norm_mlp[layer].astype(F32)[:, None]
        )

    def move(parts):
        moved = [parts[0]] + [lax.ppermute(parts[step], "fsdp", along_fsdp(step, 0)) for step in steps[1:]]
        mates = jnp.concatenate([m[1:2] for m in moved], axis=0)
        return [*moved, lax.ppermute(mates, "fsdp", along_fsdp(0, 1))]

    def output_grads(mixed, gathered):
        return call(
            functools.partial(output_grads_kernel, pieces=pieces, cores=cores),
            shape((tokens, width)),
            me_arg,
            *gathered,
            mixed,
            in_specs=[in_smem] + [in_vmem] * (len(pieces) + 1),
            scratch=[pltpu.VMEM((slot, width), BF16)],
        )

    def attention_back(layer, back, after, dh, qkv, total, normed_all, others=()):
        w = out_w[layer]
        late = layer == 1
        dafter, dattn, gain_grad, *dmixed = call(
            functools.partial(after_back_kernel, groups=fsdp, cores=cores, gain_row=2 * layer + 1),
            [shape((tokens, width), F32), shape((tokens, width)), shape((8, width), F32)]
            + ([shape((cores, tokens, 128))] * chips if late else [shape((fsdp, tokens, 128))]),
            me_arg,
            back,
            spread[layer],
            after,
            gains_all,
            dh,
            w,
            in_specs=[in_smem] + [in_vmem] * 5 + [in_hbm],
            scratch=held(output_dims[layer]),
        )
        dmixed = move(dmixed) if late else [exchange(dmixed[0], "fsdp").reshape(slot, 128)]
        whole = [pltpu.VMEM((slot, 128), BF16), pltpu.VMEM((slot, 256), BF16)]
        dqkv = [shape((cores, tokens, 256))] * chips if late else [shape((slot, 256))]
        grads = [shape((ep, fsdp, (1 if late else 2) * tokens // ep, 256))]
        outs = call(
            functools.partial(attend_back_kernel, rows=512, cores=cores, steps=steps if late else ()),
            dqkv + grads,
            me_arg,
            lengths,
            qkv,
            total,
            normed_all,
            cos_all,
            sin_all,
            *dmixed,
            *others,
            in_specs=[in_smem] * 2 + [in_vmem] * (5 + len(dmixed) + len(others)),
            scratch=[pltpu.VMEM((slot, 128), F32)] * 2 + (whole if late else []),
        )
        return dafter, dattn, gain_grad, outs[: len(dqkv)], outs[len(dqkv)]

    kept_out = [shape((slot, width)), shape((slot, 256))]

    gains_all, normed_0, qkv_0, mixed, total_0 = call(
        functools.partial(first_kernel, pieces=pieces, cores=cores, rows=512),
        [shape((8, width), F32)] + kept_out + [shape((slot, 128)), shape((slot, 128), F32)],
        me_arg,
        lengths,
        *pieces_0,
        group_0,
        cos_all,
        sin_all,
        in_specs=[in_smem] * 2 + [in_vmem] * (len(pieces) + 3),
    )
    mixed_0 = exchange(mixed.reshape(fsdp, tokens, 128), "fsdp")
    after_0, send = call(
        after_first_kernel,
        [shape((tokens, width), F32), send_shape],
        mixed_0,
        attn_out,
        hidden_0,
        gains_all,
        pick[0],
        in_specs=[in_vmem, in_hbm] + [in_vmem] * 3,
        scratch=held(output_dims[0]),
    )
    kept_0 = run_experts(0, exchange(send, "ep"))
    y_0 = exchange(kept_0[1], "ep").reshape(slots, width)
    group_1 = lax.dynamic_index_in_dim(attn_1, me, 1, False)
    y_0, send_cotangent, group_1 = lax.optimization_barrier((y_0, send_cotangent, group_1))
    dy_1 = exchange(send_cotangent, "ep")
    hidden_1, normed = call(
        middle_kernel,
        [shape((tokens, width), F32), shape((tokens, width))],
        after_0,
        y_0,
        high[0],
        low[0],
        gains_all,
    )
    normed_1, qkv_1, total_1, mixed_1, *mixed = call(
        functools.partial(second_kernel, pieces=pieces, cores=cores, rows=512),
        kept_out + [shape((slot, 128), F32), shape((slot, 128))] + [shape((cores, tokens, 128))] * chips,
        me_arg,
        lengths,
        *gather_slot(normed),
        group_1,
        cos_all,
        sin_all,
        in_specs=[in_smem] * 2 + [in_vmem] * (len(pieces) + 3),
    )
    after_1, send = call(
        functools.partial(after_second_kernel, steps=steps, cores=cores, groups=fsdp),
        [shape((tokens, width), F32), send_shape],
        me_arg,
        *move(mixed),
        attn_1,
        hidden_1,
        gains_all,
        pick[1],
        in_specs=[in_smem] + [in_vmem] * (chips + 1) + [in_hbm] + [in_vmem] * 3,
        scratch=[pltpu.VMEM((tokens, width), BF16)] + held(output_dims[1]),
    )
    send, dy_1, group_back = lax.optimization_barrier((send, dy_1, group_back))
    attn_0 = lax.all_gather(group_back, "fsdp", axis=0)
    kept_1 = run_experts(1, exchange(send, "ep"))

    back, grads, _ = experts_back(1, dy_1, kept_1)
    shard_1 = scatter_grads(grads)
    back, attn_0 = lax.optimization_barrier((back, attn_0))
    y_late, back = lax.optimization_barrier((kept_1[1], back))
    y_1 = exchange(y_late, "ep").reshape(slots, width)
    dafter, dattn, _, dqkv, few_1 = attention_back(1, back, after_1, dh_2, qkv_1, total_1, normed_1)
    dh_1, send = call(
        functools.partial(middle_back_kernel, steps=steps, cores=cores),
        [shape((tokens, width), F32), send_shape],
        me_arg,
        *move(dqkv),
        attn_1,
        hidden_1,
        gains_all,
        dafter,
        high_t[0],
        in_specs=[in_smem] + [in_vmem] * (chips + 1) + [in_hbm] + [in_vmem] * 4,
        scratch=[pltpu.VMEM((tokens, 2 * width), BF16)] + held((fsdp, fsdp, tokens, 256)),
    )
    send, dattn, y_1 = lax.optimization_barrier((send, dattn, y_1))
    gate_grad_0 = call(
        gates_kernel, shape((8, tokens), F32), y_0, dh_1, live_col, pick[0], routes_t[0]
    )
    hidden_out, gate_grad_1 = call(
        final_kernel,
        [shape((tokens, width)), shape((8, tokens), F32)],
        after_1,
        y_1,
        high[1],
        low[1],
        dh_2,
        pick[1],
        routes_t[1],
    )
    dy_0, gathered, gate_grad_0, gate_grad_1, hidden_out = lax.optimization_barrier(
        (exchange(send, "ep"), gather_slot(dattn), gate_grad_0, gate_grad_1, hidden_out)
    )
    back, grads, (part_1, output_1) = experts_back(
        0, dy_0, kept_0, (part_of(1, shard_1), output_grads(mixed_1, gathered))
    )
    dafter, dattn, gain_grad, dqkv, few_0 = attention_back(
        0, back, after_0, dh_1, qkv_0, total_0, normed_0, (few_1,)
    )

    output_0 = scatter_grads(
        call(output_part_kernel, shape((fsdp, tokens, width + 128)), mixed_0, dattn, gain_grad)
    )
    rows = call(rows_kernel, shape((tokens, 2 * width + 256)), output_0, output_1, part_1)
    few = few_0.reshape(ep * fsdp, 2 * tokens // ep, 256)
    few = lax.all_to_all(few, ("ep", "fsdp"), 0, 0, tiled=True).reshape(ep, fsdp, 2 * tokens // ep, 256)
    few, grads, rows = lax.optimization_barrier((few, grads, rows))
    shard_0 = scatter_grads(grads)
    rows = exchange(rows.reshape(ep, tokens // ep, rows.shape[1]), "ep")
    few, rows, dqkv = lax.optimization_barrier((few, rows, dqkv))
    piece = call(sum_slots_kernel, shape((tokens // ep, rows.shape[2] + 4 * width)), few, rows)
    arrived = [piece] + [lax.ppermute(piece, "ep", along_ep(0, k)) for k in (1, 2, 3)]
    dh_0 = call(
        last_back_kernel,
        shape((tokens, width), F32),
        exchange(dqkv[0].reshape(fsdp, tokens, 256), "fsdp"),
        attn_0,
        hidden_0,
        gains_all,
        dafter,
        in_specs=[in_vmem, in_hbm] + [in_vmem] * 3,
        scratch=held((fsdp, fsdp, tokens + 16, 256)),
    )
    expert_grads = call(expert_out_kernel, [shape(w_gate.shape, F32)] * 3, shard_0, shard_1)
    piece = call(
        functools.partial(join_kernel, count=side),
        shape((side * piece.shape[0], piece.shape[1])),
        place,
        *arrived,
        in_specs=[in_smem] + [in_vmem] * side,
        scratch=[pltpu.VMEM((side * piece.shape[0], piece.shape[1]), F32)],
    )
    arrived = [piece] + [lax.ppermute(piece, "ep", along_ep(k, 0)) for k in (1, 2, 3)]
    arrived[0], dh_0, expert_grads = lax.optimization_barrier((arrived[0], dh_0, expert_grads))
    half = width // 2
    query_grad, key_grad, value_grad, output_grad, attn_gain_grad, mlp_gain_grad = call(
        functools.partial(attention_out_kernel, count=side),
        [shape((2, tokens, width), F32)]
        + [shape((2, tokens, half), F32)] * 2
        + [shape((2, tokens, width), F32)]
        + [shape((2, tokens), F32)] * 2,
        place,
        *arrived,
        w_query,
        w_key,
        w_value,
        norm_attn.astype(F32).T,
        in_specs=[in_smem] + [in_vmem] * (side + 4),
        scratch=[pltpu.VMEM((tokens, piece.shape[1]), BF16)],
    )
    gates_grad = jnp.swapaxes(jnp.stack([gate_grad_0, gate_grad_1]), 1, 2)[:, None]

    return (
        hidden_out[None],
        dh_0[None],
        gates_grad,
        attn_gain_grad,
        query_grad,
        key_grad,
        value_grad,
        output_grad,
        mlp_gain_grad,
        *expert_grads,
    )


def solution(mesh):
    row = P(None, "fsdp", None)
    expert = P(None, "ep", "fsdp", None)
    hidden = P("ep", "fsdp", None)
    gain = P(None, "fsdp")
    return jax.shard_map(
        on_device,
        mesh=mesh,
        in_specs=(hidden, hidden, P("ep"), expert, expert, gain, row, row, row, row, gain, expert, expert, expert),
        out_specs=(hidden, hidden, expert, gain, row, row, row, row, gain, expert, expert, expert),
        check_vma=False,
    )
```

```python
import functools

import jax
import jax.numpy as jnp
import numpy as np
from jax import lax
from jax.experimental import pallas as pl
from jax.experimental.pallas import tpu as pltpu
from jax.sharding import PartitionSpec as P

HD = 64
EPS = 1e-06
THETA = 10000.0
NEG_FILL = -1e30
MOST = 40
MIB = 1024 * 1024
VMEM = 62
F32 = jnp.float32
BF16 = jnp.bfloat16


def dot(left, right):
    return lax.dot_general(left, right, (((1,), (0,)), ((), ())), preferred_element_type=F32)


def dot_nt(left, right):
    return lax.dot_general(left, right, (((1,), (1,)), ((), ())), preferred_element_type=F32)


def dot_tn(left, right):
    return lax.dot_general(left, right, (((0,), (0,)), ((), ())), preferred_element_type=F32)


def split_low(value):
    high = value.astype(BF16)
    return high, (value - high.astype(F32)).astype(BF16)


def rms_parts(hidden):
    scale = lax.rsqrt(jnp.mean(hidden * hidden, axis=-1, keepdims=True) + EPS)
    return hidden * scale, scale


def rms_back(hidden, gain, grad):
    unit, scale = rms_parts(hidden)
    scaled = grad * gain
    return scale * (scaled - unit * jnp.mean(scaled * unit, axis=-1, keepdims=True))


def swap_halves(value):
    lane = lax.broadcasted_iota(jnp.int32, value.shape, 1) % HD
    return jnp.where(lane < HD // 2, pltpu.roll(value, 128 - HD // 2, 1), pltpu.roll(value, HD // 2, 1))


def low_lanes(shape):
    return lax.broadcasted_iota(jnp.int32, shape, 1) < HD


def call(kernel, outs, *args, vmem=VMEM, scratch=(), **extra):
    return pl.pallas_call(
        kernel,
        out_shape=outs,
        scratch_shapes=scratch,
        compiler_params=pltpu.CompilerParams(vmem_limit_bytes=vmem * MIB),
        **extra,
    )(*args)


def shape(dims, dtype=BF16):
    return jax.ShapeDtypeStruct(dims, dtype)


def routing_kernel(routes_ref, gates_ref, live_ref, *out_refs):
    experts, tokens = out_refs[0].shape[0] // MOST, routes_ref.shape[2]
    earlier = lax.broadcasted_iota(jnp.int32, (tokens, tokens), 0) < lax.broadcasted_iota(
        jnp.int32, (tokens, tokens), 1
    )
    earlier = earlier.astype(F32).astype(BF16)
    expert_id = lax.broadcasted_iota(jnp.int32, (experts, tokens), 0)
    place_id = lax.broadcasted_iota(jnp.int32, (experts, MOST, tokens), 1).astype(F32)
    for layer in range(routes_ref.shape[0]):
        named = jnp.zeros((experts, tokens), F32)
        weight = jnp.zeros((experts, tokens), F32)
        for k in range(routes_ref.shape[1]):
            same = routes_ref[layer, k : k + 1, :] == expert_id
            named = named + jnp.where(same, 1.0, 0.0)
            weight = weight + jnp.where(same, gates_ref[layer, k : k + 1, :], 0.0)
        weight = weight * live_ref[0:1, :]
        rank = dot(named.astype(BF16), earlier)
        rank = jnp.where(named > 0.5, rank, -1.0)
        here = rank[:, None, :] == place_id
        pick = jnp.where(here, 1.0, 0.0).reshape(experts * MOST, tokens)
        weights = jnp.where(here, weight[:, None, :], 0.0).reshape(experts * MOST, tokens)
        high, low = split_low(weights)
        outs = out_refs[5 * layer : 5 * layer + 5]
        outs[0][...] = pick.astype(BF16)
        outs[1][...] = pick.T.astype(BF16)
        outs[2][...] = high
        outs[3][...] = high.astype(F32).T.astype(BF16)
        outs[4][...] = low.astype(F32).T.astype(BF16)


def put_groups(wq_ref, wk_ref, wv_ref, out_ref):
    rows = wq_ref.shape[1]
    low_half = low_lanes((rows, 128))
    groups = wq_ref.shape[2] // 128
    for g in range(groups):
        out_ref[g, 0:rows, 0:128] = wq_ref[0, :, g * 128 : (g + 1) * 128]
    for j in range(groups // 2):
        key = wk_ref[0, :, j * 128 : (j + 1) * 128].astype(F32)
        value = wv_ref[0, :, j * 128 : (j + 1) * 128].astype(F32)
        out_ref[2 * j, 0:rows, 128:256] = jnp.where(low_half, key, pltpu.roll(value, HD, 1)).astype(BF16)
        out_ref[2 * j + 1, 0:rows, 128:256] = jnp.where(low_half, pltpu.roll(key, HD, 1), value).astype(BF16)


def group_kernel(wq_ref, wk_ref, wv_ref, wo_ref, attn_ref, mlp_ref, out_ref, wo_out_ref):
    gains = jnp.concatenate([attn_ref[...].astype(F32), mlp_ref[...].astype(F32)], axis=1)
    gains = jnp.concatenate([gains, jnp.zeros((14, 256), F32)], axis=0).astype(BF16)
    put_groups(wq_ref, wk_ref, wv_ref, out_ref)
    wo_out_ref[...] = wo_ref[0]
    for g in range(out_ref.shape[0]):
        out_ref[g, wq_ref.shape[1] :, :] = gains


def shards_kernel(wq_ref, wk_ref, wv_ref, wo_ref, gate_ref, up_ref, down_ref, attn_ref, *expert_refs):
    put_groups(wq_ref, wk_ref, wv_ref, attn_ref)
    groups = wq_ref.shape[2] // 128
    for j in range(attn_ref.shape[0] - groups):
        attn_ref[groups + j] = wo_ref[0, :, j * 256 : (j + 1) * 256]
    for layer, out_ref in enumerate(expert_refs):
        for e in range(2):
            out_ref[3 * e] = gate_ref[layer, e]
            out_ref[3 * e + 1] = up_ref[layer, e]
            out_ref[3 * e + 2] = down_ref[layer, e]


def fetch(source, held_ref, sem):
    copy = pltpu.make_async_copy(source, held_ref, sem)
    copy.start()
    return copy


def blocks_of(w_ref, groups):
    return w_ref if len(w_ref.shape) == 2 else w_ref.at[:, pl.ds(groups, w_ref.shape[1] - groups)]


def times_output(mixed, held_ref):
    if len(held_ref.shape) == 2:
        return dot(mixed, held_ref[...])
    return jnp.concatenate(
        [dot(mixed, held_ref[:, j].reshape(mixed.shape[1], 256)) for j in range(held_ref.shape[1])], axis=1
    )


def times_output_t(grad, held_ref):
    if len(held_ref.shape) == 2:
        return dot_nt(grad, held_ref[...])
    return sum(
        dot_nt(grad[:, j * 256 : (j + 1) * 256], held_ref[:, j].reshape(grad.shape[1], 256))
        for j in range(held_ref.shape[1])
    )


def relative(me, cores, count, step, flip):
    return lax.rem(me // cores - step + count, count) * cores + lax.rem(me % cores + flip, cores)


def turned(chunk, cos, sin):
    return chunk * cos + swap_halves(chunk) * sin


def wide(qkv_ref):
    keyval = qkv_ref[:, 128:256].astype(F32)
    low_half = low_lanes(keyval.shape)
    turn = pltpu.roll(keyval, HD, 1)
    zero = jnp.zeros_like(keyval)
    keys = (jnp.where(low_half, keyval, zero).astype(BF16), jnp.where(low_half, zero, turn).astype(BF16))
    return keys, (jnp.where(low_half, turn, zero).astype(BF16), jnp.where(low_half, zero, keyval).astype(BF16))


def masks(length, slot, rows):
    ahead = jnp.where(lax.broadcasted_iota(jnp.int32, (1, slot), 1) < length, 0.0, NEG_FILL)
    row_id = lax.broadcasted_iota(jnp.int32, (rows, rows), 0)
    return ahead, jnp.where(lax.broadcasted_iota(jnp.int32, (rows, rows), 1) <= row_id, 0.0, NEG_FILL)


def masked(scores, ahead, causal):
    rows, span = scores.shape
    own = scores[:, span - rows :] + (ahead[:, span - rows : span] + causal)
    if span == rows:
        return own
    return jnp.concatenate([scores[:, : span - rows] + ahead[:, : span - rows], own], axis=1)


def attend(length, qkv_ref, rows, put):
    slot = qkv_ref.shape[0]
    key_wide, value_wide = wide(qkv_ref)
    ahead, causal = masks(length, slot, rows)
    for block in range(slot // rows):
        span = (block + 1) * rows
        query = qkv_ref[pl.ds(block * rows, rows), 0:128] * jnp.asarray(HD**-0.5, BF16)
        mixed = jnp.zeros((rows, 128), F32)
        totals = []
        for head in range(2):
            scores = masked(dot_nt(query, key_wide[head][:span]), ahead, causal)
            top = jnp.max(scores, axis=-1, keepdims=True)
            expo = jnp.exp(scores - top)
            total = jnp.sum(expo, axis=-1, keepdims=True)
            probs = (expo * (1.0 / total)).astype(BF16)
            mixed = mixed + dot(probs, value_wide[head][:span])
            totals.append(top + jnp.log(total))
        put(block, mixed.astype(BF16), totals)


def put_moved(me, cores, moved_refs, owner, piece):
    chips = len(moved_refs)
    step = lax.rem(owner // cores - me // cores + chips, chips)
    flip = lax.rem(owner % cores + me % cores, cores)
    for k in range(chips):

        @pl.when(step == k)
        def _():
            moved_refs[k][flip] = piece


def place_moved(me, cores, steps, moved, mate_ref, out_ref, size, dim):
    for k, step in enumerate(steps):
        for flip, piece in ((0, moved[k][0]), (1, mate_ref[k])):
            at = pl.ds(pl.multiple_of(relative(me, cores, len(steps), step, flip) * size, size), size)
            if dim == 0:
                out_ref[at, :] = piece
            else:
                out_ref[:, at] = piece


def first_kernel(
    me_ref, length_ref, *refs, pieces, cores, rows
):
    moved = refs[: len(pieces)]
    w_ref, cos_ref, sin_ref, gains_ref, normed_ref, qkv_ref, mixed_ref, total_ref = refs[len(pieces) :]
    me = me_ref[0]
    shards, _, _ = w_ref.shape
    tokens = moved[0].shape[0]
    behind = [w_ref[s, tokens:, :].astype(F32) for s in range(shards)]
    for row in range(2):
        for half in range(2):
            gains_ref[2 * row + half : 2 * row + half + 1, :] = jnp.concatenate(
                [b[row : row + 1, half * 128 : (half + 1) * 128] for b in behind], axis=1
            )
    gain = gains_ref[0:1, :]
    for (step, flip), piece in zip(pieces, moved):
        at = relative(me, cores, shards // cores, step, flip) * tokens
        unit, _ = rms_parts(piece[...].astype(F32))
        normed_ref[pl.ds(pl.multiple_of(at, tokens), tokens), :] = (unit * gain).astype(BF16)
    weights = w_ref[:, :tokens, :].reshape(shards * tokens, 256)
    raw = dot(normed_ref[...], weights)
    cos, sin = cos_ref[...], sin_ref[...]
    qkv_ref[:, 0:128] = turned(raw[:, 0:128], cos, sin).astype(BF16)
    keyval = raw[:, 128:256]
    qkv_ref[:, 128:256] = jnp.where(low_lanes(keyval.shape), turned(keyval, cos, sin), keyval).astype(BF16)

    def put(block, mixed, totals):
        at = pl.ds(block * rows, rows)
        mixed_ref[at, :] = mixed
        for head in range(2):
            total_ref[at, head * HD : (head + 1) * HD] = jnp.broadcast_to(totals[head], (rows, HD))

    attend(length_ref[0], qkv_ref, rows, put)


def second_kernel(me_ref, length_ref, *refs, pieces, cores, rows):
    moved = refs[: len(pieces)]
    w_ref, cos_ref, sin_ref, normed_ref, qkv_ref, total_ref, mixed_ref = refs[len(pieces) : len(pieces) + 7]
    moved_refs = refs[len(pieces) + 7 :]
    me = me_ref[0]
    tokens = moved[0].shape[0]
    devices = normed_ref.shape[0] // tokens
    chips = devices // cores
    for (step, flip), piece in zip(pieces, moved):
        at = relative(me, cores, chips, step, flip) * tokens
        normed_ref[pl.ds(pl.multiple_of(at, tokens), tokens), :] = piece[...]
    normed = normed_ref[...]
    cos, sin = cos_ref[...], sin_ref[...]
    raw = dot(normed, w_ref[...].reshape(normed.shape[1], 256))
    qkv_ref[:, 0:128] = turned(raw[:, 0:128], cos, sin).astype(BF16)
    keyval = raw[:, 128:256]
    qkv_ref[:, 128:256] = jnp.where(low_lanes(keyval.shape), turned(keyval, cos, sin), keyval).astype(BF16)

    def put(block, mixed, totals):
        at = pl.ds(block * rows, rows)
        for head in range(2):
            total_ref[at, head * HD : (head + 1) * HD] = jnp.broadcast_to(totals[head], (rows, HD))
        mixed_ref[at, :] = mixed
        for part in range(rows // tokens):
            put_moved(me, cores, moved_refs, block * (rows // tokens) + part, mixed[part * tokens : (part + 1) * tokens])

    attend(length_ref[0], qkv_ref, rows, put)


def middle_kernel(after_ref, back_ref, high_ref, low_ref, gains_ref, hidden_ref, normed_ref):
    back = back_ref[...]
    hidden = after_ref[...] + (dot(high_ref[...], back) + dot(low_ref[...], back))
    hidden_ref[...] = hidden
    unit, _ = rms_parts(hidden)
    normed_ref[...] = (unit * gains_ref[2:3, :]).astype(BF16)


def attend_back_kernel(
    me_ref, length_ref, qkv_ref, total_ref, normed_ref, cos_ref, sin_ref, *refs, rows, cores, steps
):
    slot = qkv_ref.shape[0]
    if steps:
        count = len(steps)
        moved, mate_ref = refs[:count], refs[count]
        moved_refs = refs[count + 1 : 2 * count + 1]
        grads_ref, dk_ref, dv_ref, grad_ref, out_ref = refs[2 * count + 1 :]
        place_moved(me_ref[0], cores, steps, moved, mate_ref, grad_ref, slot // count // cores, 0)
    else:
        grad_ref, other_ref, out_ref, grads_ref, dk_ref, dv_ref = refs
    length = length_ref[0]
    key_wide, value_wide = wide(qkv_ref)
    ahead, causal = masks(length, slot, rows)
    low_half = low_lanes((slot, 128))
    dk_ref[...] = jnp.zeros((slot, 128), F32)
    dv_ref[...] = jnp.zeros((slot, 128), F32)
    low_row = low_lanes((rows, 128))
    zero_row = jnp.zeros((rows, 128), BF16)
    for block in range(slot // rows):
        span = (block + 1) * rows
        at = pl.ds(block * rows, rows)
        query = qkv_ref[at, 0:128] * jnp.asarray(HD**-0.5, BF16)
        grad = grad_ref[at, :]
        dq = jnp.zeros((rows, 128), F32)
        for head in range(2):
            keep = low_row if head == 0 else jnp.logical_not(low_row)
            scores = masked(dot_nt(query, key_wide[head][:span]), ahead, causal)
            probs = jnp.exp(scores - total_ref[at, head * HD : head * HD + 1])
            dprobs = dot_nt(grad, value_wide[head][:span])
            mean = jnp.sum(dprobs * probs, axis=-1, keepdims=True)
            dscores = (probs * (dprobs - mean)).astype(BF16)
            dq = dq + dot(dscores, key_wide[head][:span])
            dk_ref[:span, :] += dot_tn(dscores, jnp.where(keep, query, zero_row))
            dv_ref[:span, :] += dot_tn(probs.astype(BF16), jnp.where(keep, grad, zero_row))
        dq = dq * (HD**-0.5)
        out_ref[at, 0:128] = (dq * cos_ref[at, :] - swap_halves(dq) * sin_ref[at, :]).astype(BF16)
    dk = dk_ref[...]
    dk = dk + pltpu.roll(dk, HD, 1)
    dk = dk * cos_ref[...] - swap_halves(dk) * sin_ref[...]
    dv = dv_ref[...]
    dv = dv + pltpu.roll(dv, HD, 1)
    out_ref[:, 128:256] = jnp.where(low_half, dk, dv).astype(BF16)
    grads = dot_tn(normed_ref[...], out_ref[...])
    devices = slot // 128
    size = grads.shape[0] // devices
    for owner in range(devices):
        at = slice(owner * size, (owner + 1) * size)
        if steps:
            put_moved(me_ref[0], cores, moved_refs, owner, out_ref[owner * 128 : (owner + 1) * 128, :])
        parts = grads_ref.shape[0]
        few = grads[at].reshape(parts, size // parts, grads.shape[1])
        if not steps:
            few = jnp.concatenate([few, other_ref[:, owner].astype(F32)], axis=1)
        grads_ref[:, owner] = few.astype(BF16)


def after_step(mixed, copy, held_ref, hidden_ref, gain, pick_ref, after_ref, send_ref):
    copy.wait()
    after = hidden_ref[...].astype(F32) + times_output(mixed, held_ref)
    after_ref[...] = after
    unit, _ = rms_parts(after)
    send_ref[...] = dot(pick_ref[...], (unit * gain).astype(BF16)).astype(BF16).reshape(send_ref.shape)


def after_first_kernel(
    mixed_ref, w_ref, hidden_ref, gains_ref, pick_ref, after_ref, send_ref, held_ref, sem
):
    copy = fetch(w_ref, held_ref, sem)
    mixed = jnp.concatenate([mixed_ref[g] for g in range(mixed_ref.shape[0])], axis=1)
    after_step(mixed, copy, held_ref, hidden_ref, gains_ref[1:2, :], pick_ref, after_ref, send_ref)


def after_second_kernel(me_ref, *refs, steps, cores, groups):
    moved, mate_ref = refs[: len(steps)], refs[len(steps)]
    w_ref, hidden_ref, gains_ref, pick_ref, after_ref, send_ref, mixed_out_ref, held_ref, sem = refs[len(steps) + 1 :]
    copy = fetch(blocks_of(w_ref, groups), held_ref, sem)
    place_moved(me_ref[0], cores, steps, moved, mate_ref, mixed_out_ref, 128, 1)
    after_step(mixed_out_ref[...], copy, held_ref, hidden_ref, gains_ref[3:4, :], pick_ref, after_ref, send_ref)


def pack(weights, grad, send_ref):
    send_ref[...] = dot(weights, grad.astype(BF16)).astype(BF16).reshape(send_ref.shape)


def cotangent_kernel(grad_ref, live_ref, weights_ref, dh_ref, send_ref):
    grad = grad_ref[...].astype(F32) * live_ref[...]
    dh_ref[...] = grad
    pack(weights_ref[...], grad, send_ref)


def after_back_kernel(
    me_ref, back_ref, place_ref, after_ref, gains_ref, dh_ref, w_ref, dafter_ref, dattn_ref, gain_grad_ref, *refs, groups, cores, gain_row
):
    *dmixed_refs, held_ref, sem = refs
    copy = fetch(blocks_of(w_ref, groups), held_ref, sem)
    dmoe = dot(place_ref[...], back_ref[...])
    unit, _ = rms_parts(after_ref[...])
    gain_grad_ref[...] = jnp.broadcast_to(jnp.sum(dmoe * unit, axis=0, keepdims=True), gain_grad_ref.shape)
    dafter = dh_ref[...] + rms_back(after_ref[...], gains_ref[gain_row : gain_row + 1, :], dmoe)
    dafter_ref[...] = dafter
    dattn = dafter.astype(BF16)
    dattn_ref[...] = dattn
    copy.wait()
    dmixed = times_output_t(dattn, held_ref).astype(BF16)
    for g in range(groups):
        if len(dmixed_refs) == 1:
            dmixed_refs[0][g] = dmixed[:, g * 128 : (g + 1) * 128]
        else:
            put_moved(me_ref[0], cores, dmixed_refs, g, dmixed[:, g * 128 : (g + 1) * 128])


def project_back(grads, copy, held_ref, hidden, gain, dafter):
    rows, groups = grads.shape[0], held_ref.shape[1]
    copy.wait()
    dnormed = sum(
        dot_nt(grads[:, g * 256 : (g + 1) * 256], held_ref[:, g, 0:rows].reshape(hidden.shape[1], 256))
        for g in range(groups)
    )
    return dafter + rms_back(hidden, gain, dnormed)


def middle_back_kernel(me_ref, *refs, steps, cores):
    moved, mate_ref = refs[: len(steps)], refs[len(steps)]
    w_ref, hidden_ref, gains_ref, dafter_ref, weights_ref, dh_ref, send_ref, back_ref, held_ref, sem = refs[len(steps) + 1 :]
    copy = fetch(w_ref.at[:, pl.ds(0, held_ref.shape[1])], held_ref, sem)
    place_moved(me_ref[0], cores, steps, moved, mate_ref, back_ref, 256, 1)
    dh = project_back(back_ref[...], copy, held_ref, hidden_ref[...], gains_ref[2:3, :], dafter_ref[...])
    dh_ref[...] = dh
    pack(weights_ref[...], dh, send_ref)


def last_back_kernel(back_ref, w_ref, hidden_ref, gains_ref, dafter_ref, dh_ref, held_ref, sem):
    copy = fetch(w_ref.at[:, pl.ds(0, held_ref.shape[1])], held_ref, sem)
    grads = jnp.concatenate([back_ref[g] for g in range(back_ref.shape[0])], axis=1)
    dh_ref[...] = project_back(
        grads, copy, held_ref, hidden_ref[...].astype(F32), gains_ref[0:1, :], dafter_ref[...]
    )


def output_grads_kernel(me_ref, *refs, pieces, cores):
    moved, (mixed_ref, out_ref, all_ref) = refs[: len(pieces)], refs[len(pieces) :]
    tokens = moved[0].shape[0]
    chips = all_ref.shape[0] // tokens // cores
    for (step, flip), piece in zip(pieces, moved):
        at = relative(me_ref[0], cores, chips, step, flip) * tokens
        all_ref[pl.ds(pl.multiple_of(at, tokens), tokens), :] = piece[...]
    out_ref[...] = dot_tn(mixed_ref[...], all_ref[...]).astype(BF16)


def output_part_kernel(mixed_ref, dattn_ref, gain_grad_ref, out_ref):
    shards, rows, _ = out_ref.shape
    mixed = jnp.concatenate([mixed_ref[g] for g in range(mixed_ref.shape[0])], axis=1)
    width = mixed.shape[1]
    out_ref[:, :, 0:width] = dot_tn(mixed, dattn_ref[...]).astype(BF16).reshape(shards, rows, width)
    gain = jnp.broadcast_to(gain_grad_ref[0:1, :], (128, width)).T
    lane = lax.broadcasted_iota(jnp.int32, gain.shape, 1)
    out_ref[:, :, width:] = jnp.where(lane == 0, gain, 0.0).astype(BF16).reshape(shards, rows, 128)


def sum_slots_kernel(few_ref, rows_ref, out_ref):
    count, groups, _, lanes = few_ref.shape
    size, first = rows_ref.shape[1:]
    out_ref[:, 0:first] = sum(rows_ref[e].astype(F32) for e in range(count)).astype(BF16)
    few = sum(few_ref[e].astype(F32) for e in range(count))
    for layer in range(2):
        for g in range(groups):
            at = first + (layer * groups + g) * lanes
            out_ref[:, at : at + lanes] = few[g, layer * size : (layer + 1) * size].astype(BF16)


def join_kernel(place_ref, *refs, count):
    arrived, out_ref, held_ref = refs[:count], refs[count], refs[count + 1]
    size = arrived[0].shape[0]
    for k, piece in enumerate(arrived):
        at = lax.rem(place_ref[0] - k + count, count) * size
        held_ref[pl.ds(pl.multiple_of(at, size), size), :] = piece[...].astype(F32)
    out_ref[...] = held_ref[...].astype(BF16)


def attention_out_kernel(place_ref, *refs, count):
    arrived = refs[:count]
    (wq_ref, wk_ref, wv_ref, gain_ref, query_ref, key_ref, value_ref, out_ref, attn_ref, mlp_ref, ref) = refs[count:]
    width = wq_ref.shape[2]
    groups = width // 128
    size = arrived[0].shape[0]
    for k, piece in enumerate(arrived):
        at = lax.rem(place_ref[1] - k + count, count) * size
        ref[pl.ds(pl.multiple_of(at, size), size), :] = piece[...]
    low_half = low_lanes((size * count, 128))
    for layer in range(2):
        first = 2 * width + 256 + layer * 2 * width
        total = jnp.zeros(low_half.shape, F32)
        for g in range(groups):
            query = ref[:, first + g * 256 : first + g * 256 + 128].astype(F32)
            query_ref[layer, :, g * 128 : (g + 1) * 128] = query
            total = total + query * wq_ref[layer, :, g * 128 : (g + 1) * 128].astype(F32)
        for j in range(groups // 2):
            even = ref[:, first + 512 * j + 128 : first + 512 * j + 256].astype(F32)
            odd = ref[:, first + 512 * j + 384 : first + 512 * j + 512].astype(F32)
            key = jnp.where(low_half, even, pltpu.roll(odd, HD, 1))
            value = jnp.where(low_half, pltpu.roll(even, HD, 1), odd)
            at = slice(j * 128, (j + 1) * 128)
            key_ref[layer, :, at] = key
            value_ref[layer, :, at] = value
            total = total + key * wk_ref[layer, :, at].astype(F32) + value * wv_ref[layer, :, at].astype(F32)
        out_ref[layer] = ref[:, layer * width : (layer + 1) * width].astype(F32)
        gain = jnp.sum(total, axis=1, keepdims=True) / gain_ref[:, layer : layer + 1]
        attn_ref[layer : layer + 1, :] = jnp.broadcast_to(gain, low_half.shape).T[0:1, :]
        column = ref[:, 2 * width + layer * 128 : 2 * width + (layer + 1) * 128]
        mlp_ref[layer : layer + 1, :] = column.astype(F32).T[0:1, :]


def part_kernel(shard_ref, gate_ref, up_ref, gain_ref, part_ref):
    total = jnp.zeros(gate_ref.shape[1:], F32)
    for e in range(2):
        total = total + shard_ref[3 * e].astype(F32) * gate_ref[e].astype(F32)
        total = total + shard_ref[3 * e + 1].astype(F32) * up_ref[e].astype(F32)
    gain = jnp.sum(total, axis=1, keepdims=True) / gain_ref[...]
    lane = lax.broadcasted_iota(jnp.int32, (total.shape[0], 128), 1)
    part_ref[...] = jnp.where(lane == 0, gain, 0.0).astype(BF16)


def rows_kernel(first_ref, second_ref, part_ref, out_ref):
    width = second_ref.shape[1]
    out_ref[:, 0:width] = first_ref[:, 0:width]
    out_ref[:, width : 2 * width] = second_ref[...]
    out_ref[:, 2 * width : 2 * width + 128] = first_ref[:, width:]
    out_ref[:, 2 * width + 128 :] = part_ref[...]


def expert_out_kernel(first_ref, second_ref, gate_ref, up_ref, down_ref):
    for layer, ref in enumerate((first_ref, second_ref)):
        for e in range(2):
            gate_ref[layer, e] = ref[3 * e].astype(F32)
            up_ref[layer, e] = ref[3 * e + 1].astype(F32)
            down_ref[layer, e] = ref[3 * e + 2].astype(F32)


def gate_grads(back, dh, pick_ref, routes_ref, out_ref):
    high, low = split_low(dh)
    slots, tokens = pick_ref.shape
    product = dot_nt(back, high) + dot_nt(back, low)
    product = product * pick_ref[...].astype(F32)
    each = jnp.sum(product.reshape(slots // MOST, MOST, tokens), axis=1)
    expert_id = lax.broadcasted_iota(jnp.int32, each.shape, 0)
    for k in range(routes_ref.shape[0]):
        out_ref[k : k + 1, :] = jnp.sum(
            jnp.where(routes_ref[k : k + 1, :] == expert_id, each, 0.0), axis=0, keepdims=True
        )


def gates_kernel(back_ref, dh_ref, live_ref, pick_ref, routes_ref, out_ref):
    gate_grads(back_ref[...], dh_ref[...] * live_ref[...], pick_ref, routes_ref, out_ref)


def final_kernel(after_ref, back_ref, high_ref, low_ref, dh_ref, pick_ref, routes_ref, hidden_ref, out_ref):
    back = back_ref[...]
    hidden = after_ref[...] + (dot(high_ref[...], back) + dot(low_ref[...], back))
    hidden_ref[...] = hidden.astype(BF16)
    gate_grads(back, dh_ref[...], pick_ref, routes_ref, out_ref)


def rows_of(ref, expert):
    both = ref[...].astype(F32)
    rows = both[:, expert * MOST : (expert + 1) * MOST, :]
    return rows.reshape(rows.shape[0] * MOST, rows.shape[2]).astype(BF16)


def weights_of(w_ref, which):
    part = w_ref[:, which]
    return part.reshape(part.shape[0] * part.shape[1], part.shape[2])


def put_rows(rows, expert, held_ref, out_ref):
    sources = out_ref.shape[0]
    rows = rows.reshape(sources, MOST, rows.shape[1])
    if expert == 0:
        held_ref[...] = rows
    else:
        out_ref[...] = jnp.concatenate([held_ref[...], rows], axis=1).astype(BF16)


def expert_kernel(x_ref, w_ref, y_ref, gate_ref, up_ref, held_ref):
    def one(expert):
        rows = rows_of(x_ref, expert)
        gate = dot(rows, weights_of(w_ref, 0))
        up = dot(rows, weights_of(w_ref, 1))
        gate_ref[0] = gate.astype(BF16)
        up_ref[0] = up.astype(BF16)
        act = (gate * (1.0 / (1.0 + jnp.exp(-gate))) * up).astype(BF16)
        put_rows(dot_nt(act, weights_of(w_ref, 2)), expert, held_ref, y_ref)

    for expert in range(2):
        pl.when(pl.program_id(0) == expert)(functools.partial(one, expert))


def expert_back_kernel(dy_ref, w_ref, gate_ref, up_ref, dx_ref, dgate_ref, dup_ref, held_ref):
    def one(expert):
        rows = rows_of(dy_ref, expert)
        dact = dot(rows, weights_of(w_ref, 2))
        gate = gate_ref[0].astype(F32)
        up = up_ref[0].astype(F32)
        sigma = 1.0 / (1.0 + jnp.exp(-gate))
        dgate = (dact * up * (sigma * (1.0 + gate * (1.0 - sigma)))).astype(BF16)
        dup = (dact * (gate * sigma)).astype(BF16)
        dgate_ref[0] = dgate
        dup_ref[0] = dup
        dx = dot_nt(dgate, weights_of(w_ref, 0)) + dot_nt(dup, weights_of(w_ref, 1))
        put_rows(dx, expert, held_ref, dx_ref)

    for expert in range(2):
        pl.when(pl.program_id(0) == expert)(functools.partial(one, expert))


def expert_grads_kernel(x_ref, dy_ref, gate_ref, up_ref, dgate_ref, dup_ref, out_ref):
    shards, _, rows, hidden = out_ref.shape

    def one(expert):
        x = rows_of(x_ref, expert)
        gate = gate_ref[0].astype(F32)
        act = (gate * (1.0 / (1.0 + jnp.exp(-gate))) * up_ref[0].astype(F32)).astype(BF16)
        out_ref[:, 0] = dot_tn(x, dgate_ref[0]).astype(BF16).reshape(shards, rows, hidden)
        out_ref[:, 1] = dot_tn(x, dup_ref[0]).astype(BF16).reshape(shards, rows, hidden)
        out_ref[:, 2] = dot_tn(rows_of(dy_ref, expert), act).astype(BF16).reshape(shards, rows, hidden)

    for expert in range(2):
        pl.when(pl.program_id(0) == expert)(functools.partial(one, expert))


def whole_block(dims):
    return pl.BlockSpec(dims, lambda e: (0,) * len(dims))


def expert_block(dims):
    return pl.BlockSpec((1,) + dims, lambda e: (e,) + (0,) * len(dims))


def weight_block(dims):
    return pl.BlockSpec((dims[0], 3) + dims[2:], lambda e: (0, e, 0, 0))


def expert_call(kernel, specs, out_specs, outs, *args, vmem=VMEM, scratch=()):
    return pl.pallas_call(
        kernel,
        grid=(2,),
        in_specs=specs,
        out_specs=out_specs,
        out_shape=outs,
        scratch_shapes=scratch,
        compiler_params=pltpu.CompilerParams(
            vmem_limit_bytes=vmem * MIB, dimension_semantics=("arbitrary",)
        ),
    )(*args)


def on_device(
    hidden_in,
    cotangent,
    lengths,
    routes,
    gates,
    norm_attn,
    w_query,
    w_key,
    w_value,
    w_output,
    norm_mlp,
    w_gate,
    w_up,
    w_down,
):
    _, tokens, width = hidden_in.shape
    hidden_units = w_gate.shape[3]
    ep = lax.axis_size("ep")
    fsdp = lax.axis_size("fsdp")
    slot = tokens * fsdp
    slots = ep * 2 * MOST
    pair = 2 * MOST
    me = lax.axis_index("fsdp")

    def exchange(value, axis):
        return lax.all_to_all(value, axis, 0, 0, tiled=True)

    def gather(value):
        return lax.all_gather(value, "fsdp", axis=0, tiled=True)

    cores = 2
    chips = fsdp // cores
    side = 4
    here = lax.axis_index("ep")
    place = jnp.stack([here % side, here // side, here, me]).astype(jnp.int32)
    me_arg = me.reshape(1).astype(jnp.int32)

    def along_fsdp(step, flip):
        return [
            (f, (f // cores + step) % chips * cores + (f % cores + flip) % cores) for f in range(fsdp)
        ]

    def along_ep(step_z, step_x):
        return [
            (e, (e // side + step_z) % (ep // side) * side + (e % side + step_x) % side) for e in range(ep)
        ]

    steps = (0, 1, 3, 2)
    pieces = [(step, flip) for flip in range(cores) for step in steps]

    def gather_slot(value):
        own = [value] + [lax.ppermute(value, "fsdp", along_fsdp(step, 0)) for step in steps[1:]]
        return own + [lax.ppermute(piece, "fsdp", along_fsdp(0, 1)) for piece in own]

    def layer_of(array, layer):
        dims = (1,) + array.shape[1:]
        return pl.BlockSpec(dims, lambda _: (layer,) + (0,) * (len(dims) - 1))

    hidden_0 = hidden_in[0]
    pieces_0 = gather_slot(hidden_0)
    mine = [w_query, w_key, w_value, w_output, w_gate, w_up, w_down]
    group_0, output_0 = pl.pallas_call(
        group_kernel,
        grid=(1,),
        in_specs=[layer_of(w, 0) for w in (w_query, w_key, w_value, w_output)]
        + [pl.BlockSpec((2, tokens), lambda _: (0, 0))] * 2,
        out_specs=[
            pl.BlockSpec((fsdp, tokens + 16, 256), lambda _: (0, 0, 0)),
            pl.BlockSpec((tokens, width), lambda _: (0, 0)),
        ],
        out_shape=[shape((fsdp, tokens + 16, 256)), shape((tokens, width))],
        compiler_params=pltpu.CompilerParams(vmem_limit_bytes=VMEM * MIB),
    )(*mine[:4], norm_attn, norm_mlp)
    expert_dims = (6,) + w_gate.shape[2:]
    blocks = fsdp + width // 256
    blocks = fsdp + width // 256
    group_back, group_0 = group_0, exchange(group_0, "fsdp")
    shard_1, *expert_shards = pl.pallas_call(
        shards_kernel,
        grid=(1,),
        in_specs=[layer_of(w, 1) for w in mine[:4]] + [pl.BlockSpec(w.shape, lambda _: (0,) * 4) for w in mine[4:]],
        out_specs=[pl.BlockSpec((blocks, tokens, 256), lambda _: (0, 0, 0))]
        + [pl.BlockSpec(expert_dims, lambda _: (0, 0, 0))] * 2,
        out_shape=[shape((blocks, tokens, 256)), shape(expert_dims), shape(expert_dims)],
        compiler_params=pltpu.CompilerParams(vmem_limit_bytes=VMEM * MIB),
    )(*mine)
    attn_out = gather(output_0)
    experts_0 = lax.all_gather(expert_shards[0], "fsdp", axis=0)
    attn_1 = lax.all_gather(shard_1, "fsdp", axis=0)
    experts_1 = lax.all_gather(expert_shards[1], "fsdp", axis=0)
    out_w = (attn_out, attn_1)
    expert_w = (experts_0, experts_1)


    lane = np.arange(128)
    frequency = np.float32(THETA) ** (np.float32(-2.0) * (lane % 32).astype(np.float32) / np.float32(HD))
    angles = np.arange(slot, dtype=np.float32)[:, None] * frequency.astype(np.float32)[None, :]
    cos_all = jnp.asarray(np.cos(angles).astype(np.float32))
    sin_all = jnp.asarray((np.sin(angles) * np.where(lane % HD < HD // 2, -1.0, 1.0)[None, :]).astype(np.float32))
    live = (me * tokens + jnp.arange(tokens, dtype=jnp.int32) < lengths[0]).astype(F32)
    live_col = live[:, None]
    live_row = jnp.broadcast_to(live[None, :], (8, tokens))
    routes_t = jnp.swapaxes(routes[:, 0], 1, 2)
    gates_t = jnp.swapaxes(gates[:, 0], 1, 2)

    by_row, by_token = shape((slots, tokens)), shape((tokens, slots))
    routing = call(
        routing_kernel, [by_row, by_token, by_row, by_token, by_token] * 2, routes_t, gates_t, live_row
    )
    pick, spread, high_t, high, low = zip(routing[:5], routing[5:])
    send_shape = shape((ep, pair, width))

    dh_2, send_cotangent = call(
        cotangent_kernel,
        [shape((tokens, width), F32), send_shape],
        cotangent[0],
        live_col,
        high_t[1],
    )

    in_smem = pl.BlockSpec(memory_space=pltpu.SMEM)
    in_vmem = pl.BlockSpec(memory_space=pltpu.VMEM)
    in_hbm = pl.BlockSpec(memory_space=pltpu.HBM)

    def held(dims):
        return [pltpu.VMEM(dims, BF16), pltpu.SemaphoreType.DMA(())]

    output_dims = ((width, width), (fsdp, blocks - fsdp, tokens, 256))

    units_out = shape((2, ep * MOST, hidden_units))
    units_spec = expert_block((ep * MOST, hidden_units))
    pair_spec = whole_block((ep, pair, width))
    held_rows = [pltpu.VMEM((ep, MOST, width), F32)]

    def run_experts(layer, received):
        return received, *expert_call(
            expert_kernel,
            [pair_spec, weight_block(expert_w[layer].shape)],
            [pair_spec, units_spec, units_spec],
            [send_shape, units_out, units_out],
            received,
            expert_w[layer],
            scratch=held_rows,
        )

    def experts_back(layer, dy, kept, beside=()):
        x, _, gate, up = kept
        dx, dgate, dup = expert_call(
            expert_back_kernel,
            [pair_spec, weight_block(expert_w[layer].shape), units_spec, units_spec],
            [pair_spec, units_spec, units_spec],
            [send_shape, units_out, units_out],
            dy,
            expert_w[layer],
            gate,
            up,
            scratch=held_rows,
        )
        back = exchange(dx, "ep").reshape(slots, width)
        (grads,) = expert_call(
            expert_grads_kernel,
            [pair_spec, pair_spec, units_spec, units_spec, units_spec, units_spec],
            [weight_block(expert_w[layer].shape)],
            [shape(expert_w[layer].shape)],
            x,
            dy,
            gate,
            up,
            dgate,
            dup,
        )
        return lax.optimization_barrier((back, grads, beside))

    def scatter_grads(grads):
        return lax.psum_scatter(grads, "fsdp", scatter_dimension=0, tiled=False)

    def part_of(layer, shard):
        return call(
            part_kernel, shape((tokens, 128)), shard, w_gate[layer], w_up[layer], norm_mlp[layer].astype(F32)[:, None]
        )

    def move(parts):
        moved = [parts[0]] + [lax.ppermute(parts[step], "fsdp", along_fsdp(step, 0)) for step in steps[1:]]
        mates = jnp.concatenate([m[1:2] for m in moved], axis=0)
        return [*moved, lax.ppermute(mates, "fsdp", along_fsdp(0, 1))]

    def output_grads(mixed, gathered):
        return call(
            functools.partial(output_grads_kernel, pieces=pieces, cores=cores),
            shape((tokens, width)),
            me_arg,
            *gathered,
            mixed,
            in_specs=[in_smem] + [in_vmem] * (len(pieces) + 1),
            scratch=[pltpu.VMEM((slot, width), BF16)],
        )

    def attention_back(layer, back, after, dh, qkv, total, normed_all, others=()):
        w = out_w[layer]
        late = layer == 1
        dafter, dattn, gain_grad, *dmixed = call(
            functools.partial(after_back_kernel, groups=fsdp, cores=cores, gain_row=2 * layer + 1),
            [shape((tokens, width), F32), shape((tokens, width)), shape((8, width), F32)]
            + ([shape((cores, tokens, 128))] * chips if late else [shape((fsdp, tokens, 128))]),
            me_arg,
            back,
            spread[layer],
            after,
            gains_all,
            dh,
            w,
            in_specs=[in_smem] + [in_vmem] * 5 + [in_hbm],
            scratch=held(output_dims[layer]),
        )
        dmixed = move(dmixed) if late else [exchange(dmixed[0], "fsdp").reshape(slot, 128)]
        whole = [pltpu.VMEM((slot, 128), BF16), pltpu.VMEM((slot, 256), BF16)]
        dqkv = [shape((cores, tokens, 256))] * chips if late else [shape((slot, 256))]
        grads = [shape((ep, fsdp, (1 if late else 2) * tokens // ep, 256))]
        outs = call(
            functools.partial(attend_back_kernel, rows=512, cores=cores, steps=steps if late else ()),
            dqkv + grads,
            me_arg,
            lengths,
            qkv,
            total,
            normed_all,
            cos_all,
            sin_all,
            *dmixed,
            *others,
            in_specs=[in_smem] * 2 + [in_vmem] * (5 + len(dmixed) + len(others)),
            scratch=[pltpu.VMEM((slot, 128), F32)] * 2 + (whole if late else []),
        )
        return dafter, dattn, gain_grad, outs[: len(dqkv)], outs[len(dqkv)]

    kept_out = [shape((slot, width)), shape((slot, 256))]

    gains_all, normed_0, qkv_0, mixed, total_0 = call(
        functools.partial(first_kernel, pieces=pieces, cores=cores, rows=512),
        [shape((8, width), F32)] + kept_out + [shape((slot, 128)), shape((slot, 128), F32)],
        me_arg,
        lengths,
        *pieces_0,
        group_0,
        cos_all,
        sin_all,
        in_specs=[in_smem] * 2 + [in_vmem] * (len(pieces) + 3),
    )
    mixed_0 = exchange(mixed.reshape(fsdp, tokens, 128), "fsdp")
    after_0, send = call(
        after_first_kernel,
        [shape((tokens, width), F32), send_shape],
        mixed_0,
        attn_out,
        hidden_0,
        gains_all,
        pick[0],
        in_specs=[in_vmem, in_hbm] + [in_vmem] * 3,
        scratch=held(output_dims[0]),
    )
    kept_0 = run_experts(0, exchange(send, "ep"))
    y_0 = exchange(kept_0[1], "ep").reshape(slots, width)
    group_1 = lax.dynamic_index_in_dim(attn_1, me, 1, False)
    y_0, send_cotangent, group_1 = lax.optimization_barrier((y_0, send_cotangent, group_1))
    dy_1 = exchange(send_cotangent, "ep")
    hidden_1, normed = call(
        middle_kernel,
        [shape((tokens, width), F32), shape((tokens, width))],
        after_0,
        y_0,
        high[0],
        low[0],
        gains_all,
    )
    normed_1, qkv_1, total_1, mixed_1, *mixed = call(
        functools.partial(second_kernel, pieces=pieces, cores=cores, rows=512),
        kept_out + [shape((slot, 128), F32), shape((slot, 128))] + [shape((cores, tokens, 128))] * chips,
        me_arg,
        lengths,
        *gather_slot(normed),
        group_1,
        cos_all,
        sin_all,
        in_specs=[in_smem] * 2 + [in_vmem] * (len(pieces) + 3),
    )
    after_1, send = call(
        functools.partial(after_second_kernel, steps=steps, cores=cores, groups=fsdp),
        [shape((tokens, width), F32), send_shape],
        me_arg,
        *move(mixed),
        attn_1,
        hidden_1,
        gains_all,
        pick[1],
        in_specs=[in_smem] + [in_vmem] * (chips + 1) + [in_hbm] + [in_vmem] * 3,
        scratch=[pltpu.VMEM((tokens, width), BF16)] + held(output_dims[1]),
    )
    send, dy_1, group_back = lax.optimization_barrier((send, dy_1, group_back))
    attn_0 = lax.all_gather(group_back, "fsdp", axis=0)
    kept_1 = run_experts(1, exchange(send, "ep"))

    back, grads, _ = experts_back(1, dy_1, kept_1)
    shard_1 = scatter_grads(grads)
    back, attn_0 = lax.optimization_barrier((back, attn_0))
    y_late, back = lax.optimization_barrier((kept_1[1], back))
    y_1 = exchange(y_late, "ep").reshape(slots, width)
    dafter, dattn, _, dqkv, few_1 = attention_back(1, back, after_1, dh_2, qkv_1, total_1, normed_1)
    dh_1, send = call(
        functools.partial(middle_back_kernel, steps=steps, cores=cores),
        [shape((tokens, width), F32), send_shape],
        me_arg,
        *move(dqkv),
        attn_1,
        hidden_1,
        gains_all,
        dafter,
        high_t[0],
        in_specs=[in_smem] + [in_vmem] * (chips + 1) + [in_hbm] + [in_vmem] * 4,
        scratch=[pltpu.VMEM((tokens, 2 * width), BF16)] + held((fsdp, fsdp, tokens, 256)),
    )
    send, dattn, y_1 = lax.optimization_barrier((send, dattn, y_1))
    gate_grad_0 = call(
        gates_kernel, shape((8, tokens), F32), y_0, dh_1, live_col, pick[0], routes_t[0]
    )
    hidden_out, gate_grad_1 = call(
        final_kernel,
        [shape((tokens, width)), shape((8, tokens), F32)],
        after_1,
        y_1,
        high[1],
        low[1],
        dh_2,
        pick[1],
        routes_t[1],
    )
    dy_0, gathered, gate_grad_0, gate_grad_1, hidden_out = lax.optimization_barrier(
        (exchange(send, "ep"), gather_slot(dattn), gate_grad_0, gate_grad_1, hidden_out)
    )
    back, grads, (part_1, output_1) = experts_back(
        0, dy_0, kept_0, (part_of(1, shard_1), output_grads(mixed_1, gathered))
    )
    dafter, dattn, gain_grad, dqkv, few_0 = attention_back(
        0, back, after_0, dh_1, qkv_0, total_0, normed_0, (few_1,)
    )

    output_0 = scatter_grads(
        call(output_part_kernel, shape((fsdp, tokens, width + 128)), mixed_0, dattn, gain_grad)
    )
    rows = call(rows_kernel, shape((tokens, 2 * width + 256)), output_0, output_1, part_1)
    few = few_0.reshape(ep * fsdp, 2 * tokens // ep, 256)
    few = lax.all_to_all(few, ("ep", "fsdp"), 0, 0, tiled=True).reshape(ep, fsdp, 2 * tokens // ep, 256)
    few, grads, rows = lax.optimization_barrier((few, grads, rows))
    shard_0 = scatter_grads(grads)
    rows = exchange(rows.reshape(ep, tokens // ep, rows.shape[1]), "ep")
    few, rows, dqkv = lax.optimization_barrier((few, rows, dqkv))
    piece = call(sum_slots_kernel, shape((tokens // ep, rows.shape[2] + 4 * width)), few, rows)
    arrived = [piece] + [lax.ppermute(piece, "ep", along_ep(0, k)) for k in (1, 2, 3)]
    dh_0 = call(
        last_back_kernel,
        shape((tokens, width), F32),
        exchange(dqkv[0].reshape(fsdp, tokens, 256), "fsdp"),
        attn_0,
        hidden_0,
        gains_all,
        dafter,
        in_specs=[in_vmem, in_hbm] + [in_vmem] * 3,
        scratch=held((fsdp, fsdp, tokens + 16, 256)),
    )
    expert_grads = call(expert_out_kernel, [shape(w_gate.shape, F32)] * 3, shard_0, shard_1)
    piece = call(
        functools.partial(join_kernel, count=side),
        shape((side * piece.shape[0], piece.shape[1])),
        place,
        *arrived,
        in_specs=[in_smem] + [in_vmem] * side,
        scratch=[pltpu.VMEM((side * piece.shape[0], piece.shape[1]), F32)],
    )
    arrived = [piece] + [lax.ppermute(piece, "ep", along_ep(k, 0)) for k in (1, 2, 3)]
    arrived[0], dh_0, expert_grads = lax.optimization_barrier((arrived[0], dh_0, expert_grads))
    half = width // 2
    query_grad, key_grad, value_grad, output_grad, attn_gain_grad, mlp_gain_grad = call(
        functools.partial(attention_out_kernel, count=side),
        [shape((2, tokens, width), F32)]
        + [shape((2, tokens, half), F32)] * 2
        + [shape((2, tokens, width), F32)]
        + [shape((2, tokens), F32)] * 2,
        place,
        *arrived,
        w_query,
        w_key,
        w_value,
        norm_attn.astype(F32).T,
        in_specs=[in_smem] + [in_vmem] * (side + 4),
        scratch=[pltpu.VMEM((tokens, piece.shape[1]), BF16)],
    )
    gates_grad = jnp.swapaxes(jnp.stack([gate_grad_0, gate_grad_1]), 1, 2)[:, None]

    return (
        hidden_out[None],
        dh_0[None],
        gates_grad,
        attn_gain_grad,
        query_grad,
        key_grad,
        value_grad,
        output_grad,
        mlp_gain_grad,
        *expert_grads,
    )


def solution(mesh):
    row = P(None, "fsdp", None)
    expert = P(None, "ep", "fsdp", None)
    hidden = P("ep", "fsdp", None)
    gain = P(None, "fsdp")
    return jax.shard_map(
        on_device,
        mesh=mesh,
        in_specs=(hidden, hidden, P("ep"), expert, expert, gain, row, row, row, row, gain, expert, expert, expert),
        out_specs=(hidden, hidden, expert, gain, row, row, row, row, gain, expert, expert, expert),
        check_vma=False,
    )
```
